32 devices in a mesh: seq: 4 (over x, core), fsdp: 8 (over z, y).
Axes of the slice: x: 2, y: 2, z: 4, core: 2. Of those that a mesh axis runs over, the one named last changes fastest.
Arguments:
- inputs: bfloat16 [8, 2048, 2048], P('fsdp', 'seq'), may hold values from -6 to 6
- teacher: bfloat16 [8, 2048, 2048], P('fsdp', 'seq'), may hold values from -6 to 6
- segment_ids: int32 [8, 2048], P('fsdp', 'seq'), may hold values from 0 to 15, never falling along the last dimension, each value on 1 to 1024 neighbouring positions
- valid: int32 [8, 2048], P('fsdp', 'seq'), may hold values from 0 to 1, as said below
- decay_rate: float32 [16], replicated, may hold values from 4.8828126e-05 to 0.03125
- w_query: bfloat16 [2048, 2048], P(('seq', 'fsdp')), may hold values from -0.125 to 0.125
- w_key: bfloat16 [2048, 2048], P(('seq', 'fsdp')), may hold values from -0.125 to 0.125
- w_value: bfloat16 [2048, 2048], P(('seq', 'fsdp')), may hold values from -0.125 to 0.125
- w_gate: bfloat16 [2048, 2048], P(('seq', 'fsdp')), may hold values from -0.125 to 0.125
- w_out: bfloat16 [2048, 2048], P(('seq', 'fsdp')), may hold values from -0.25 to 0.25
- w_first: bfloat16 [2048, 5632], P(('seq', 'fsdp')), may hold values from -0.125 to 0.125
- w_second: bfloat16 [2048, 5632], P(('seq', 'fsdp')), may hold values from -0.125 to 0.125
- w_down: bfloat16 [5632, 2048], P(('seq', 'fsdp')), may hold values from -0.078125 to 0.078125
Outputs:
- layer_out: bfloat16 [8, 2048, 2048], P('fsdp', 'seq')
- mse_loss: float32 [], replicated
- input_grad: float32 [8, 2048, 2048], P('fsdp', 'seq')
- grad_query: float32 [2048, 2048], P(('seq', 'fsdp'))
- grad_key: float32 [2048, 2048], P(('seq', 'fsdp'))
- grad_value: float32 [2048, 2048], P(('seq', 'fsdp'))
- grad_gate: float32 [2048, 2048], P(('seq', 'fsdp'))
- grad_out: float32 [2048, 2048], P(('seq', 'fsdp'))
- grad_first: float32 [2048, 5632], P(('seq', 'fsdp'))
- grad_second: float32 [2048, 5632], P(('seq', 'fsdp'))
- grad_down: float32 [5632, 2048], P(('seq', 'fsdp'))
The draws below stay inside these ranges and needn't reach their ends.
Inputs may be any that keep to these rules, and one draw needn't show every extreme that they name: `segment_ids`: along a sequence the ids never fall; a document has 1 to 1024 tokens. The first token of every sequence is valid.
All inputs are finite; a program needn't handle non-finite values.
Results may differ from the reference program's by a relative error of at most 0.009.
Values may be sent and summed in bfloat16 or wider, within the bound.
A program may use at most 352 MiB of HBM per device.

```python
import math
import jax
import jax.numpy as jnp
import numpy as np
from jax import lax

D = 2048
HEADS = 16
HEAD_DIM = 128
FF = 5632
LEN = 2048
SEQS = 8
TOKENS = 16384
DOCS = 16
DOC_MOST = 1024


def draw_valid(key, part):
    position = jnp.arange(SEQS * LEN, dtype=jnp.int32).reshape(SEQS, LEN)
    level = 300 + 600 * position // (SEQS * LEN)
    ticket = jax.random.randint(key, (SEQS, LEN), 0, 1000)
    chosen = (ticket < level) | (position % LEN == 0)
    return chosen.astype(jnp.int32)


def level_of(stream_key, shape, cuts, low, top_value):
    gain = 1.0
    for dim, blocks in cuts:
        draws = jax.random.uniform(jax.random.fold_in(jax.random.fold_in(stream_key, 6), dim), (blocks,), jnp.float32, low / len(cuts), top_value / len(cuts))
        gain = gain * jnp.repeat(jnp.exp(draws), shape[dim] // blocks).reshape((-1,) + (1,) * (len(shape) - 1 - dim))
    return gain


def length_profile(number_of, total, limit, skew):
    loads = [(1 << 20) // math.isqrt(standing ** skew) + 1 for standing in range(2, number_of + 1)]
    spare, holding = total - limit - (number_of - 1), [1] * (number_of - 1)
    while spare > 0:
        movable = [i for i in range(number_of - 1) if holding[i] < limit]
        mass, remaining = sum([loads[i] for i in movable]), spare
        for i in movable:
            addition = min(limit - holding[i], max(1, remaining * loads[i] // mass), spare)
            holding[i] = holding[i] + addition
            spare = spare - addition
    return np.array([limit] + holding)


def uneven(own_key, number_of, total, limit, lean):
    if number_of == 2:
        one = jax.random.randint(own_key, (), max(1, total - limit), min(limit, total - 1) + 1)
        return jnp.stack([one, total - one])
    tallies = jnp.asarray(length_profile(number_of, total, limit, lean), jnp.int32)
    couples = (number_of - 1) // 2
    giver, receiver = tallies[1:1 + 2 * couples:2], tallies[2:2 + 2 * couples:2]
    margin = jnp.minimum(giver - 1, limit - receiver)
    moved = jax.random.randint(jax.random.fold_in(own_key, 1), (couples,), 0, 1 << 20) % (margin + 1)
    tallies = tallies.at[1:1 + 2 * couples:2].set(giver - moved).at[2:2 + 2 * couples:2].set(receiver + moved)
    return tallies[jax.random.permutation(jax.random.fold_in(own_key, 2), number_of)]


def bell_draw(key, shape, scale, bound, cuts=(), kind=jnp.bfloat16):
    entries = jax.random.normal(key, shape, jnp.float32) * scale
    if len(cuts) > 0:
        entries = level_of(key, shape, cuts, -0.22, 0.18) * entries
    return jnp.clip(entries, min=-bound, max=bound).astype(kind)


def setup_inputs(seed: int = 0) -> dict:
    key_list = jax.random.split(jax.random.key(seed), 14)
    return {
        "inputs": bell_draw(key_list[0], (SEQS, LEN, D), 1.0, 6.0, ((0, 8), (1, 4))),
        "teacher": bell_draw(key_list[1], (SEQS, LEN, D), 1.0, 6.0, ((0, 8), (1, 4))),
        "segment_ids": jax.vmap(lambda own: jnp.searchsorted(jnp.cumsum(uneven(own, DOCS, LEN, DOC_MOST, 2)), jnp.arange(LEN), side="right"))(jax.random.split(key_list[2], SEQS)).reshape((SEQS, LEN)).astype(jnp.int32),
        "valid": draw_valid(jax.random.fold_in(key_list[13], 71), 0),
        "decay_rate": jnp.clip(jnp.exp(jax.random.uniform(key_list[4], (HEADS,), jnp.float32, math.log(4.882812572759576e-05), math.log(0.03125))), 4.882812572759576e-05, 0.03125),
        "w_query": bell_draw(key_list[5], (D, D), D ** -0.5, 0.125, ((0, 32),)),
        "w_key": bell_draw(key_list[6], (D, D), D ** -0.5, 0.125, ((0, 32),)),
        "w_value": bell_draw(key_list[7], (D, D), D ** -0.5, 0.125, ((0, 32),)),
        "w_gate": bell_draw(key_list[8], (D, D), D ** -0.5, 0.125, ((0, 32),)),
        "w_out": bell_draw(key_list[9], (D, D), (D // 4) ** -0.5, 0.25, ((0, 32),)),
        "w_first": bell_draw(key_list[10], (D, FF), D ** -0.5, 0.125, ((0, 32),)),
        "w_second": bell_draw(key_list[11], (D, FF), D ** -0.5, 0.125, ((0, 32),)),
        "w_down": bell_draw(key_list[12], (FF, D), FF ** -0.5, 0.078125, ((0, 32),)),
    }


@jax.custom_vjp
def low(v):
    return lax.optimization_barrier(v.astype(jnp.bfloat16)).astype(jnp.float32)

@jax.custom_vjp
def low_back(v):
    return v

def low_keep(v):
    return (low(v), None)

def low_pass(kept, grad):
    return (grad,)

def back_keep(v):
    return (v, None)

def back_low(kept, grad):
    return (low(grad),)
low.defvjp(low_keep, low_pass)
low_back.defvjp(back_keep, back_low)

def srms(tensor):
    return tensor * lax.rsqrt(lax.optimization_barrier(jnp.mean(tensor * tensor, axis=-1, keepdims=True)) + 1e-06)

def matmul(left_side, right_side):
    return jnp.dot(left_side, right_side, precision=lax.Precision.HIGHEST, preferred_element_type=jnp.float32)

def decayed_attention(query, key_rows, value_rows, segment, decay_rate):
    query = query.reshape(LEN, HEADS, HEAD_DIM)
    key_rows = key_rows.reshape(LEN, HEADS, HEAD_DIM)
    value_rows = value_rows.reshape(LEN, HEADS, HEAD_DIM)
    position = jnp.arange(LEN)
    distance = jnp.maximum(position[:, None] - position[None, :], 0).astype(jnp.float32)
    allowed = (position[:, None] >= position[None, :]) & (segment[:, None] == segment[None, :])
    weights = jnp.where(allowed[None], jnp.exp(-decay_rate[:, None, None] * distance[None]), 0.0)
    scores = jnp.einsum('thd,jhd->htj', query, key_rows, precision=lax.Precision.HIGHEST) * weights
    mixed = jnp.einsum('htj,jhd->thd', scores, value_rows, precision=lax.Precision.HIGHEST)
    return mixed.reshape(LEN, D)

def layer(block_in, weights, segment, decay_rate):
    w_query, w_key, w_value, w_gate, w_out, w_first, w_second, w_down = weights
    group_size = block_in.shape[0]
    flat_in = block_in.reshape(-1, D)
    normed = low(srms(flat_in))
    query = low(jax.nn.silu(low_back(matmul(normed, w_query))))
    key_rows = low(jax.nn.silu(low_back(matmul(normed, w_key))))
    value_rows = low(jax.nn.silu(low_back(matmul(normed, w_value))))
    gate_act = jax.nn.silu(low_back(matmul(normed, w_gate)))

    def one_sequence(pieces):
        return decayed_attention(pieces[0], pieces[1], pieces[2], pieces[3], decay_rate)
    mixed = lax.map(jax.checkpoint(one_sequence), (query.reshape(group_size, LEN, D), key_rows.reshape(group_size, LEN, D), value_rows.reshape(group_size, LEN, D), segment))
    mixed = low_back(mixed.reshape(-1, D))
    joined = low(srms(mixed) * gate_act)
    hidden = flat_in + low_back(matmul(joined, w_out))
    second = low(srms(hidden))
    part_one = low_back(matmul(second, w_first))
    part_two = low_back(matmul(second, w_second))
    glu_rows = low(part_one * part_two)
    final_rows = hidden + low_back(matmul(glu_rows, w_down))
    return final_rows.reshape(group_size, LEN, D)

def reference(inputs, teacher, segment_ids, valid, decay_rate, w_query, w_key, w_value, w_gate, w_out, w_first, w_second, w_down):
    weights = tuple((weight.astype(jnp.float32) for weight in (w_query, w_key, w_value, w_gate, w_out, w_first, w_second, w_down)))
    valid_count = jnp.sum(valid).astype(jnp.float32)
    group_size = 2 if SEQS % 2 == 0 else 1
    group_count = SEQS // group_size
    blocks = (inputs.reshape(group_count, group_size, LEN, D), teacher.reshape(group_count, group_size, LEN, D), segment_ids.reshape(group_count, group_size, LEN), valid.reshape(group_count, group_size, LEN))

    def group_step(carried, block_seq):
        grads, loss_sum = carried
        block_in, block_teacher, block_segment, block_valid = block_seq

        def forward(block_x, block_weights):
            return layer(block_x, block_weights, block_segment, decay_rate)
        out_rows, pullback = jax.vjp(forward, block_in.astype(jnp.float32), weights)
        error_rows = out_rows - block_teacher.astype(jnp.float32)
        keep_mask = block_valid.astype(jnp.float32)[..., None]
        loss_sum = loss_sum + jnp.sum(keep_mask * error_rows * error_rows)
        cotangent = TOKENS / valid_count * keep_mask * error_rows
        grad_in, grad_weights = pullback(cotangent)
        grads = jax.tree.map(jnp.add, grads, grad_weights)
        return ((grads, loss_sum), (out_rows.astype(jnp.bfloat16), grad_in))
    start_grads = tuple((jnp.zeros(weight.shape, jnp.float32) for weight in weights))
    (grads, loss_sum), (outputs, input_grads) = lax.scan(group_step, (start_grads, jnp.zeros((), jnp.float32)), blocks)
    mse_loss = loss_sum / (D * valid_count)
    return (outputs.reshape(SEQS, LEN, D), mse_loss, input_grads.reshape(SEQS, LEN, D), grads[0], grads[1], grads[2], grads[3], grads[4], grads[5], grads[6], grads[7])
```

```python
import functools

import jax
import jax.numpy as jnp
from jax import lax
from jax.experimental import pallas as pl
from jax.experimental.pallas import tpu as pltpu
from jax.sharding import PartitionSpec as P

CHUNK = 256
WIDE = jnp.float32
LOW = jnp.bfloat16
VMEM_BYTES = 56 * 1024 * 1024


def dot(left, right, left_dim=1, right_dim=0):
    return lax.dot_general(
        left, right, (((left_dim,), (right_dim,)), ((), ())), preferred_element_type=WIDE
    )


def decays(rate, place_col, place_row, chunk):
    rows = jnp.exp(-rate * place_col)
    cols = jnp.exp(rate * place_row)
    entry = jnp.exp(-rate * (place_col + 1.0))
    tail = jnp.exp(-rate * (chunk - 1.0 - place_col))
    return rows, cols, entry, tail


def masks(bounds_ref, seg_col, seg_row, n, chunk):
    before = bounds_ref[n]
    last = bounds_ref[n + 1]
    row = lax.broadcasted_iota(jnp.int32, (chunk, chunk), 0)
    col = lax.broadcasted_iota(jnp.int32, (chunk, chunk), 1)
    inner = (seg_col == seg_row) & (row >= col)
    return inner, seg_col == before, seg_col == last, jnp.where(before == last, 1.0, 0.0)


def places(chunk):
    place_col = lax.broadcasted_iota(jnp.int32, (chunk, 1), 0).astype(WIDE)
    place_row = lax.broadcasted_iota(jnp.int32, (1, chunk), 1).astype(WIDE)
    return place_col, place_row


def attend_kernel(
    heads, hd, rate_ref, bounds_ref, segc_ref, segr_ref, z_ref, au_ref, a_ref, ss_ref, st_ref, state
):
    n = pl.program_id(0)
    chunk = z_ref.shape[0]

    @pl.when(n == 0)
    def _():
        state[...] = jnp.zeros_like(state)

    inner, entry_on, tail_on, carry = masks(bounds_ref, segc_ref[...], segr_ref[...], n, chunk)
    place_col, place_row = places(chunk)
    total = jnp.zeros((chunk, 1), WIDE)
    for h in range(heads):
        rate = rate_ref[h]
        base = h * 4 * hd
        zq, zk, zv, zu = (z_ref[:, base + i * hd : base + (i + 1) * hd] for i in range(4))
        q = (zq * jax.nn.sigmoid(zq)).astype(LOW)
        k = (zk * jax.nn.sigmoid(zk)).astype(LOW)
        v = (zv * jax.nn.sigmoid(zv)).astype(LOW)
        u = zu * jax.nn.sigmoid(zu)
        rows, cols, entry, tail = decays(rate, place_col, place_row, chunk)
        scores = dot(q, k, 1, 1)
        weighted = jnp.where(inner, scores * rows * cols, 0.0).astype(LOW)
        held = state[h]
        st_ref[0, h] = held.astype(LOW)
        a = dot(weighted, v) + jnp.where(entry_on, entry, 0.0) * dot(q, held.astype(LOW))
        kt = (k.astype(WIDE) * jnp.where(tail_on, tail, 0.0)).astype(LOW)
        state[h] = carry * jnp.exp(jnp.full((1, 1), -rate * chunk, WIDE)) * held + dot(kt, v, 0, 0)
        a_ref[:, h * hd : (h + 1) * hd] = a
        au_ref[:, h * hd : (h + 1) * hd] = (a * u).astype(LOW)
        total = total + jnp.sum(a * a, axis=1, keepdims=True)
    ss_ref[...] = total


def attend(z, seg, bounds, rates, heads, hd):
    length = z.shape[0]
    count = length // CHUNK
    block = lambda width: pl.BlockSpec((CHUNK, width), lambda n, *_: (n, 0))
    return pl.pallas_call(
        functools.partial(attend_kernel, heads, hd),
        grid_spec=pltpu.PrefetchScalarGridSpec(
            num_scalar_prefetch=2,
            grid=(count,),
            in_specs=[
                block(1),
                pl.BlockSpec((1, CHUNK), lambda n, *_: (0, n)),
                block(heads * 4 * hd),
            ],
            out_specs=[
                block(heads * hd),
                block(heads * hd),
                block(1),
                pl.BlockSpec((1, heads, hd, hd), lambda n, *_: (n, 0, 0, 0)),
            ],
            scratch_shapes=[pltpu.VMEM((heads, hd, hd), WIDE)],
        ),
        out_shape=[
            jax.ShapeDtypeStruct((length, heads * hd), LOW),
            jax.ShapeDtypeStruct((length, heads * hd), WIDE),
            jax.ShapeDtypeStruct((length, 1), WIDE),
            jax.ShapeDtypeStruct((count, heads, hd, hd), LOW),
        ],
        compiler_params=pltpu.CompilerParams(vmem_limit_bytes=VMEM_BYTES),
        cost_estimate=pl.CostEstimate(
            flops=length * heads * hd * CHUNK * 6,
            bytes_accessed=length * heads * hd * 22,
            transcendentals=length * heads * hd * 4,
        ),
        name="attend",
    )(rates, bounds, seg.reshape(length, 1), seg.reshape(1, length), z)


def slope(z):
    sg = jax.nn.sigmoid(z)
    return sg * (1.0 + z * (1.0 - sg))


def attend_back_kernel(
    heads,
    hd,
    count,
    rate_ref,
    bounds_ref,
    segc_ref,
    segr_ref,
    z_ref,
    a_ref,
    dj_ref,
    ra_ref,
    m_ref,
    st_ref,
    dz_ref,
    o_ref,
    later,
):
    n = count - 1 - pl.program_id(0)
    chunk = z_ref.shape[0]

    @pl.when(pl.program_id(0) == 0)
    def _():
        later[...] = jnp.zeros_like(later)

    inner, entry_on, tail_on, carry = masks(bounds_ref, segc_ref[...], segr_ref[...], n, chunk)
    place_col, place_row = places(chunk)
    ra = ra_ref[...]
    m = m_ref[...]
    for h in range(heads):
        rate = rate_ref[h]
        base = h * 4 * hd
        span = slice(h * hd, (h + 1) * hd)
        zq, zk, zv, zu = (z_ref[:, base + i * hd : base + (i + 1) * hd] for i in range(4))
        q = (zq * jax.nn.sigmoid(zq)).astype(LOW)
        k = (zk * jax.nn.sigmoid(zk)).astype(LOW)
        v = (zv * jax.nn.sigmoid(zv)).astype(LOW)
        u = zu * jax.nn.sigmoid(zu)
        an = a_ref[:, span] * ra
        dj = dj_ref[:, span]
        o_ref[:, span] = (an * u).astype(LOW)
        da = (ra * (dj * u - an * m)).astype(LOW)
        rows, cols, entry, tail = decays(rate, place_col, place_row, chunk)
        entry = jnp.where(entry_on, entry, 0.0)
        tail = jnp.where(tail_on, tail, 0.0)
        decay = jnp.where(inner, rows * cols, 0.0)
        weighted = (dot(q, k, 1, 1) * decay).astype(LOW)
        grads = (dot(da, v, 1, 1) * decay).astype(LOW)
        held = st_ref[0, h]
        after = later[h]
        after_low = after.astype(LOW)
        dq = dot(grads, k) + entry * dot(da, held, 1, 1)
        dk = dot(grads, q, 0, 0) + tail * dot(v, after_low, 1, 1)
        dv = dot(weighted, da, 0, 0) + tail * dot(k, after_low)
        qe = (q.astype(WIDE) * entry).astype(LOW)
        later[h] = carry * jnp.exp(jnp.full((1, 1), -rate * chunk, WIDE)) * after + dot(qe, da, 0, 0)
        dz_ref[:, base : base + hd] = (dq * slope(zq)).astype(LOW)
        dz_ref[:, base + hd : base + 2 * hd] = (dk * slope(zk)).astype(LOW)
        dz_ref[:, base + 2 * hd : base + 3 * hd] = (dv * slope(zv)).astype(LOW)
        dz_ref[:, base + 3 * hd : base + 4 * hd] = (dj * an * slope(zu)).astype(LOW)


def attend_back(z, a, dj, ra, m, states, seg, bounds, rates, heads, hd):
    length = z.shape[0]
    count = length // CHUNK
    block = lambda width: pl.BlockSpec((CHUNK, width), lambda n, *_: (count - 1 - n, 0))
    return pl.pallas_call(
        functools.partial(attend_back_kernel, heads, hd, count),
        grid_spec=pltpu.PrefetchScalarGridSpec(
            num_scalar_prefetch=2,
            grid=(count,),
            in_specs=[
                block(1),
                pl.BlockSpec((1, CHUNK), lambda n, *_: (0, count - 1 - n)),
                block(heads * 4 * hd),
                block(heads * hd),
                block(heads * hd),
                block(1),
                block(1),
                pl.BlockSpec((1, heads, hd, hd), lambda n, *_: (count - 1 - n, 0, 0, 0)),
            ],
            out_specs=[block(heads * 4 * hd), block(heads * hd)],
            scratch_shapes=[pltpu.VMEM((heads, hd, hd), WIDE)],
        ),
        out_shape=[
            jax.ShapeDtypeStruct((length, heads * 4 * hd), LOW),
            jax.ShapeDtypeStruct((length, heads * hd), LOW),
        ],
        compiler_params=pltpu.CompilerParams(vmem_limit_bytes=VMEM_BYTES),
        cost_estimate=pl.CostEstimate(
            flops=length * heads * hd * CHUNK * 12,
            bytes_accessed=length * heads * hd * 34,
            transcendentals=length * heads * hd * 8,
        ),
        name="attend_back",
    )(rates, bounds, seg.reshape(length, 1), seg.reshape(1, length), z, a, dj, ra, m, states)


class Moves:
    def __init__(self):
        self.seq = lax.axis_size("seq")
        self.fsdp = lax.axis_size("fsdp")
        self.inner = 2 if self.fsdp == 8 else 4
        self.outer = self.fsdp // self.inner
        self.chips = self.seq // 2
        s = lax.axis_index("seq")
        f = lax.axis_index("fsdp")
        self.s, self.f = s, f
        self.chip, self.core = s // 2, s % 2
        self.out_at, self.in_at = f // self.inner, f % self.inner
        chips, inner, outer = self.chips, self.inner, self.outer
        self.core_perm = [(i, i ^ 1) for i in range(self.seq)]
        self.chip_perm = [
            (x * 2 + c, (x + 1) % chips * 2 + c) for x in range(chips) for c in range(2)
        ]
        self.out_perm = [
            (o * inner + i, (o + 1) % outer * inner + i)
            for o in range(outer)
            for i in range(inner)
        ]
        self.in_perm = [
            (o * inner + i, o * inner + (i + 1) % inner)
            for o in range(outer)
            for i in range(inner)
        ]

    def to_core(self, v):
        return lax.ppermute(v, "seq", self.core_perm)

    def to_chip(self, v):
        return lax.ppermute(v, "seq", self.chip_perm)

    def to_out(self, v):
        return lax.ppermute(v, "fsdp", self.out_perm)

    def to_in(self, v):
        return lax.ppermute(v, "fsdp", self.in_perm)

    def gather_seq(self, v):
        whole = jnp.zeros((self.seq,) + v.shape, v.dtype)
        now = v
        for k in range(self.chips):
            later = self.to_chip(now) if k < self.chips - 1 else None
            other = self.to_core(now)
            chip = (self.chip - k) % self.chips
            whole = lax.dynamic_update_index_in_dim(whole, now, chip * 2 + self.core, 0)
            whole = lax.dynamic_update_index_in_dim(whole, other, chip * 2 + 1 - self.core, 0)
            now = later
        return whole.reshape((-1,) + v.shape[1:])

    def scatter_seq(self, part, kind):
        held = None
        for k in range(self.chips):
            term = part((self.chip - 1 - k) % self.chips)
            give = lax.dynamic_index_in_dim(term, 1 - self.core, 0, False)
            keep = lax.dynamic_index_in_dim(term, self.core, 0, False)
            total = keep.astype(WIDE) + self.to_core(give).astype(WIDE)
            if held is not None:
                total = total + held.astype(WIDE)
            if k < self.chips - 1:
                held = self.to_chip(total.astype(kind))
        return total

    def swap_seq(self, blocks):
        pick = lambda i: lax.dynamic_index_in_dim(blocks, i, 0, False)
        whole = lax.dynamic_update_index_in_dim(jnp.zeros_like(blocks), pick(self.s), self.s, 0)
        for dx in range(self.chips):
            for dc in range(2):
                if dx == 0 and dc == 0:
                    continue
                to = (self.chip + dx) % self.chips * 2 + (self.core ^ dc)
                source = (self.chip - dx) % self.chips * 2 + (self.core ^ dc)
                perm = [
                    (x * 2 + c, (x + dx) % self.chips * 2 + (c ^ dc))
                    for x in range(self.chips)
                    for c in range(2)
                ]
                got = lax.ppermute(pick(to), "seq", perm)
                whole = lax.dynamic_update_index_in_dim(whole, got, source, 0)
        return whole

    def gather_fsdp(self, v):
        a, r, n = v.shape
        whole = jnp.zeros((a, self.fsdp, r, n), v.dtype)
        now = v
        for k in range(self.outer):
            later = self.to_out(now) if k < self.outer - 1 else None
            out_at = (self.out_at - k) % self.outer
            piece = now
            for j in range(self.inner):
                in_at = (self.in_at - j) % self.inner
                whole = lax.dynamic_update_slice_in_dim(
                    whole, piece[:, None], out_at * self.inner + in_at, 1
                )
                if j < self.inner - 1:
                    piece = self.to_in(piece)
            now = later
        return whole.reshape(a * self.fsdp * r, n)

    def scatter_fsdp(self, g, a):
        n = g.shape[1]
        r = g.shape[0] // (a * self.fsdp)
        g = g.reshape(a, self.fsdp, r, n)
        pick = lambda o, i: lax.dynamic_slice_in_dim(g, o * self.inner + i, 1, 1)[:, 0]
        held = None
        for k in range(self.outer):
            out_at = (self.out_at - 1 - k) % self.outer
            total = None
            for j in range(self.inner):
                term = pick(out_at, (self.in_at - 1 - j) % self.inner).astype(WIDE)
                total = term if total is None else term + self.to_in(total.astype(LOW)).astype(WIDE)
            if held is not None:
                total = total + held.astype(WIDE)
            if k < self.outer - 1:
                held = self.to_out(total.astype(LOW))
        return total

    def sum_all(self, v):
        for axis, size in (("seq", self.seq), ("fsdp", self.fsdp)):
            step = 1
            while step < size:
                v = v + lax.ppermute(v, axis, [(i, i ^ step) for i in range(size)])
                step *= 2
        return v


def on_device(
    inputs,
    teacher,
    segment_ids,
    valid,
    decay_rate,
    w_query,
    w_key,
    w_value,
    w_gate,
    w_out,
    w_first,
    w_second,
    w_down,
):
    move = Moves()
    seq = move.seq
    batch, block_len, width = inputs.shape
    assert batch == 1
    heads_all = decay_rate.shape[0]
    hd = width // heads_all
    heads = heads_all // seq
    own_rows = w_query.shape[0]
    ff = w_first.shape[1]
    ffs = ff // seq
    cols = heads * 4 * hd

    keep = valid.astype(WIDE).reshape(block_len, 1)
    count = move.sum_all(jnp.sum(keep).reshape(1, 1))

    seg = move.gather_seq(segment_ids.reshape(block_len))
    length = seg.shape[0]
    bounds = jnp.concatenate([jnp.full((1,), -1, jnp.int32), seg[CHUNK - 1 :: CHUNK]])
    rates = lax.dynamic_slice_in_dim(decay_rate, move.s * heads, heads, 0)

    attn_own = jnp.stack(
        [w.reshape(own_rows, seq, heads, hd) for w in (w_query, w_key, w_value, w_gate)], axis=3
    )
    attn_own = attn_own.reshape(own_rows, seq, cols).transpose(1, 0, 2)
    glu_own = jnp.stack([w_first.reshape(own_rows, seq, ffs), w_second.reshape(own_rows, seq, ffs)])
    glu_own = glu_own.transpose(2, 0, 1, 3)

    full_attn = move.gather_fsdp(move.swap_seq(attn_own))
    full_out = move.gather_fsdp(w_out[None])
    glu_mid = move.swap_seq(glu_own)
    full_first = move.gather_fsdp(glu_mid[:, 0])
    full_second = move.gather_fsdp(glu_mid[:, 1])
    full_down = move.gather_fsdp(w_down[None])

    x32 = inputs.reshape(block_len, width).astype(WIDE)
    r1 = lax.rsqrt(jnp.mean(x32 * x32, axis=-1, keepdims=True) + 1e-6)
    n1 = x32 * r1
    n1_all = move.gather_seq(n1.astype(LOW))
    z = dot(n1_all, full_attn)
    au, a, ss, states = attend(z, seg, bounds, rates, heads, hd)

    def rows_of(v, chip):
        return lax.dynamic_slice_in_dim(v, chip * 2 * block_len, 2 * block_len, 0)

    def scatter_product(pairs):
        def part(chip):
            total = sum(dot(rows_of(v, chip), w, 1, d) for v, w, d in pairs)
            return total.astype(LOW).reshape(2, block_len, -1)

        return move.scatter_seq(part, LOW)

    out_rows = scatter_product([(au, full_out, 0)])
    ss_own = move.scatter_seq(lambda chip: rows_of(ss, chip).reshape(2, block_len, 1), WIDE)
    ra = lax.rsqrt(ss_own / width + 1e-6)
    mixed_out = out_rows * ra
    hsum = x32 + mixed_out
    r2 = lax.rsqrt(jnp.mean(hsum * hsum, axis=-1, keepdims=True) + 1e-6)
    m2 = hsum * r2
    n2_all = move.gather_seq(m2.astype(LOW))

    g1 = dot(n2_all, full_first)
    g2 = dot(n2_all, full_second)
    p = (g1 * g2).astype(LOW)
    g1 = g1.astype(LOW)
    g2 = g2.astype(LOW)
    y = hsum + scatter_product([(p, full_down, 0)])
    layer_out = y.astype(LOW).reshape(1, block_len, width)

    error = y - teacher.reshape(block_len, width).astype(WIDE)
    loss = move.sum_all(jnp.sum(keep * error * error).reshape(1, 1)) / (width * count)
    tokens = block_len * seq * move.fsdp
    dy = tokens / count * keep * error
    dy_all = move.gather_seq(dy.astype(LOW))

    grad_down = dot(p, dy_all, 0, 0).astype(LOW)
    dp = dot(dy_all, full_down, 1, 1)
    dg1 = (dp * g2.astype(WIDE)).astype(LOW)
    dg2 = (dp * g1.astype(WIDE)).astype(LOW)
    dn2 = scatter_product([(dg1, full_first, 1), (dg2, full_second, 1)])
    grad_first = dot(n2_all, dg1, 0, 0).astype(LOW)
    grad_second = dot(n2_all, dg2, 0, 0).astype(LOW)
    dh = dy + r2 * (dn2 - m2 * jnp.mean(dn2 * m2, axis=-1, keepdims=True))
    dhb = dh.astype(LOW)
    mean_own = jnp.mean(dhb.astype(WIDE) * mixed_out, axis=-1, keepdims=True)
    dh_all = move.gather_seq(dhb)
    small = move.gather_seq(jnp.concatenate([ra, mean_own], axis=1))

    dj = dot(dh_all, full_out, 1, 1)
    dz, o = attend_back(
        z, a, dj, small[:, :1], small[:, 1:], states, seg, bounds, rates, heads, hd
    )
    grad_out = dot(o, dh_all, 0, 0).astype(LOW)
    grad_attn = dot(n1_all, dz, 0, 0).astype(LOW)
    dn1 = scatter_product([(dz, full_attn, 1)])
    input_grad = dh + r1 * (dn1 - n1 * jnp.mean(dn1 * n1, axis=-1, keepdims=True))

    share_down = move.scatter_fsdp(grad_down, 1)[0]
    share_first = move.scatter_fsdp(grad_first, seq).astype(LOW)
    share_second = move.scatter_fsdp(grad_second, seq).astype(LOW)
    share_first = move.swap_seq(share_first).transpose(1, 0, 2).reshape(own_rows, ff).astype(WIDE)
    share_second = move.swap_seq(share_second).transpose(1, 0, 2).reshape(own_rows, ff).astype(WIDE)
    share_out = move.scatter_fsdp(grad_out, 1)[0]
    share_attn = move.swap_seq(move.scatter_fsdp(grad_attn, seq).astype(LOW))
    share_attn = share_attn.reshape(seq, own_rows, heads, 4, hd).transpose(3, 1, 0, 2, 4)
    share_attn = share_attn.reshape(4, own_rows, width).astype(WIDE)

    return (
        layer_out,
        loss.reshape(()),
        input_grad.reshape(1, block_len, width),
        share_attn[0],
        share_attn[1],
        share_attn[2],
        share_attn[3],
        share_out,
        share_first,
        share_second,
        share_down,
    )


def solution(mesh):
    rows = P(("seq", "fsdp"), None)
    tokens = P("fsdp", "seq", None)
    return jax.shard_map(
        on_device,
        mesh=mesh,
        in_specs=(tokens, tokens, P("fsdp", "seq"), P("fsdp", "seq"), P()) + (rows,) * 8,
        out_specs=(tokens, P(), tokens) + (rows,) * 8,
        check_vma=False,
    )
```

```python
import functools

import jax
import jax.numpy as jnp
from jax import lax
from jax.experimental import pallas as pl
from jax.experimental.pallas import tpu as pltpu
from jax.sharding import PartitionSpec as P

CHUNK = 256
WIDE = jnp.float32
LOW = jnp.bfloat16
VMEM_BYTES = 56 * 1024 * 1024


def dot(left, right, left_dim=1, right_dim=0):
    return lax.dot_general(
        left, right, (((left_dim,), (right_dim,)), ((), ())), preferred_element_type=WIDE
    )


def decays(rate, place_col, place_row, chunk):
    rows = jnp.exp(-rate * place_col)
    cols = jnp.exp(rate * place_row)
    entry = jnp.exp(-rate * (place_col + 1.0))
    tail = jnp.exp(-rate * (chunk - 1.0 - place_col))
    return rows, cols, entry, tail


def masks(bounds_ref, seg_col, seg_row, n, chunk):
    before = bounds_ref[n]
    last = bounds_ref[n + 1]
    row = lax.broadcasted_iota(jnp.int32, (chunk, chunk), 0)
    col = lax.broadcasted_iota(jnp.int32, (chunk, chunk), 1)
    inner = (seg_col == seg_row) & (row >= col)
    return inner, seg_col == before, seg_col == last, jnp.where(before == last, 1.0, 0.0)


def places(chunk):
    place_col = lax.broadcasted_iota(jnp.int32, (chunk, 1), 0).astype(WIDE)
    place_row = lax.broadcasted_iota(jnp.int32, (1, chunk), 1).astype(WIDE)
    return place_col, place_row


def attend_kernel(
    heads, hd, rate_ref, bounds_ref, segc_ref, segr_ref, z_ref, au_ref, a_ref, ss_ref, st_ref, state
):
    n = pl.program_id(0)
    chunk = z_ref.shape[0]

    @pl.when(n == 0)
    def _():
        state[...] = jnp.zeros_like(state)

    inner, entry_on, tail_on, carry = masks(bounds_ref, segc_ref[...], segr_ref[...], n, chunk)
    place_col, place_row = places(chunk)
    total = jnp.zeros((chunk, 1), WIDE)
    for h in range(heads):
        rate = rate_ref[h]
        base = h * 4 * hd
        zq, zk, zv, zu = (z_ref[:, base + i * hd : base + (i + 1) * hd] for i in range(4))
        q = (zq * jax.nn.sigmoid(zq)).astype(LOW)
        k = (zk * jax.nn.sigmoid(zk)).astype(LOW)
        v = (zv * jax.nn.sigmoid(zv)).astype(LOW)
        u = zu * jax.nn.sigmoid(zu)
        rows, cols, entry, tail = decays(rate, place_col, place_row, chunk)
        scores = dot(q, k, 1, 1)
        weighted = jnp.where(inner, scores * rows * cols, 0.0).astype(LOW)
        held = state[h]
        st_ref[0, h] = held.astype(LOW)
        a = dot(weighted, v) + jnp.where(entry_on, entry, 0.0) * dot(q, held.astype(LOW))
        kt = (k.astype(WIDE) * jnp.where(tail_on, tail, 0.0)).astype(LOW)
        state[h] = carry * jnp.exp(jnp.full((1, 1), -rate * chunk, WIDE)) * held + dot(kt, v, 0, 0)
        a_ref[:, h * hd : (h + 1) * hd] = a
        au_ref[:, h * hd : (h + 1) * hd] = (a * u).astype(LOW)
        total = total + jnp.sum(a * a, axis=1, keepdims=True)
    ss_ref[...] = total


def attend(z, seg, bounds, rates, heads, hd):
    length = z.shape[0]
    count = length // CHUNK
    block = lambda width: pl.BlockSpec((CHUNK, width), lambda n, *_: (n, 0))
    return pl.pallas_call(
        functools.partial(attend_kernel, heads, hd),
        grid_spec=pltpu.PrefetchScalarGridSpec(
            num_scalar_prefetch=2,
            grid=(count,),
            in_specs=[
                block(1),
                pl.BlockSpec((1, CHUNK), lambda n, *_: (0, n)),
                block(heads * 4 * hd),
            ],
            out_specs=[
                block(heads * hd),
                block(heads * hd),
                block(1),
                pl.BlockSpec((1, heads, hd, hd), lambda n, *_: (n, 0, 0, 0)),
            ],
            scratch_shapes=[pltpu.VMEM((heads, hd, hd), WIDE)],
        ),
        out_shape=[
            jax.ShapeDtypeStruct((length, heads * hd), LOW),
            jax.ShapeDtypeStruct((length, heads * hd), WIDE),
            jax.ShapeDtypeStruct((length, 1), WIDE),
            jax.ShapeDtypeStruct((count, heads, hd, hd), LOW),
        ],
        compiler_params=pltpu.CompilerParams(vmem_limit_bytes=VMEM_BYTES),
        cost_estimate=pl.CostEstimate(
            flops=length * heads * hd * CHUNK * 6,
            bytes_accessed=length * heads * hd * 22,
            transcendentals=length * heads * hd * 4,
        ),
        name="attend",
    )(rates, bounds, seg.reshape(length, 1), seg.reshape(1, length), z)


def slope(z):
    sg = jax.nn.sigmoid(z)
    return sg * (1.0 + z * (1.0 - sg))


def attend_back_kernel(
    heads,
    hd,
    count,
    rate_ref,
    bounds_ref,
    segc_ref,
    segr_ref,
    z_ref,
    a_ref,
    dj_ref,
    ra_ref,
    m_ref,
    st_ref,
    dz_ref,
    o_ref,
    later,
):
    n = count - 1 - pl.program_id(0)
    chunk = z_ref.shape[0]

    @pl.when(pl.program_id(0) == 0)
    def _():
        later[...] = jnp.zeros_like(later)

    inner, entry_on, tail_on, carry = masks(bounds_ref, segc_ref[...], segr_ref[...], n, chunk)
    place_col, place_row = places(chunk)
    ra = ra_ref[...]
    m = m_ref[...]
    for h in range(heads):
        rate = rate_ref[h]
        base = h * 4 * hd
        span = slice(h * hd, (h + 1) * hd)
        zq, zk, zv, zu = (z_ref[:, base + i * hd : base + (i + 1) * hd] for i in range(4))
        q = (zq * jax.nn.sigmoid(zq)).astype(LOW)
        k = (zk * jax.nn.sigmoid(zk)).astype(LOW)
        v = (zv * jax.nn.sigmoid(zv)).astype(LOW)
        u = zu * jax.nn.sigmoid(zu)
        an = a_ref[:, span] * ra
        dj = dj_ref[:, span]
        o_ref[:, span] = (an * u).astype(LOW)
        da = (ra * (dj * u - an * m)).astype(LOW)
        rows, cols, entry, tail = decays(rate, place_col, place_row, chunk)
        entry = jnp.where(entry_on, entry, 0.0)
        tail = jnp.where(tail_on, tail, 0.0)
        decay = jnp.where(inner, rows * cols, 0.0)
        weighted = (dot(q, k, 1, 1) * decay).astype(LOW)
        grads = (dot(da, v, 1, 1) * decay).astype(LOW)
        held = st_ref[0, h]
        after = later[h]
        after_low = after.astype(LOW)
        dq = dot(grads, k) + entry * dot(da, held, 1, 1)
        dk = dot(grads, q, 0, 0) + tail * dot(v, after_low, 1, 1)
        dv = dot(weighted, da, 0, 0) + tail * dot(k, after_low)
        qe = (q.astype(WIDE) * entry).astype(LOW)
        later[h] = carry * jnp.exp(jnp.full((1, 1), -rate * chunk, WIDE)) * after + dot(qe, da, 0, 0)
        dz_ref[:, base : base + hd] = (dq * slope(zq)).astype(LOW)
        dz_ref[:, base + hd : base + 2 * hd] = (dk * slope(zk)).astype(LOW)
        dz_ref[:, base + 2 * hd : base + 3 * hd] = (dv * slope(zv)).astype(LOW)
        dz_ref[:, base + 3 * hd : base + 4 * hd] = (dj * an * slope(zu)).astype(LOW)


def attend_back(z, a, dj, ra, m, states, seg, bounds, rates, heads, hd):
    length = z.shape[0]
    count = length // CHUNK
    block = lambda width: pl.BlockSpec((CHUNK, width), lambda n, *_: (count - 1 - n, 0))
    return pl.pallas_call(
        functools.partial(attend_back_kernel, heads, hd, count),
        grid_spec=pltpu.PrefetchScalarGridSpec(
            num_scalar_prefetch=2,
            grid=(count,),
            in_specs=[
                block(1),
                pl.BlockSpec((1, CHUNK), lambda n, *_: (0, count - 1 - n)),
                block(heads * 4 * hd),
                block(heads * hd),
                block(heads * hd),
                block(1),
                block(1),
                pl.BlockSpec((1, heads, hd, hd), lambda n, *_: (count - 1 - n, 0, 0, 0)),
            ],
            out_specs=[block(heads * 4 * hd), block(heads * hd)],
            scratch_shapes=[pltpu.VMEM((heads, hd, hd), WIDE)],
        ),
        out_shape=[
            jax.ShapeDtypeStruct((length, heads * 4 * hd), LOW),
            jax.ShapeDtypeStruct((length, heads * hd), LOW),
        ],
        compiler_params=pltpu.CompilerParams(vmem_limit_bytes=VMEM_BYTES),
        cost_estimate=pl.CostEstimate(
            flops=length * heads * hd * CHUNK * 12,
            bytes_accessed=length * heads * hd * 34,
            transcendentals=length * heads * hd * 8,
        ),
        name="attend_back",
    )(rates, bounds, seg.reshape(length, 1), seg.reshape(1, length), z, a, dj, ra, m, states)


def empty(shape, kind):
    return pl.pallas_call(
        lambda out: None,
        out_shape=jax.ShapeDtypeStruct(shape, kind),
        out_specs=pl.BlockSpec(memory_space=pl.ANY),
        name="empty",
    )()


def pack_kernel(seq, heads, hd, *refs):
    weights, glu, attn_out, glu_outs = refs[:4], refs[4:6], refs[6], refs[7:]
    for i in range(seq):
        for h in range(heads):
            for m, w in enumerate(weights):
                to, at = (h * 4 + m) * hd, (i * heads + h) * hd
                attn_out[i, :, to : to + hd] = w[:, at : at + hd]
        for w, out in zip(glu, glu_outs):
            n = out.shape[2]
            out[i] = w[:, i * n : (i + 1) * n]


def pack_columns(weights, glu, seq, heads, hd):
    r, kind = weights[0].shape[0], weights[0].dtype
    n = glu[0].shape[1] // seq
    return pl.pallas_call(
        functools.partial(pack_kernel, seq, heads, hd),
        out_shape=[jax.ShapeDtypeStruct((seq, r, heads * 4 * hd), kind)]
        + [jax.ShapeDtypeStruct((seq, r, n), kind)] * 2,
        compiler_params=pltpu.CompilerParams(vmem_limit_bytes=VMEM_BYTES),
        name="pack_columns",
    )(*weights, *glu)


class Net:
    def __init__(self, shape, send_sem, recv_sem, local_sem):
        self.seq, self.fsdp, self.inner = shape
        self.outer = self.fsdp // self.inner
        self.chips = self.seq // 2
        self.send_sem, self.recv_sem, self.local_sem = send_sem, recv_sem, local_sem
        self.used = 0
        self.locals = 0
        self.s, self.f = lax.axis_index("seq"), lax.axis_index("fsdp")
        self.chip, self.core = self.s // 2, self.s % 2
        self.o, self.i = self.f // self.inner, self.f % self.inner
        self.sent = []

    def seq_peers(self):
        for dx in range(self.chips):
            for dc in range(2):
                if dx or dc:
                    yield dx, dc, lax.rem(self.chip + dx, self.chips) * 2 + lax.rem(self.core + dc, 2)

    def at_seq(self, s):
        return (s, self.f)

    def at_inner(self, j):
        return (self.s, self.o * self.inner + lax.rem(self.i + j, self.inner))

    def at_outer(self, k):
        return (self.s, lax.rem(self.o + k, self.outer) * self.inner + self.i)

    def barrier(self):
        peers = [self.at_seq(s) for _, _, s in self.seq_peers()]
        peers += [self.at_inner(j) for j in range(1, self.inner)]
        peers += [self.at_outer(1), self.at_outer(self.outer - 1)]
        sem = pltpu.get_barrier_semaphore()
        for peer in peers:
            pl.semaphore_signal(sem, inc=1, device_id=peer, device_id_type=pl.DeviceIdType.MESH)
        pl.semaphore_wait(sem, len(peers))

    def send(self, src, dst, device):
        copy = pltpu.make_async_remote_copy(
            src_ref=src,
            dst_ref=dst,
            send_sem=self.send_sem.at[self.used],
            recv_sem=self.recv_sem.at[self.used],
            device_id=device,
            device_id_type=pl.DeviceIdType.MESH,
        )
        self.used += 1
        copy.start()
        self.sent.append(copy)
        return copy

    def copy(self, src, dst):
        copy = pltpu.make_async_copy(src, dst, self.local_sem.at[self.locals])
        self.locals += 1
        copy.start()
        return copy

    def finish(self):
        for copy in self.sent:
            copy.wait_send()
        self.sent = []


def net_shape(mesh_seq, mesh_fsdp):
    return mesh_seq, mesh_fsdp, 2 if mesh_fsdp == 8 else 4


class Ring:
    def __init__(self, net, piece, full):
        self.net, self.piece, self.full = net, piece, full
        self.copies = [net.copy(piece, full.at[:, net.o, net.i])]
        self.at = 0
        self.coming = None
        self.side = []

    def step(self):
        net, full = self.net, self.full
        if self.at >= net.outer:
            return
        if self.coming is not None:
            self.coming.wait_recv()
        spot = full.at[:, lax.rem(net.o + net.outer - self.at, net.outer), net.i]
        src = self.piece if self.at == 0 else spot
        self.coming = None
        if self.at < net.outer - 1:
            self.coming = net.send(src, spot, net.at_outer(1))
        for j in range(1, net.inner):
            self.side.append(net.send(src, spot, net.at_inner(j)))
        self.at += 1

    def done(self):
        while self.at < self.net.outer:
            self.step()
        for copy in self.side:
            copy.wait_recv()
        for copy in self.copies:
            copy.wait()


def swap(net, blocks, got):
    own = net.copy(blocks.at[net.s], got.at[net.s])
    coming = [
        net.send(blocks.at[s], got.at[net.s], net.at_seq(s)) for _, _, s in net.seq_peers()
    ]
    return own, coming


def arrive(pair):
    own, coming = pair
    own.wait()
    for copy in coming:
        copy.wait_recv()


class Rows:
    def __init__(self, net, own, whole):
        t = own.shape[0]
        self.net, self.whole = net, whole
        spot = lambda s: whole.at[pl.ds(pl.multiple_of(s * t, t), t)]
        self.spot = spot
        self.far = [
            net.send(own, spot(net.s), net.at_seq(lax.rem(net.chip + dx, net.chips) * 2 + net.core))
            for dx in range(1, net.chips)
        ]
        self.near = [net.send(own, spot(net.s), net.at_seq(net.chip * 2 + 1 - net.core))]
        self.own = net.copy(own, spot(net.s))

    def turn(self):
        net = self.net
        for dx, copy in zip(range(1, net.chips), self.far):
            copy.wait_recv()
            spot = self.spot(lax.rem(net.chip + net.chips - dx, net.chips) * 2 + net.core)
            self.near.append(net.send(spot, spot, net.at_seq(net.chip * 2 + 1 - net.core)))

    def done(self):
        for copy in self.near:
            copy.wait_recv()
        self.own.wait()


def gather_kernel(
    shape,
    attn_ref,
    first_ref,
    second_ref,
    out_ref,
    down_ref,
    n1_ref,
    seg_ref,
    attn_mid,
    first_mid,
    second_mid,
    full_attn,
    full_first,
    full_second,
    full_out,
    full_down,
    n1_all,
    seg_all,
    send_sem,
    recv_sem,
    local_sem,
):
    net = Net(shape, send_sem, recv_sem, local_sem)
    net.barrier()
    attn_swap = swap(net, attn_ref, attn_mid)
    seg_own = net.copy(seg_ref, seg_all.at[net.s])
    segs = [net.send(seg_ref, seg_all.at[net.s], net.at_seq(s)) for _, _, s in net.seq_peers()]
    first_swap = swap(net, first_ref, first_mid)
    second_swap = swap(net, second_ref, second_mid)
    rows = Rows(net, n1_ref, n1_all)
    arrive(attn_swap)
    rings = [Ring(net, attn_mid, full_attn)]
    rings[0].step()
    rings.append(Ring(net, out_ref, full_out))
    rings[0].step()
    rings[0].step()
    rings[0].step()
    arrive(first_swap)
    arrive(second_swap)
    rows.turn()
    rings.append(Ring(net, first_mid, full_first))
    rings.append(Ring(net, second_mid, full_second))
    rings.append(Ring(net, down_ref, full_down))
    for ring in rings[1:]:
        for _ in range(net.outer):
            ring.step()
    for ring in rings:
        ring.done()
    rows.done()
    seg_own.wait()
    for copy in segs:
        copy.wait_recv()
    net.finish()


HBM = pl.BlockSpec(memory_space=pl.ANY)


def gather_all(shape, attn, first, second, w_out, w_down, n1, seg):
    seq, fsdp, inner = shape
    outer = fsdp // inner
    like = lambda v, lead: jax.ShapeDtypeStruct(lead + v.shape[-2:], v.dtype)
    ring = lambda v: like(v, (v.shape[0], outer, inner))
    outs = [like(v, (seq,)) for v in (attn, first, second)]
    outs += [ring(v) for v in (attn, first, second, w_out, w_down)]
    outs.append(jax.ShapeDtypeStruct((seq * n1.shape[0], n1.shape[1]), n1.dtype))
    outs.append(jax.ShapeDtypeStruct((seq,) + seg.shape, seg.dtype))
    copies = 4 * (seq - 1) + 2 * seq + 5 * (outer * inner + outer)
    got = pl.pallas_call(
        functools.partial(gather_kernel, shape),
        in_specs=[HBM] * 7,
        out_specs=[HBM] * len(outs),
        out_shape=outs,
        scratch_shapes=[
            pltpu.SemaphoreType.DMA((copies,)),
            pltpu.SemaphoreType.DMA((copies,)),
            pltpu.SemaphoreType.DMA((16,)),
        ],
        compiler_params=pltpu.CompilerParams(
            collective_id=0, has_side_effects=True, vmem_limit_bytes=VMEM_BYTES
        ),
        name="gather_all",
    )(attn, first, second, w_out, w_down, n1, seg)
    flat = lambda v: v.reshape(-1, v.shape[-1])
    return [flat(v) for v in got[3:8]] + list(got[8:])


class Sum:
    def __init__(self, net, g, side, send, recv, load):
        self.net, self.g, self.side_ref = net, g, side
        self.send_buf, self.recv_buf, self.load = send, recv, load
        self.side = []
        self.ring = []
        for k in range(net.outer):
            o = self.spot(k)
            now = []
            for j in range(1, net.inner):
                to = lax.rem(net.i + j, net.inner)
                now.append(net.send(g.at[:, o, to], side.at[j - 1, :, o], net.at_inner(j)))
            self.side.append(now)
        self.at = 0

    def spot(self, k):
        return lax.rem(self.net.o + 2 * self.net.outer - 1 - k, self.net.outer)

    def step(self, final=None):
        net, k = self.net, self.at
        self.at += 1
        o = self.spot(k)
        terms = self.load
        loads = [net.copy(self.g.at[:, o, net.i], terms.at[0])]
        for j, copy in enumerate(self.side[k]):
            copy.wait_recv()
            loads.append(net.copy(self.side_ref.at[j, :, o], terms.at[j + 1]))
        if k > 0:
            self.ring[k - 1].wait_recv()
        for load in loads:
            load.wait()
        a = terms.shape[1]

        def one(i, _):
            total = terms[0, i].astype(WIDE)
            for j in range(1, net.inner):
                total = total + terms[j, i].astype(WIDE)
            if k > 0:
                total = total + self.recv_buf[k - 1, i].astype(WIDE)
            if k < net.outer - 1:
                self.send_buf[k, i] = total.astype(LOW)
            else:
                final(i, total)
            return 0

        lax.fori_loop(0, a, one, 0)
        if k < net.outer - 1:
            self.ring.append(net.send(self.send_buf.at[k], self.recv_buf.at[k], net.at_outer(1)))


def scatter_kernel(shape, heads, hd, *refs):
    names = ("down", "first", "second", "attn", "out")
    it = iter(refs)
    take = lambda: {name: next(it) for name in names}
    grads = take()
    o_down, o_first, o_second, o_out = (next(it) for _ in range(4))
    o_attn = [next(it) for _ in range(4)]
    sides, sends, recvs, loads = take(), take(), take(), take()
    totals = {name: next(it) for name in ("first", "second", "attn")}
    gots = {name: next(it) for name in ("first", "second", "attn")}
    send_sem, recv_sem, local_sem = (next(it) for _ in range(3))
    net = Net(shape, send_sem, recv_sem, local_sem)
    net.barrier()
    sums = {n: Sum(net, grads[n], sides[n], sends[n], recvs[n], loads[n]) for n in names}

    def run(name, final):
        for k in range(net.outer):
            sums[name].step(final)

    def keep(name):
        def final(i, rows):
            totals[name][i] = rows.astype(LOW)

        return final

    def place(ref):
        def final(i, rows):
            ref[...] = rows

        return final

    swaps = {}
    run("down", place(o_down))
    for name in ("first", "second", "attn"):
        run(name, keep(name))
        swaps[name] = swap(net, totals[name], gots[name])
    run("out", place(o_out))
    for name, ref in (("first", o_first), ("second", o_second)):
        arrive(swaps[name])
        n = gots[name].shape[2]
        for i in range(net.seq):
            ref[:, i * n : (i + 1) * n] = gots[name][i].astype(WIDE)
    arrive(swaps["attn"])
    for i in range(net.seq):
        for h in range(heads):
            for m in range(4):
                at, to = (h * 4 + m) * hd, (i * heads + h) * hd
                o_attn[m][:, to : to + hd] = gots["attn"][i, :, at : at + hd].astype(WIDE)
    net.finish()


def scatter_all(shape, heads, hd, grads):
    seq, fsdp, inner = shape
    outer = fsdp // inner
    names = ("down", "first", "second", "attn", "out")
    lead = {"down": 1, "out": 1, "first": seq, "second": seq, "attn": seq}
    blocks = [
        g.reshape(lead[n], outer, inner, g.shape[0] // (lead[n] * fsdp), g.shape[1])
        for n, g in zip(names, grads)
    ]
    size = {n: (g.shape[0], g.shape[3], g.shape[4]) for n, g in zip(names, blocks)}
    row = lambda n: jax.ShapeDtypeStruct((size[n][1], size[n][2]), WIDE)
    wide = lambda n: jax.ShapeDtypeStruct((size[n][1], size[n][2] * seq), WIDE)
    attn = jax.ShapeDtypeStruct((size["attn"][1], seq * heads * hd), WIDE)
    outs = [row("down"), wide("first"), wide("second"), row("out")] + [attn] * 4
    side = [
        jax.ShapeDtypeStruct((inner - 1, size[n][0], outer) + size[n][1:], LOW) for n in names
    ]
    scratch = [pltpu.VMEM((outer - 1,) + size[n], LOW) for n in names] * 2
    scratch += [pltpu.VMEM((inner,) + size[n], LOW) for n in names]
    scratch += [pltpu.VMEM(size[n], LOW) for n in ("first", "second", "attn")] * 2
    copies = 5 * (outer * inner + outer) + 3 * seq
    scratch += [
        pltpu.SemaphoreType.DMA((copies,)),
        pltpu.SemaphoreType.DMA((copies,)),
        pltpu.SemaphoreType.DMA((5 * outer * inner + 8,)),
    ]
    got = pl.pallas_call(
        functools.partial(scatter_kernel, shape, heads, hd),
        in_specs=[HBM] * 5,
        out_specs=[pl.BlockSpec(memory_space=pltpu.VMEM)] * len(outs) + [HBM] * 5,
        out_shape=outs + side,
        scratch_shapes=scratch,
        compiler_params=pltpu.CompilerParams(
            collective_id=1, has_side_effects=True, vmem_limit_bytes=VMEM_BYTES
        ),
        name="scatter_all",
    )(*blocks)
    return got[:8]


class Moves:
    def __init__(self):
        self.seq = lax.axis_size("seq")
        self.fsdp = lax.axis_size("fsdp")
        self.inner = 2 if self.fsdp == 8 else 4
        self.outer = self.fsdp // self.inner
        self.chips = self.seq // 2
        s = lax.axis_index("seq")
        f = lax.axis_index("fsdp")
        self.s, self.f = s, f
        self.chip, self.core = s // 2, s % 2
        self.out_at, self.in_at = f // self.inner, f % self.inner
        chips, inner, outer = self.chips, self.inner, self.outer
        self.core_perm = [(i, i ^ 1) for i in range(self.seq)]
        self.chip_perm = [
            (x * 2 + c, (x + 1) % chips * 2 + c) for x in range(chips) for c in range(2)
        ]
        self.out_perm = [
            (o * inner + i, (o + 1) % outer * inner + i)
            for o in range(outer)
            for i in range(inner)
        ]
        self.in_perm = [
            (o * inner + i, o * inner + (i + 1) % inner)
            for o in range(outer)
            for i in range(inner)
        ]

    def to_core(self, v):
        return lax.ppermute(v, "seq", self.core_perm)

    def to_chip(self, v):
        return lax.ppermute(v, "seq", self.chip_perm)

    def to_out(self, v):
        return lax.ppermute(v, "fsdp", self.out_perm)

    def to_in(self, v):
        return lax.ppermute(v, "fsdp", self.in_perm)

    def gather_seq(self, v):
        whole = empty((self.seq * v.shape[0],) + v.shape[1:], v.dtype)
        t = v.shape[0]
        now = v
        for k in range(self.chips):
            later = self.to_chip(now) if k < self.chips - 1 else None
            other = self.to_core(now)
            chip = (self.chip - k) % self.chips
            place = lambda whole, part, i: lax.dynamic_update_slice_in_dim(whole, part, i * t, 0)
            whole = place(whole, now, chip * 2 + self.core)
            whole = place(whole, other, chip * 2 + 1 - self.core)
            now = later
        return whole

    def sum_axis(self, v, axis, size):
        step = 1
        while step < size:
            v = v + lax.ppermute(v, axis, [(i, i ^ step) for i in range(size)])
            step *= 2
        return v

    def sum_seq(self, v):
        return self.sum_axis(v, "seq", self.seq)

    def sum_all(self, v):
        return self.sum_axis(self.sum_seq(v), "fsdp", self.fsdp)


class ScatterSeq:
    def __init__(self, move, part, kind=LOW):
        self.move, self.part, self.kind = move, part, kind
        self.held = None
        self.term = None
        for k in range(move.chips - 1):
            total = self.own(k)
            self.held = move.to_chip(total.astype(kind))

    def own(self, k, *tokens):
        move = self.move
        self.term = self.part((move.chip - 1 - k) % move.chips, *tokens)
        term = self.term.reshape((2, -1) + self.term.shape[1:])
        give = lax.dynamic_index_in_dim(term, 1 - move.core, 0, False)
        keep = lax.dynamic_index_in_dim(term, move.core, 0, False)
        total = keep.astype(WIDE) + move.to_core(give).astype(WIDE)
        if self.held is not None:
            total = total + self.held.astype(WIDE)
        return total

    def done(self, *tokens):
        return self.own(self.move.chips - 1, *tokens)


def after(v, *tokens):
    if not tokens:
        return v
    return lax.optimization_barrier((v,) + tokens)[0]


def on_device(
    inputs,
    teacher,
    segment_ids,
    valid,
    decay_rate,
    w_query,
    w_key,
    w_value,
    w_gate,
    w_out,
    w_first,
    w_second,
    w_down,
):
    move = Moves()
    seq = move.seq
    batch, block_len, width = inputs.shape
    assert batch == 1
    heads_all = decay_rate.shape[0]
    hd = width // heads_all
    heads = heads_all // seq
    own_rows = w_query.shape[0]
    ff = w_first.shape[1]
    ffs = ff // seq
    cols = heads * 4 * hd

    shape = net_shape(seq, move.fsdp)
    keep = valid.astype(WIDE).reshape(block_len, 1)
    count_own = jnp.sum(keep).reshape(1, 1)

    attn_own, first_own, second_own = pack_columns(
        (w_query, w_key, w_value, w_gate), (w_first, w_second), seq, heads, hd
    )
    x32 = inputs.reshape(block_len, width).astype(WIDE)
    r1 = lax.rsqrt(jnp.mean(x32 * x32, axis=-1, keepdims=True) + 1e-6)
    n1 = x32 * r1
    full_attn, full_first, full_second, full_out, full_down, n1_all, seg = gather_all(
        shape,
        attn_own,
        first_own,
        second_own,
        w_out[None],
        w_down[None],
        n1.astype(LOW),
        segment_ids.reshape(1, block_len),
    )
    seg = seg.reshape(seq * block_len)
    length = seg.shape[0]
    count = move.sum_all(after(count_own, n1_all))

    bounds = jnp.concatenate([jnp.full((1,), -1, jnp.int32), seg[CHUNK - 1 :: CHUNK]])
    rates = lax.dynamic_slice_in_dim(decay_rate, move.s * heads, heads, 0)

    z = dot(n1_all, full_attn)
    au, a, ss, states = attend(z, seg, bounds, rates, heads, hd)
    ss_all = move.sum_seq(ss.reshape(length))

    def rows_of(v, chip):
        return lax.dynamic_slice_in_dim(v, chip * 2 * block_len, 2 * block_len, 0)

    def product_scatter(pairs):
        def part(chip, *tokens):
            left = [rows_of(after(v, *tokens), chip) for v, _, _ in pairs]
            return sum(dot(l, w, 1, d) for l, (_, w, d) in zip(left, pairs)).astype(LOW)

        return ScatterSeq(move, part)

    out_sum = product_scatter([(au, full_out, 0)])
    ra_all = lax.rsqrt(ss_all / width + 1e-6).reshape(length, 1)
    ra = lax.dynamic_slice_in_dim(ra_all, move.s * block_len, block_len, 0)
    mixed_out = out_sum.done() * ra
    hsum = x32 + mixed_out
    r2 = lax.rsqrt(jnp.mean(hsum * hsum, axis=-1, keepdims=True) + 1e-6)
    m2 = hsum * r2
    m2_low = m2.astype(LOW)
    n2_all = move.gather_seq(m2_low)

    g1 = dot(n2_all, full_first)
    g2 = dot(n2_all, full_second)
    p = (g1 * g2).astype(LOW)
    g1 = g1.astype(LOW)
    g2 = g2.astype(LOW)
    y_sum = product_scatter([(p, full_down, 0)])
    y = hsum + y_sum.done()
    layer_out = y.astype(LOW).reshape(1, block_len, width)

    error = y - teacher.reshape(block_len, width).astype(WIDE)
    tokens = block_len * seq * move.fsdp
    dy = tokens / count * keep * error
    dyb = dy.astype(LOW)
    dy_all = move.gather_seq(dyb)

    dp = dot(dy_all, full_down, 1, 1)
    dg1 = (dp * g2.astype(WIDE)).astype(LOW)
    dg2 = (dp * g1.astype(WIDE)).astype(LOW)
    dn2_sum = product_scatter([(dg1, full_first, 1), (dg2, full_second, 1)])
    grad_down = dot(after(p, dn2_sum.term), dy_all, 0, 0).astype(LOW)
    dn2 = dn2_sum.done(grad_down)
    dh = dy + r2 * (dn2 - m2 * jnp.mean(dn2 * m2, axis=-1, keepdims=True))
    dhb = dh.astype(LOW)
    mean_own = jnp.mean(after(dhb, dn2_sum.term).astype(WIDE) * mixed_out, axis=-1)
    dh_all = move.gather_seq(dhb)
    mean_all = move.gather_seq(mean_own).reshape(length, 1)
    grad_first = dot(after(n2_all, mean_own), dg1, 0, 0).astype(LOW)
    grad_second = dot(after(n2_all, grad_first), dg2, 0, 0).astype(LOW)

    dj = dot(dh_all, after(full_out, grad_second), 1, 1)
    dz, o = attend_back(z, a, dj, ra_all, mean_all, states, seg, bounds, rates, heads, hd)
    dn1_sum = product_scatter([(dz, full_attn, 1)])
    grad_attn = dot(after(n1_all, dn1_sum.term), dz, 0, 0).astype(LOW)
    grad_out = dot(after(o, grad_attn), dh_all, 0, 0).astype(LOW)
    dn1 = dn1_sum.done(grad_out)
    input_grad = dh + r1 * (dn1 - n1 * jnp.mean(dn1 * n1, axis=-1, keepdims=True))
    loss_own = after(jnp.sum(keep * error * error).reshape(1, 1), dhb)
    loss = move.sum_all(loss_own) / (width * count)

    share_down, share_first, share_second, share_out, *share_attn = scatter_all(
        shape, heads, hd, (grad_down, grad_first, grad_second, grad_attn, grad_out)
    )

    return (
        layer_out,
        loss.reshape(()),
        input_grad.reshape(1, block_len, width),
        share_attn[0],
        share_attn[1],
        share_attn[2],
        share_attn[3],
        share_out,
        share_first,
        share_second,
        share_down,
    )


def solution(mesh):
    rows = P(("seq", "fsdp"), None)
    tokens = P("fsdp", "seq", None)
    return jax.shard_map(
        on_device,
        mesh=mesh,
        in_specs=(tokens, tokens, P("fsdp", "seq"), P("fsdp", "seq"), P()) + (rows,) * 8,
        out_specs=(tokens, P(), tokens) + (rows,) * 8,
        check_vma=False,
    )
```

```python
import functools

import jax
import jax.numpy as jnp
from jax import lax
from jax.experimental import pallas as pl
from jax.experimental.pallas import tpu as pltpu
from jax.sharding import PartitionSpec as P

CHUNK = 256
WIDE = jnp.float32
LOW = jnp.bfloat16
VMEM_BYTES = 60 * 1024 * 1024


def dot(left, right, left_dim=1, right_dim=0):
    return lax.dot_general(
        left, right, (((left_dim,), (right_dim,)), ((), ())), preferred_element_type=WIDE
    )


def decays(rate, place_col, place_row, chunk):
    rows = jnp.exp(-rate * place_col)
    cols = jnp.exp(rate * place_row)
    entry = jnp.exp(-rate * (place_col + 1.0))
    tail = jnp.exp(-rate * (chunk - 1.0 - place_col))
    return rows, cols, entry, tail


def masks(bounds_ref, seg_col, seg_row, n, chunk):
    before = bounds_ref[n]
    last = bounds_ref[n + 1]
    row = lax.broadcasted_iota(jnp.int32, (chunk, chunk), 0)
    col = lax.broadcasted_iota(jnp.int32, (chunk, chunk), 1)
    inner = (seg_col == seg_row) & (row >= col)
    return inner, seg_col == before, seg_col == last, jnp.where(before == last, 1.0, 0.0)


def places(chunk):
    place_col = lax.broadcasted_iota(jnp.int32, (chunk, 1), 0).astype(WIDE)
    place_row = lax.broadcasted_iota(jnp.int32, (1, chunk), 1).astype(WIDE)
    return place_col, place_row


def attend_kernel(
    heads, hd, rate_ref, bounds_ref, segc_ref, segr_ref, z_ref, au_ref, a_ref, ss_ref, st_ref, state
):
    n = pl.program_id(0)
    chunk = z_ref.shape[0]

    @pl.when(n == 0)
    def _():
        state[...] = jnp.zeros_like(state)

    inner, entry_on, tail_on, carry = masks(bounds_ref, segc_ref[...], segr_ref[...], n, chunk)
    place_col, place_row = places(chunk)
    total = jnp.zeros((chunk, 1), WIDE)
    for h in range(heads):
        rate = rate_ref[h]
        base = h * 4 * hd
        zq, zk, zv, zu = (z_ref[:, base + i * hd : base + (i + 1) * hd] for i in range(4))
        q = (zq * jax.nn.sigmoid(zq)).astype(LOW)
        k = (zk * jax.nn.sigmoid(zk)).astype(LOW)
        v = (zv * jax.nn.sigmoid(zv)).astype(LOW)
        u = zu * jax.nn.sigmoid(zu)
        rows, cols, entry, tail = decays(rate, place_col, place_row, chunk)
        scores = dot(q, k, 1, 1)
        weighted = jnp.where(inner, scores * rows * cols, 0.0).astype(LOW)
        held = state[h]
        st_ref[0, h] = held.astype(LOW)
        a = dot(weighted, v) + jnp.where(entry_on, entry, 0.0) * dot(q, held.astype(LOW))
        kt = (k.astype(WIDE) * jnp.where(tail_on, tail, 0.0)).astype(LOW)
        state[h] = carry * jnp.exp(jnp.full((1, 1), -rate * chunk, WIDE)) * held + dot(kt, v, 0, 0)
        a_ref[:, h * hd : (h + 1) * hd] = a
        au_ref[:, h * hd : (h + 1) * hd] = (a * u).astype(LOW)
        total = total + jnp.sum(a * a, axis=1, keepdims=True)
    ss_ref[...] = total


def attend(z, seg, bounds, rates, heads, hd):
    length = z.shape[0]
    count = length // CHUNK
    block = lambda width: pl.BlockSpec((CHUNK, width), lambda n, *_: (n, 0))
    return pl.pallas_call(
        functools.partial(attend_kernel, heads, hd),
        grid_spec=pltpu.PrefetchScalarGridSpec(
            num_scalar_prefetch=2,
            grid=(count,),
            in_specs=[
                block(1),
                pl.BlockSpec((1, CHUNK), lambda n, *_: (0, n)),
                block(heads * 4 * hd),
            ],
            out_specs=[
                block(heads * hd),
                block(heads * hd),
                block(1),
                pl.BlockSpec((1, heads, hd, hd), lambda n, *_: (n, 0, 0, 0)),
            ],
            scratch_shapes=[pltpu.VMEM((heads, hd, hd), WIDE)],
        ),
        out_shape=[
            jax.ShapeDtypeStruct((length, heads * hd), LOW),
            jax.ShapeDtypeStruct((length, heads * hd), WIDE),
            jax.ShapeDtypeStruct((length, 1), WIDE),
            jax.ShapeDtypeStruct((count, heads, hd, hd), LOW),
        ],
        compiler_params=pltpu.CompilerParams(vmem_limit_bytes=VMEM_BYTES),
        cost_estimate=pl.CostEstimate(
            flops=length * heads * hd * CHUNK * 6,
            bytes_accessed=length * heads * hd * 22,
            transcendentals=length * heads * hd * 4,
        ),
        name="attend",
    )(rates, bounds, seg.reshape(length, 1), seg.reshape(1, length), z)


def slope(z):
    sg = jax.nn.sigmoid(z)
    return sg * (1.0 + z * (1.0 - sg))


def attend_back(
    heads, hd, n, rate_ref, bounds_ref, segc_ref, segr_ref, z_ref, a_ref, dj_ref, ra_ref, m_ref,
    st_ref, dz_ref, o_ref, later
):
    chunk = z_ref.shape[0]
    inner, entry_on, tail_on, carry = masks(bounds_ref, segc_ref[...], segr_ref[...], n, chunk)
    place_col, place_row = places(chunk)
    ra = ra_ref[...]
    m = m_ref[...]
    for h in range(heads):
        rate = rate_ref[h]
        base = h * 4 * hd
        span = slice(h * hd, (h + 1) * hd)
        zq, zk, zv, zu = (z_ref[:, base + i * hd : base + (i + 1) * hd] for i in range(4))
        q = (zq * jax.nn.sigmoid(zq)).astype(LOW)
        k = (zk * jax.nn.sigmoid(zk)).astype(LOW)
        v = (zv * jax.nn.sigmoid(zv)).astype(LOW)
        u = zu * jax.nn.sigmoid(zu)
        an = a_ref[:, span] * ra
        dj = dj_ref[:, span]
        o_ref[:, span] = (an * u).astype(LOW)
        da = (ra * (dj * u - an * m)).astype(LOW)
        rows, cols, entry, tail = decays(rate, place_col, place_row, chunk)
        entry = jnp.where(entry_on, entry, 0.0)
        tail = jnp.where(tail_on, tail, 0.0)
        decay = jnp.where(inner, rows * cols, 0.0)
        weighted = (dot(q, k, 1, 1) * decay).astype(LOW)
        grads = (dot(da, v, 1, 1) * decay).astype(LOW)
        held = st_ref[0, h]
        after = later[h]
        after_low = after.astype(LOW)
        dq = dot(grads, k) + entry * dot(da, held, 1, 1)
        dk = dot(grads, q, 0, 0) + tail * dot(v, after_low, 1, 1)
        dv = dot(weighted, da, 0, 0) + tail * dot(k, after_low)
        qe = (q.astype(WIDE) * entry).astype(LOW)
        later[h] = carry * jnp.exp(jnp.full((1, 1), -rate * chunk, WIDE)) * after + dot(qe, da, 0, 0)
        dz_ref[:, base : base + hd] = (dq * slope(zq)).astype(LOW)
        dz_ref[:, base + hd : base + 2 * hd] = (dk * slope(zk)).astype(LOW)
        dz_ref[:, base + 2 * hd : base + 3 * hd] = (dv * slope(zv)).astype(LOW)
        dz_ref[:, base + 3 * hd : base + 4 * hd] = (dj * an * slope(zu)).astype(LOW)


def empty(shape, kind):
    return pl.pallas_call(
        lambda out: None,
        out_shape=jax.ShapeDtypeStruct(shape, kind),
        out_specs=pl.BlockSpec(memory_space=pl.ANY),
        name="empty",
    )()


def pack_kernel(seq, heads, hd, *refs):
    weights, glu, attn_out, glu_outs = refs[:4], refs[4:6], refs[6], refs[7:]
    for i in range(seq):
        for h in range(heads):
            for m, w in enumerate(weights):
                to, at = (h * 4 + m) * hd, (i * heads + h) * hd
                attn_out[i, :, to : to + hd] = w[:, at : at + hd]
        for w, out in zip(glu, glu_outs):
            n = out.shape[2]
            out[i] = w[:, i * n : (i + 1) * n]


def pack_columns(weights, glu, seq, heads, hd):
    r, kind = weights[0].shape[0], weights[0].dtype
    n = glu[0].shape[1] // seq
    return pl.pallas_call(
        functools.partial(pack_kernel, seq, heads, hd),
        out_shape=[jax.ShapeDtypeStruct((seq, r, heads * 4 * hd), kind)]
        + [jax.ShapeDtypeStruct((seq, r, n), kind)] * 2,
        compiler_params=pltpu.CompilerParams(vmem_limit_bytes=VMEM_BYTES),
        name="pack_columns",
    )(*weights, *glu)


def unpack_kernel(seq, heads, hd, attn, first, second, o_first, o_second, *o_attn):
    for i in range(seq):
        for h in range(heads):
            for m in range(4):
                at, to = (h * 4 + m) * hd, (i * heads + h) * hd
                o_attn[m][:, to : to + hd] = attn[i, :, at : at + hd].astype(WIDE)
        for ref, out in ((first, o_first), (second, o_second)):
            n = ref.shape[2]
            out[:, i * n : (i + 1) * n] = ref[i].astype(WIDE)


def unpack_columns(attn, first, second, heads, hd):
    seq, r = attn.shape[:2]
    shape = lambda n: jax.ShapeDtypeStruct((r, seq * n), WIDE)
    return pl.pallas_call(
        functools.partial(unpack_kernel, seq, heads, hd),
        out_shape=[shape(first.shape[2]), shape(second.shape[2])] + [shape(heads * hd)] * 4,
        compiler_params=pltpu.CompilerParams(vmem_limit_bytes=VMEM_BYTES),
        name="unpack_columns",
    )(attn, first, second)


class Net:
    def __init__(self, shape, send_sem, recv_sem, local_sem):
        self.seq, self.fsdp, self.inner = shape
        self.outer = self.fsdp // self.inner
        self.chips = self.seq // 2
        self.send_sem, self.recv_sem, self.local_sem = send_sem, recv_sem, local_sem
        self.used = 0
        self.locals = 0
        self.s, self.f = lax.axis_index("seq"), lax.axis_index("fsdp")
        self.chip, self.core = self.s // 2, self.s % 2
        self.o, self.i = self.f // self.inner, self.f % self.inner
        self.sent = []

    def seq_peers(self):
        for dx in range(self.chips):
            for dc in range(2):
                if dx or dc:
                    yield dx, dc, lax.rem(self.chip + dx, self.chips) * 2 + lax.rem(self.core + dc, 2)

    def at_seq(self, s):
        return (s, self.f)

    def at_inner(self, j):
        return (self.s, self.o * self.inner + lax.rem(self.i + j, self.inner))

    def at_outer(self, k):
        return (self.s, lax.rem(self.o + k, self.outer) * self.inner + self.i)

    def barrier(self):
        peers = [self.at_seq(s) for _, _, s in self.seq_peers()]
        peers += [self.at_inner(j) for j in range(1, self.inner)]
        peers += [self.at_outer(1), self.at_outer(self.outer - 1)]
        sem = pltpu.get_barrier_semaphore()
        for peer in peers:
            pl.semaphore_signal(sem, inc=1, device_id=peer, device_id_type=pl.DeviceIdType.MESH)
        pl.semaphore_wait(sem, len(peers))

    def send(self, src, dst, device):
        copy = pltpu.make_async_remote_copy(
            src_ref=src,
            dst_ref=dst,
            send_sem=self.send_sem.at[self.used],
            recv_sem=self.recv_sem.at[self.used],
            device_id=device,
            device_id_type=pl.DeviceIdType.MESH,
        )
        self.used += 1
        copy.start()
        self.sent.append(copy)
        return copy

    def copy(self, src, dst):
        copy = pltpu.make_async_copy(src, dst, self.local_sem.at[self.locals])
        self.locals += 1
        copy.start()
        return copy

    def left(self, copy):
        copy.wait_send()
        self.sent = [other for other in self.sent if other is not copy]

    def finish(self):
        for copy in self.sent:
            copy.wait_send()
        self.sent = []


def net_shape(mesh_seq, mesh_fsdp):
    return mesh_seq, mesh_fsdp, 2 if mesh_fsdp == 8 else 4


class Ring:
    def __init__(self, net, piece, full):
        self.net, self.piece, self.full = net, piece, full
        self.copies = [net.copy(piece, full.at[:, net.o, net.i])]
        self.at = 0
        self.coming = None
        self.side = []

    def step(self):
        net, full = self.net, self.full
        if self.at >= net.outer:
            return
        if self.coming is not None:
            self.coming.wait_recv()
        spot = full.at[:, lax.rem(net.o + net.outer - self.at, net.outer), net.i]
        src = self.piece if self.at == 0 else spot
        self.coming = None
        if self.at < net.outer - 1:
            self.coming = net.send(src, spot, net.at_outer(1))
        for j in range(1, net.inner):
            self.side.append(net.send(src, spot, net.at_inner(j)))
        self.at += 1

    def done(self):
        while self.at < self.net.outer:
            self.step()
        for copy in self.side:
            copy.wait_recv()
        for copy in self.copies:
            copy.wait()


def swap(net, blocks, got):
    own = net.copy(blocks.at[net.s], got.at[net.s])
    coming = [
        net.send(blocks.at[s], got.at[net.s], net.at_seq(s)) for _, _, s in net.seq_peers()
    ]
    return own, coming


def arrive(pair):
    own, coming = pair
    own.wait()
    for copy in coming:
        copy.wait_recv()


class Rows:
    def __init__(self, net, own, whole):
        t = own.shape[0]
        self.net, self.whole = net, whole
        spot = lambda s: whole.at[pl.ds(pl.multiple_of(s * t, t), t)]
        self.spot = spot
        self.far = [
            net.send(own, spot(net.s), net.at_seq(lax.rem(net.chip + dx, net.chips) * 2 + net.core))
            for dx in range(1, net.chips)
        ]
        self.near = [net.send(own, spot(net.s), net.at_seq(net.chip * 2 + 1 - net.core))]
        self.own = net.copy(own, spot(net.s))

    def turn(self):
        net = self.net
        for dx, copy in zip(range(1, net.chips), self.far):
            copy.wait_recv()
            spot = self.spot(lax.rem(net.chip + net.chips - dx, net.chips) * 2 + net.core)
            self.near.append(net.send(spot, spot, net.at_seq(net.chip * 2 + 1 - net.core)))

    def done(self):
        for copy in self.near:
            copy.wait_recv()
        self.own.wait()


def gather_kernel(
    shape,
    attn_ref,
    first_ref,
    second_ref,
    out_ref,
    down_ref,
    n1_ref,
    seg_ref,
    count_ref,
    attn_mid,
    first_mid,
    second_mid,
    full_attn,
    full_first,
    full_second,
    full_out,
    full_down,
    n1_all,
    seg_all,
    count_all,
    seq_buf,
    in_buf,
    out_buf,
    send_sem,
    recv_sem,
    local_sem,
):
    net = Net(shape, send_sem, recv_sem, local_sem)
    net.barrier()
    count = Total(net, count_ref, seq_buf, in_buf, out_buf)
    attn_swap = swap(net, attn_ref, attn_mid)
    seg_own = net.copy(seg_ref, seg_all.at[net.s])
    segs = [net.send(seg_ref, seg_all.at[net.s], net.at_seq(s)) for _, _, s in net.seq_peers()]
    first_swap = swap(net, first_ref, first_mid)
    second_swap = swap(net, second_ref, second_mid)
    rows = Rows(net, n1_ref, n1_all)
    arrive(attn_swap)
    count.step()
    rings = [Ring(net, attn_mid, full_attn)]
    rings.append(Ring(net, out_ref, full_out))
    for _ in range(net.outer):
        rings[0].step()
        count.step()
    arrive(first_swap)
    arrive(second_swap)
    rows.turn()
    rings.append(Ring(net, first_mid, full_first))
    rings.append(Ring(net, second_mid, full_second))
    rings.append(Ring(net, down_ref, full_down))
    for ring in rings[1:]:
        for _ in range(net.outer):
            ring.step()
    count_all[...] = count.done()
    for ring in rings:
        ring.done()
    rows.done()
    seg_own.wait()
    for copy in segs:
        copy.wait_recv()
    net.finish()


HBM = pl.BlockSpec(memory_space=pl.ANY)


def gather_all(shape, attn, first, second, w_out, w_down, n1, seg, count):
    seq, fsdp, inner = shape
    outer = fsdp // inner
    like = lambda v, lead: jax.ShapeDtypeStruct(lead + v.shape[-2:], v.dtype)
    ring = lambda v: like(v, (v.shape[0], outer, inner))
    outs = [like(v, (seq,)) for v in (attn, first, second)]
    outs += [ring(v) for v in (attn, first, second, w_out, w_down)]
    outs.append(jax.ShapeDtypeStruct((seq * n1.shape[0], n1.shape[1]), n1.dtype))
    outs.append(jax.ShapeDtypeStruct((seq,) + seg.shape, seg.dtype))
    outs.append(jax.ShapeDtypeStruct(count.shape, count.dtype))
    copies = 4 * (seq - 1) + 2 * seq + 5 * (outer * inner + outer) + total_copies(shape)
    in_vmem = pl.BlockSpec(memory_space=pltpu.VMEM)
    got = pl.pallas_call(
        functools.partial(gather_kernel, shape),
        in_specs=[HBM] * 7 + [in_vmem],
        out_specs=[HBM] * (len(outs) - 1) + [in_vmem],
        out_shape=outs,
        scratch_shapes=total_scratch(shape)
        + [
            pltpu.SemaphoreType.DMA((copies,)),
            pltpu.SemaphoreType.DMA((copies,)),
            pltpu.SemaphoreType.DMA((16,)),
        ],
        compiler_params=pltpu.CompilerParams(
            collective_id=0, has_side_effects=True, vmem_limit_bytes=VMEM_BYTES
        ),
        name="gather_all",
    )(attn, first, second, w_out, w_down, n1, seg, count)
    flat = lambda v: v.reshape(-1, v.shape[-1])
    return [flat(v) for v in got[3:8]] + list(got[8:])


class Total:
    def __init__(self, net, own, seq_buf, in_buf, out_buf):
        self.net, self.bufs, self.stage = net, (seq_buf, in_buf, out_buf), 0
        self.coming = self.share(seq_buf, net.s, own[...], [net.at_seq(s) for _, _, s in net.seq_peers()])

    def share(self, buf, at, value, devices):
        buf[at] = value
        return [self.net.send(buf.at[at], buf.at[at], device) for device in devices]

    def gathered(self, buf):
        for copy in self.coming:
            copy.wait_recv()
        total = buf[0]
        for j in range(1, buf.shape[0]):
            total = total + buf[j]
        return total

    def step(self):
        net, (seq_buf, in_buf, out_buf) = self.net, self.bufs
        if self.stage == 0:
            peers = [net.at_inner(j) for j in range(1, net.inner)]
            self.coming = self.share(in_buf, net.i, self.gathered(seq_buf), peers)
        elif self.stage == 1:
            self.coming = self.share(out_buf, net.o, self.gathered(in_buf), [net.at_outer(1)])
        elif self.stage < net.outer:
            self.coming[-1].wait_recv()
            at = lax.rem(net.o + net.outer - self.stage + 1, net.outer)
            self.coming = [net.send(out_buf.at[at], out_buf.at[at], net.at_outer(1))]
        self.stage += 1

    def done(self):
        while self.stage < self.net.outer:
            self.step()
        return self.gathered(self.bufs[2])


def total_scratch(shape):
    seq, fsdp, inner = shape
    return [pltpu.VMEM((n, 8, 128), WIDE) for n in (seq, inner, fsdp // inner)]


def total_copies(shape):
    seq, fsdp, inner = shape
    return seq + inner + fsdp // inner


class Sum:
    def __init__(self, net, g, side, ring, send, load):
        self.net, self.g, self.side_ref, self.ring_ref = net, g, side, ring
        self.send_buf, self.load = send, load
        self.side = []
        self.ring = []
        for k in range(net.outer):
            o = self.spot(k)
            now = []
            for j in range(1, net.inner):
                to = lax.rem(net.i + j, net.inner)
                now.append(net.send(g.at[:, o, to], side.at[j - 1, :, o], net.at_inner(j)))
            self.side.append(now)
        self.at = 0

    def spot(self, k):
        return lax.rem(self.net.o + 2 * self.net.outer - 1 - k, self.net.outer)

    def step(self, final):
        net, k = self.net, self.at
        self.at += 1
        o = self.spot(k)
        terms = self.load
        loads = [net.copy(self.g.at[:, o, net.i], terms.at[0])]
        for j, copy in enumerate(self.side[k]):
            copy.wait_recv()
            loads.append(net.copy(self.side_ref.at[j, :, o], terms.at[j + 1]))
        count = net.inner
        if k > 0:
            self.ring[k - 1].wait_recv()
            loads.append(net.copy(self.ring_ref.at[k - 1], terms.at[count]))
            count += 1
        if k >= 2:
            net.left(self.ring[k - 2])
        for load in loads:
            load.wait()

        def one(i, _):
            total = terms[0, i].astype(WIDE)
            for j in range(1, count):
                total = total + terms[j, i].astype(WIDE)
            if k < net.outer - 1:
                self.send_buf[k % 2, i] = total.astype(LOW)
            else:
                final(i, total)
            return 0

        lax.fori_loop(0, terms.shape[1], one, 0)
        if k < net.outer - 1:
            self.ring.append(net.send(self.send_buf.at[k % 2], self.ring_ref.at[k], net.at_outer(1)))


GRADS = ("down", "first", "second", "attn", "out")
SPLIT = ("first", "second", "attn")
LOADS = ("down", "first", "attn", "out")


def back_kernel(
    shape, heads, hd,
    rate_ref, bounds_ref, segc, segr, z, a, dh, ra, mean, states, w_out, w_attn, n1, loss_ref,
    g_down, g_first, g_second,
    dn1_ref, o_down, o_out, o_loss, got_first, got_second, got_attn, g_attn,
    side_down, side_first, side_second, side_attn, side_out,
    ring_down, ring_first, ring_second, ring_attn, ring_out,
    core_in, chip_in,
    dz_all, later, dj, o_chunk, out_acc, g_out, stage, term, wide_tile,
    *rest
):
    it = iter(rest)
    take = lambda names: {name: next(it) for name in names}
    sends, loads = take(GRADS), take(LOADS)
    loads["second"] = loads["first"]
    total_bufs = [next(it) for _ in range(3)]
    send_sem, recv_sem, local_sem = (next(it) for _ in range(3))
    net = Net(shape, send_sem, recv_sem, local_sem)
    grads = dict(down=g_down, first=g_first, second=g_second, attn=g_attn, out=g_out)
    sides = dict(down=side_down, first=side_first, second=side_second, attn=side_attn, out=side_out)
    rings = dict(down=ring_down, first=ring_first, second=ring_second, attn=ring_attn, out=ring_out)
    gots = dict(first=got_first, second=got_second, attn=got_attn)
    owned = dict(down=o_down, out=o_out)
    length, cols = dz_all.shape
    width = dh.shape[1]
    count = length // CHUNK
    wide = min(512, width)

    net.barrier()
    sums, swaps, queue = {}, {}, []
    loss = Total(net, loss_ref, *total_bufs)

    def begin(name):
        sums[name] = Sum(net, grads[name], sides[name], rings[name], sends[name], loads[name])
        queue.extend([name] * net.outer)

    def pump(times=1):
        for _ in range(min(times, len(queue))):
            name = queue.pop(0)

            def final(i, rows):
                if name in owned:
                    owned[name][...] = rows
                else:
                    totals[i] = rows.astype(LOW)

            totals = sends[name].at[(net.outer - 1) % 2]
            sums[name].step(final)
            if name in SPLIT and sums[name].at == net.outer:
                swaps[name] = swap(net, totals, gots[name])

    loss.step()
    for name in ("down", "first", "second"):
        begin(name)

    later[...] = jnp.zeros_like(later)
    out_acc[...] = jnp.zeros_like(out_acc)

    def chunks(top, steps):
        def body(segc_ref, segr_ref, z_ref, a_ref, dh_ref, ra_ref, m_ref, st_ref):
            n = top - pl.program_id(0)
            dj[...] = dot(dh_ref[...], w_out[...], 1, 1)
            rows = pl.ds(pl.multiple_of(n * CHUNK, CHUNK), CHUNK)
            attend_back(
                heads, hd, n, rate_ref, bounds_ref, segc_ref, segr_ref, z_ref, a_ref, dj, ra_ref,
                m_ref, st_ref, dz_all.at[rows], o_chunk, later,
            )

            def add(j, _):
                at = pl.ds(pl.multiple_of(j * wide, wide), wide)
                out_acc[:, at] += dot(o_chunk[...], dh_ref[:, at], 0, 0)
                return 0

            lax.fori_loop(0, width // wide, add, 0)

        block = lambda n: pl.BlockSpec((CHUNK, n), lambda i: (top - i, 0))
        pltpu.emit_pipeline(
            body,
            grid=(steps,),
            in_specs=[
                block(1),
                pl.BlockSpec((1, CHUNK), lambda i: (0, top - i)),
                block(cols),
                block(heads * hd),
                block(width),
                block(1),
                block(1),
                pl.BlockSpec((1, heads, hd, hd), lambda i: (top - i, 0, 0, 0)),
            ],
        )(segc, segr, z, a, dh, ra, mean, states)

    half = count // 2
    chunks(count - 1, half)
    loss.step()
    pump()
    chunks(count - 1 - half, count - half)
    loss.step()
    pump()

    own_rows = dn1_ref.shape[0]
    tile = min(256, own_rows)
    used = [None, None]
    turns = [0]

    def product(row, each):
        x = dz_all[pl.ds(pl.multiple_of(row, tile), tile)]

        def one(j, _):
            at = pl.ds(pl.multiple_of(j * wide, wide), wide)
            each(at, dot(x, w_attn[at, :], 1, 1))
            return 0

        lax.fori_loop(0, width // wide, one, 0)

    def slot():
        i = turns[0] % 2
        turns[0] += 1
        if used[i] is not None:
            net.left(used[i])
        return i

    def row_of(chip, core, t):
        return (chip * 2 + core) * own_rows + t * tile

    near = {}
    far = []

    def give(dx):
        chip = lax.rem(net.chip + dx, net.chips)
        for t in range(own_rows // tile):
            i = slot()

            def store(at, part, i=i):
                stage[i, :, at] = part.astype(LOW)

            product(row_of(chip, 1 - net.core, t), store)
            spot = core_in.at[dx, pl.ds(t * tile, tile)]
            used[i] = near[dx, t] = net.send(
                stage.at[i], spot, net.at_seq(net.chip * 2 + 1 - net.core)
            )

    def keep(dx):
        chip = lax.rem(net.chip + dx, net.chips)
        for t in range(own_rows // tile):
            span = pl.ds(t * tile, tile)
            near[dx, t].wait_recv()
            loads = [net.copy(core_in.at[dx, span], term.at[0])]
            if dx == 0:
                for j, copies in enumerate(far):
                    copies[t].wait_recv()
                    loads.append(net.copy(chip_in.at[j, span], term.at[j + 1]))
            else:
                i = slot()
            for load in loads:
                load.wait()

            def store(at, part):
                total = part
                for j in range(len(loads)):
                    total = total + term[j, :, at].astype(WIDE)
                if dx == 0:
                    wide_tile[:, at] = total
                else:
                    stage[i, :, at] = total.astype(LOW)

            product(row_of(chip, net.core, t), store)
            if dx == 0:
                net.copy(wide_tile, dn1_ref.at[span]).wait()
            else:
                used[i] = net.send(
                    stage.at[i], chip_in.at[dx - 1, span], net.at_seq(chip * 2 + net.core)
                )
                far[dx - 1].append(used[i])

    for dx in range(1, net.chips):
        far.append([])
        give(dx)
        keep(dx)
    pump()

    parts = 2
    spread = net.outer // parts
    features = width // net.seq // parts

    def grad_body(n1_ref, g_ref):
        for j in range(cols // wide):
            at = slice(j * wide, (j + 1) * wide)
            got = dot(n1_ref[...], dz_all[:, at], 0, 0).astype(LOW)
            g_ref[:, :, :, :, at] = got.reshape(g_ref.shape[:-1] + (wide,))

    pltpu.emit_pipeline(
        grad_body,
        grid=(net.seq, parts),
        in_specs=[pl.BlockSpec((length, features), lambda i, j: (0, i * parts + j))],
        out_specs=[
            pl.BlockSpec((1, spread) + g_attn.shape[2:], lambda i, j: (i, j, 0, 0, 0)),
        ],
    )(n1, g_attn)
    begin("attn")
    for j in range(width // wide):
        at = slice(j * wide, (j + 1) * wide)
        g_out[:, :, :, :, at] = out_acc[:, at].astype(LOW).reshape(g_out.shape[:-1] + (wide,))
    begin("out")
    pump(2)
    give(0)
    pump()
    keep(0)
    o_loss[...] = loss.done()
    pump(len(queue))
    for name in SPLIT:
        arrive(swaps[name])
    net.finish()


def back_all(shape, heads, hd, rates, bounds, seg, z, a, dh, ra, mean, states, w_out, w_attn, n1, loss, grads):
    seq, fsdp, inner = shape
    outer = fsdp // inner
    length, width = dh.shape
    cols = z.shape[1]
    own_rows = length // seq
    chips = seq // 2
    tile = min(256, own_rows)
    lead = {"down": 1, "out": 1, "first": seq, "second": seq, "attn": seq}
    blocks = [
        g.reshape(lead[n], outer, inner, g.shape[0] // (lead[n] * fsdp), g.shape[1])
        for n, g in zip(GRADS, grads)
    ]
    size = {n: (g.shape[0], g.shape[3], g.shape[4]) for n, g in zip(GRADS, blocks)}
    size["attn"] = (seq, width // (seq * fsdp), cols)
    size["out"] = (1, width // (seq * fsdp), width)
    whole = lambda n: (size[n][0], outer, inner) + size[n][1:]
    low = lambda dims: jax.ShapeDtypeStruct(dims, LOW)
    row = lambda n: jax.ShapeDtypeStruct(size[n][1:], WIDE)
    outs = [jax.ShapeDtypeStruct((own_rows, width), WIDE), row("down"), row("out")]
    outs += [jax.ShapeDtypeStruct((8, 128), WIDE)]
    outs += [low(size[n]) for n in SPLIT] + [low(whole("attn"))]
    outs += [low((inner - 1, size[n][0], outer) + size[n][1:]) for n in GRADS]
    outs += [low((outer - 1,) + size[n]) for n in GRADS]
    outs += [low((chips, own_rows, width)), low((max(chips - 1, 1), own_rows, width))]
    in_vmem = pl.BlockSpec(memory_space=pltpu.VMEM)
    smem = pl.BlockSpec(memory_space=pltpu.SMEM)
    scratch = [
        pltpu.VMEM((length, cols), LOW),
        pltpu.VMEM((heads, hd, hd), WIDE),
        pltpu.VMEM((CHUNK, heads * hd), WIDE),
        pltpu.VMEM((CHUNK, heads * hd), LOW),
        pltpu.VMEM((heads * hd, width), WIDE),
        pltpu.VMEM(whole("out"), LOW),
        pltpu.VMEM((2, tile, width), LOW),
        pltpu.VMEM((chips, tile, width), LOW),
        pltpu.VMEM((tile, width), WIDE),
    ]
    scratch += [pltpu.VMEM((2,) + size[n], LOW) for n in GRADS]
    scratch += [pltpu.VMEM((inner + 1,) + size[n], LOW) for n in LOADS]
    scratch += total_scratch(shape)
    copies = 5 * (outer * inner + outer) + 3 * seq + total_copies(shape) + 2 * length // tile
    scratch += [
        pltpu.SemaphoreType.DMA((copies,)),
        pltpu.SemaphoreType.DMA((copies,)),
        pltpu.SemaphoreType.DMA((5 * outer * (inner + 1) + 3 + 4 * length // tile,)),
    ]
    return pl.pallas_call(
        functools.partial(back_kernel, shape, heads, hd),
        in_specs=[smem, smem] + [HBM] * 8 + [in_vmem] * 2 + [HBM, in_vmem] + [HBM] * 3,
        out_specs=[HBM] + [in_vmem] * 3 + [HBM] * (len(outs) - 4),
        out_shape=outs,
        scratch_shapes=scratch,
        compiler_params=pltpu.CompilerParams(
            collective_id=1, has_side_effects=True, vmem_limit_bytes=VMEM_BYTES
        ),
        name="back_all",
    )(
        rates, bounds, seg.reshape(length, 1), seg.reshape(1, length), z, a, dh, ra, mean, states,
        w_out, w_attn, n1, loss, *blocks
    )[:7]


class Moves:
    def __init__(self):
        self.seq = lax.axis_size("seq")
        self.fsdp = lax.axis_size("fsdp")
        self.inner = 2 if self.fsdp == 8 else 4
        self.outer = self.fsdp // self.inner
        self.chips = self.seq // 2
        s = lax.axis_index("seq")
        f = lax.axis_index("fsdp")
        self.s, self.f = s, f
        self.chip, self.core = s // 2, s % 2
        self.out_at, self.in_at = f // self.inner, f % self.inner
        chips, inner, outer = self.chips, self.inner, self.outer
        self.core_perm = [(i, i ^ 1) for i in range(self.seq)]
        self.chip_perm = [
            (x * 2 + c, (x + 1) % chips * 2 + c) for x in range(chips) for c in range(2)
        ]
        self.out_perm = [
            (o * inner + i, (o + 1) % outer * inner + i)
            for o in range(outer)
            for i in range(inner)
        ]
        self.in_perm = [
            (o * inner + i, o * inner + (i + 1) % inner)
            for o in range(outer)
            for i in range(inner)
        ]

    def to_core(self, v):
        return lax.ppermute(v, "seq", self.core_perm)

    def to_chip(self, v):
        return lax.ppermute(v, "seq", self.chip_perm)

    def to_out(self, v):
        return lax.ppermute(v, "fsdp", self.out_perm)

    def to_in(self, v):
        return lax.ppermute(v, "fsdp", self.in_perm)

    def gather_seq(self, v):
        whole = empty((self.seq * v.shape[0],) + v.shape[1:], v.dtype)
        t = v.shape[0]
        now = v
        for k in range(self.chips):
            later = self.to_chip(now) if k < self.chips - 1 else None
            other = self.to_core(now)
            chip = (self.chip - k) % self.chips
            place = lambda whole, part, i: lax.dynamic_update_slice_in_dim(whole, part, i * t, 0)
            whole = place(whole, now, chip * 2 + self.core)
            whole = place(whole, other, chip * 2 + 1 - self.core)
            now = later
        return whole

    def sum_axis(self, v, axis, size):
        step = 1
        while step < size:
            v = v + lax.ppermute(v, axis, [(i, i ^ step) for i in range(size)])
            step *= 2
        return v

    def sum_seq(self, v):
        return self.sum_axis(v, "seq", self.seq)

    def sum_all(self, v):
        return self.sum_axis(self.sum_seq(v), "fsdp", self.fsdp)


class ScatterSeq:
    def __init__(self, move, part, kind=LOW):
        self.move, self.part, self.kind = move, part, kind
        self.held = None
        self.term = None
        for k in range(move.chips - 1):
            total = self.own(k)
            self.held = move.to_chip(total.astype(kind))

    def own(self, k, *tokens):
        move = self.move
        self.term = self.part((move.chip - 1 - k) % move.chips, *tokens)
        term = self.term.reshape((2, -1) + self.term.shape[1:])
        give = lax.dynamic_index_in_dim(term, 1 - move.core, 0, False)
        keep = lax.dynamic_index_in_dim(term, move.core, 0, False)
        total = keep.astype(WIDE) + move.to_core(give).astype(WIDE)
        if self.held is not None:
            total = total + self.held.astype(WIDE)
        return total

    def done(self, *tokens):
        return self.own(self.move.chips - 1, *tokens)


def after(v, *tokens):
    if not tokens:
        return v
    return lax.optimization_barrier((v,) + tokens)[0]


def on_device(
    inputs,
    teacher,
    segment_ids,
    valid,
    decay_rate,
    w_query,
    w_key,
    w_value,
    w_gate,
    w_out,
    w_first,
    w_second,
    w_down,
):
    move = Moves()
    seq = move.seq
    batch, block_len, width = inputs.shape
    assert batch == 1
    heads_all = decay_rate.shape[0]
    hd = width // heads_all
    heads = heads_all // seq
    own_rows = w_query.shape[0]
    ff = w_first.shape[1]
    ffs = ff // seq
    cols = heads * 4 * hd

    shape = net_shape(seq, move.fsdp)
    keep = valid.astype(WIDE).reshape(block_len, 1)
    spread = lambda v: jnp.broadcast_to(v, (8, 128))

    attn_own, first_own, second_own = pack_columns(
        (w_query, w_key, w_value, w_gate), (w_first, w_second), seq, heads, hd
    )
    x32 = inputs.reshape(block_len, width).astype(WIDE)
    r1 = lax.rsqrt(jnp.mean(x32 * x32, axis=-1, keepdims=True) + 1e-6)
    n1 = x32 * r1
    full_attn, full_first, full_second, full_out, full_down, n1_all, seg, count = gather_all(
        shape,
        attn_own,
        first_own,
        second_own,
        w_out[None],
        w_down[None],
        n1.astype(LOW),
        segment_ids.reshape(1, block_len),
        spread(jnp.sum(keep)),
    )
    seg = seg.reshape(seq * block_len)
    length = seg.shape[0]
    count = count[:1, :1]

    bounds = jnp.concatenate([jnp.full((1,), -1, jnp.int32), seg[CHUNK - 1 :: CHUNK]])
    rates = lax.dynamic_slice_in_dim(decay_rate, move.s * heads, heads, 0)

    z = dot(n1_all, full_attn)
    au, a, ss, states = attend(z, seg, bounds, rates, heads, hd)
    ss_all = move.sum_seq(ss.reshape(length))

    def rows_of(v, chip):
        return lax.dynamic_slice_in_dim(v, chip * 2 * block_len, 2 * block_len, 0)

    def product_scatter(pairs):
        def part(chip, *tokens):
            left = [rows_of(after(v, *tokens), chip) for v, _, _ in pairs]
            return sum(dot(l, w, 1, d) for l, (_, w, d) in zip(left, pairs)).astype(LOW)

        return ScatterSeq(move, part)

    out_sum = product_scatter([(au, full_out, 0)])
    ra_all = lax.rsqrt(ss_all / width + 1e-6).reshape(length, 1)
    ra = lax.dynamic_slice_in_dim(ra_all, move.s * block_len, block_len, 0)
    mixed_out = out_sum.done() * ra
    hsum = x32 + mixed_out
    r2 = lax.rsqrt(jnp.mean(hsum * hsum, axis=-1, keepdims=True) + 1e-6)
    m2 = hsum * r2
    m2_low = m2.astype(LOW)
    n2_all = move.gather_seq(m2_low)

    g1 = dot(n2_all, full_first)
    g2 = dot(n2_all, full_second)
    p = (g1 * g2).astype(LOW)
    g1 = g1.astype(LOW)
    g2 = g2.astype(LOW)
    y_sum = product_scatter([(p, full_down, 0)])
    y = hsum + y_sum.done()
    layer_out = y.astype(LOW).reshape(1, block_len, width)

    error = y - teacher.reshape(block_len, width).astype(WIDE)
    tokens = block_len * seq * move.fsdp
    dy = tokens / count * keep * error
    dyb = dy.astype(LOW)
    dy_all = move.gather_seq(dyb)

    dp = dot(dy_all, full_down, 1, 1)
    dg1 = (dp * g2.astype(WIDE)).astype(LOW)
    dg2 = (dp * g1.astype(WIDE)).astype(LOW)
    dn2_sum = product_scatter([(dg1, full_first, 1), (dg2, full_second, 1)])
    grad_down = dot(after(p, dn2_sum.term), dy_all, 0, 0).astype(LOW)
    dn2 = dn2_sum.done(grad_down)
    dh = dy + r2 * (dn2 - m2 * jnp.mean(dn2 * m2, axis=-1, keepdims=True))
    dhb = dh.astype(LOW)
    mean_own = jnp.mean(after(dhb, dn2_sum.term).astype(WIDE) * mixed_out, axis=-1)
    dh_all = move.gather_seq(dhb)
    mean_all = move.gather_seq(mean_own).reshape(length, 1)
    grad_first = dot(after(n2_all, mean_own), dg1, 0, 0).astype(LOW)
    grad_second = dot(after(n2_all, grad_first), dg2, 0, 0).astype(LOW)

    dn1, share_down, share_out, loss, got_first, got_second, got_attn = back_all(
        shape, heads, hd, rates, bounds, seg, z, a, dh_all, ra_all, mean_all, states, full_out,
        full_attn, n1_all, spread(jnp.sum(keep * error * error)),
        (grad_down, grad_first, grad_second),
    )
    input_grad = dh + r1 * (dn1 - n1 * jnp.mean(dn1 * n1, axis=-1, keepdims=True))
    loss = loss[0, 0] / (width * count)
    share_first, share_second, *share_attn = unpack_columns(
        got_attn, got_first, got_second, heads, hd
    )

    return (
        layer_out,
        loss.reshape(()),
        input_grad.reshape(1, block_len, width),
        share_attn[0],
        share_attn[1],
        share_attn[2],
        share_attn[3],
        share_out,
        share_first,
        share_second,
        share_down,
    )


def solution(mesh):
    rows = P(("seq", "fsdp"), None)
    tokens = P("fsdp", "seq", None)
    return jax.shard_map(
        on_device,
        mesh=mesh,
        in_specs=(tokens, tokens, P("fsdp", "seq"), P("fsdp", "seq"), P()) + (rows,) * 8,
        out_specs=(tokens, P(), tokens) + (rows,) * 8,
        check_vma=False,
    )
```

```python
import functools

import jax
import jax.numpy as jnp
from jax import lax
from jax.experimental import pallas as pl
from jax.experimental.pallas import tpu as pltpu
from jax.sharding import PartitionSpec as P

CHUNK = 256
WIDE = jnp.float32
LOW = jnp.bfloat16
VMEM_BYTES = 60 * 1024 * 1024


def dot(left, right, left_dim=1, right_dim=0):
    return lax.dot_general(
        left, right, (((left_dim,), (right_dim,)), ((), ())), preferred_element_type=WIDE
    )


def decays(rate, place_col, place_row, chunk):
    rows = jnp.exp(-rate * place_col)
    cols = jnp.exp(rate * place_row)
    entry = jnp.exp(-rate * (place_col + 1.0))
    tail = jnp.exp(-rate * (chunk - 1.0 - place_col))
    return rows, cols, entry, tail


def masks(bounds_ref, seg_col, seg_row, n, chunk):
    before = bounds_ref[n]
    last = bounds_ref[n + 1]
    row = lax.broadcasted_iota(jnp.int32, (chunk, chunk), 0)
    col = lax.broadcasted_iota(jnp.int32, (chunk, chunk), 1)
    inner = (seg_col == seg_row) & (row >= col)
    return inner, seg_col == before, seg_col == last, jnp.where(before == last, 1.0, 0.0)


def places(chunk):
    place_col = lax.broadcasted_iota(jnp.int32, (chunk, 1), 0).astype(WIDE)
    place_row = lax.broadcasted_iota(jnp.int32, (1, chunk), 1).astype(WIDE)
    return place_col, place_row


def attend(heads, hd, n, rate_ref, seg_before, seg_row, z_ref, au_ref, a_ref, ss_ref, st_ref, state):
    chunk = z_ref.shape[0]
    seg_col = jnp.transpose(seg_row)[:, :1]
    before = jnp.where(n > 0, seg_before[:1, chunk - 1 :], -1.0)
    last = seg_row[:1, chunk - 1 :]
    row = lax.broadcasted_iota(jnp.int32, (chunk, chunk), 0)
    col = lax.broadcasted_iota(jnp.int32, (chunk, chunk), 1)
    inner = (seg_col == seg_row[:1]) & (row >= col)
    entry_on, tail_on = seg_col == before, seg_col == last
    carry = jnp.where(before == last, 1.0, 0.0)
    place_col, place_row = places(chunk)
    ones = jnp.ones((8, hd), WIDE)
    squares = jnp.zeros((8, chunk), WIDE)
    for h in range(heads):
        rate = rate_ref[h]
        base = h * 4 * hd
        zq, zk, zv, zu = (z_ref[:, base + i * hd : base + (i + 1) * hd] for i in range(4))
        q = (zq * jax.nn.sigmoid(zq)).astype(LOW)
        k = (zk * jax.nn.sigmoid(zk)).astype(LOW)
        v = (zv * jax.nn.sigmoid(zv)).astype(LOW)
        u = zu * jax.nn.sigmoid(zu)
        rows, cols, entry, tail = decays(rate, place_col, place_row, chunk)
        scores = dot(q, k, 1, 1)
        weighted = jnp.where(inner, scores * rows * cols, 0.0).astype(LOW)
        held = state[h]
        st_ref[0, h] = held.astype(LOW)
        a = dot(weighted, v) + jnp.where(entry_on, entry, 0.0) * dot(q, held.astype(LOW))
        kt = (k.astype(WIDE) * jnp.where(tail_on, tail, 0.0)).astype(LOW)
        state[h] = carry * jnp.exp(jnp.full((1, 1), -rate * chunk, WIDE)) * held + dot(kt, v, 0, 0)
        a_ref[:, h * hd : (h + 1) * hd] = a
        au_ref[:, h * hd : (h + 1) * hd] = (a * u).astype(LOW)
        squares = squares + lax.dot_general(
            ones,
            a * a,
            (((1,), (1,)), ((), ())),
            precision=lax.Precision.HIGHEST,
            preferred_element_type=WIDE,
        )
    ss_ref[...] = squares


def slope(z):
    sg = jax.nn.sigmoid(z)
    return sg * (1.0 + z * (1.0 - sg))


def attend_back(
    heads, hd, n, rate_ref, bounds_ref, segc_ref, segr_ref, z_ref, a_ref, dj_ref, ra_ref, m_ref,
    st_ref, dz_ref, o_ref, later
):
    chunk = z_ref.shape[0]
    inner, entry_on, tail_on, carry = masks(bounds_ref, segc_ref[...], segr_ref[...], n, chunk)
    place_col, place_row = places(chunk)
    ra = ra_ref[...]
    m = m_ref[...]
    for h in range(heads):
        rate = rate_ref[h]
        base = h * 4 * hd
        span = slice(h * hd, (h + 1) * hd)
        zq, zk, zv, zu = (z_ref[:, base + i * hd : base + (i + 1) * hd] for i in range(4))
        q = (zq * jax.nn.sigmoid(zq)).astype(LOW)
        k = (zk * jax.nn.sigmoid(zk)).astype(LOW)
        v = (zv * jax.nn.sigmoid(zv)).astype(LOW)
        u = zu * jax.nn.sigmoid(zu)
        an = a_ref[:, span] * ra
        dj = dj_ref[:, span]
        o_ref[:, span] = (an * u).astype(LOW)
        da = (ra * (dj * u - an * m)).astype(LOW)
        rows, cols, entry, tail = decays(rate, place_col, place_row, chunk)
        entry = jnp.where(entry_on, entry, 0.0)
        tail = jnp.where(tail_on, tail, 0.0)
        decay = jnp.where(inner, rows * cols, 0.0)
        weighted = (dot(q, k, 1, 1) * decay).astype(LOW)
        grads = (dot(da, v, 1, 1) * decay).astype(LOW)
        held = st_ref[0, h]
        after = later[h]
        after_low = after.astype(LOW)
        dq = dot(grads, k) + entry * dot(da, held, 1, 1)
        dk = dot(grads, q, 0, 0) + tail * dot(v, after_low, 1, 1)
        dv = dot(weighted, da, 0, 0) + tail * dot(k, after_low)
        qe = (q.astype(WIDE) * entry).astype(LOW)
        later[h] = carry * jnp.exp(jnp.full((1, 1), -rate * chunk, WIDE)) * after + dot(qe, da, 0, 0)
        dz_ref[:, base : base + hd] = (dq * slope(zq)).astype(LOW)
        dz_ref[:, base + hd : base + 2 * hd] = (dk * slope(zk)).astype(LOW)
        dz_ref[:, base + 2 * hd : base + 3 * hd] = (dv * slope(zv)).astype(LOW)
        dz_ref[:, base + 3 * hd : base + 4 * hd] = (dj * an * slope(zu)).astype(LOW)


def empty(shape, kind):
    return pl.pallas_call(
        lambda out: None,
        out_shape=jax.ShapeDtypeStruct(shape, kind),
        out_specs=pl.BlockSpec(memory_space=pl.ANY),
        name="empty",
    )()


def pack_kernel(seq, heads, hd, *refs):
    weights, glu, attn_out, glu_outs = refs[:4], refs[4:6], refs[6], refs[7:]
    for i in range(seq):
        for h in range(heads):
            for m, w in enumerate(weights):
                to, at = (h * 4 + m) * hd, (i * heads + h) * hd
                attn_out[i, :, to : to + hd] = w[:, at : at + hd]
        for w, out in zip(glu, glu_outs):
            n = out.shape[2]
            out[i] = w[:, i * n : (i + 1) * n]


def pack_columns(weights, glu, seq, heads, hd):
    r, kind = weights[0].shape[0], weights[0].dtype
    n = glu[0].shape[1] // seq
    return pl.pallas_call(
        functools.partial(pack_kernel, seq, heads, hd),
        out_shape=[jax.ShapeDtypeStruct((seq, r, heads * 4 * hd), kind)]
        + [jax.ShapeDtypeStruct((seq, r, n), kind)] * 2,
        compiler_params=pltpu.CompilerParams(vmem_limit_bytes=VMEM_BYTES),
        name="pack_columns",
    )(*weights, *glu)


def unpack_kernel(seq, heads, hd, attn, first, second, o_first, o_second, *o_attn):
    for i in range(seq):
        for h in range(heads):
            for m in range(4):
                at, to = (h * 4 + m) * hd, (i * heads + h) * hd
                o_attn[m][:, to : to + hd] = attn[i, :, at : at + hd].astype(WIDE)
        for ref, out in ((first, o_first), (second, o_second)):
            n = ref.shape[2]
            out[:, i * n : (i + 1) * n] = ref[i].astype(WIDE)


def unpack_columns(attn, first, second, heads, hd):
    seq, r = attn.shape[:2]
    shape = lambda n: jax.ShapeDtypeStruct((r, seq * n), WIDE)
    return pl.pallas_call(
        functools.partial(unpack_kernel, seq, heads, hd),
        out_shape=[shape(first.shape[2]), shape(second.shape[2])] + [shape(heads * hd)] * 4,
        compiler_params=pltpu.CompilerParams(vmem_limit_bytes=VMEM_BYTES),
        name="unpack_columns",
    )(attn, first, second)


class Net:
    def __init__(self, shape, send_sem, recv_sem, local_sem):
        self.seq, self.fsdp, self.inner = shape
        self.outer = self.fsdp // self.inner
        self.chips = self.seq // 2
        self.send_sem, self.recv_sem, self.local_sem = send_sem, recv_sem, local_sem
        self.used = 0
        self.locals = 0
        self.s, self.f = lax.axis_index("seq"), lax.axis_index("fsdp")
        self.chip, self.core = self.s // 2, self.s % 2
        self.o, self.i = self.f // self.inner, self.f % self.inner
        self.sent = []

    def seq_peers(self):
        for dx in range(self.chips):
            for dc in range(2):
                if dx or dc:
                    yield dx, dc, lax.rem(self.chip + dx, self.chips) * 2 + lax.rem(self.core + dc, 2)

    def at_seq(self, s):
        return (s, self.f)

    def at_inner(self, j):
        return (self.s, self.o * self.inner + lax.rem(self.i + j, self.inner))

    def at_outer(self, k):
        return (self.s, lax.rem(self.o + k, self.outer) * self.inner + self.i)

    def barrier(self):
        peers = [self.at_seq(s) for _, _, s in self.seq_peers()]
        peers += [self.at_inner(j) for j in range(1, self.inner)]
        peers += [self.at_outer(1), self.at_outer(self.outer - 1)]
        sem = pltpu.get_barrier_semaphore()
        for peer in peers:
            pl.semaphore_signal(sem, inc=1, device_id=peer, device_id_type=pl.DeviceIdType.MESH)
        pl.semaphore_wait(sem, len(peers))

    def send(self, src, dst, device):
        copy = pltpu.make_async_remote_copy(
            src_ref=src,
            dst_ref=dst,
            send_sem=self.send_sem.at[self.used],
            recv_sem=self.recv_sem.at[self.used],
            device_id=device,
            device_id_type=pl.DeviceIdType.MESH,
        )
        self.used += 1
        copy.start()
        self.sent.append(copy)
        return copy

    def copy(self, src, dst):
        copy = pltpu.make_async_copy(src, dst, self.local_sem.at[self.locals])
        self.locals += 1
        copy.start()
        return copy

    def left(self, copy):
        copy.wait_send()
        self.sent = [other for other in self.sent if other is not copy]

    def finish(self):
        for copy in self.sent:
            copy.wait_send()
        self.sent = []


def net_shape(mesh_seq, mesh_fsdp):
    return mesh_seq, mesh_fsdp, 2 if mesh_fsdp == 8 else 4


class Ring:
    def __init__(self, net, piece, full):
        self.net, self.piece, self.full = net, piece, full
        self.copies = [net.copy(piece, full.at[:, net.o, net.i])]
        self.at = 0
        self.coming = None
        self.side = []

    def step(self):
        net, full = self.net, self.full
        if self.at >= net.outer:
            return
        if self.coming is not None:
            self.coming.wait_recv()
        spot = full.at[:, lax.rem(net.o + net.outer - self.at, net.outer), net.i]
        src = self.piece if self.at == 0 else spot
        self.coming = None
        if self.at < net.outer - 1:
            self.coming = net.send(src, spot, net.at_outer(1))
        for j in range(1, net.inner):
            self.side.append(net.send(src, spot, net.at_inner(j)))
        self.at += 1

    def done(self):
        while self.at < self.net.outer:
            self.step()
        for copy in self.side:
            copy.wait_recv()
        for copy in self.copies:
            copy.wait()


class WideRing:
    def __init__(self, net, piece, full):
        self.net, self.full = net, full
        self.copies = [net.copy(piece, full.at[:, net.o, net.i])]
        self.side = [
            net.send(piece, full.at[:, net.o, net.i], net.at_inner(j)) for j in range(1, net.inner)
        ]
        self.at = 0
        self.coming = None

    def step(self):
        net, full = self.net, self.full
        if self.at >= net.outer:
            return
        if self.at == 0:
            for copy in self.side:
                copy.wait_recv()
            for copy in self.copies:
                copy.wait()
        else:
            self.coming.wait_recv()
        spot = full.at[:, lax.rem(net.o + net.outer - self.at, net.outer)]
        if self.at < net.outer - 1:
            self.coming = net.send(spot, spot, net.at_outer(1))
        self.at += 1

    def done(self):
        while self.at < self.net.outer:
            self.step()


def swap(net, blocks, got):
    own = net.copy(blocks.at[net.s], got.at[net.s])
    coming = [
        net.send(blocks.at[s], got.at[net.s], net.at_seq(s)) for _, _, s in net.seq_peers()
    ]
    return own, coming


def arrive(pair):
    own, coming = pair
    own.wait()
    for copy in coming:
        copy.wait_recv()


class Rows:
    def __init__(self, net, own, whole):
        t = own.shape[0]
        self.net, self.whole = net, whole
        spot = lambda s: whole.at[pl.ds(pl.multiple_of(s * t, t), t)]
        self.spot = spot
        self.far = [
            net.send(own, spot(net.s), net.at_seq(lax.rem(net.chip + dx, net.chips) * 2 + net.core))
            for dx in range(1, net.chips)
        ]
        self.near = [net.send(own, spot(net.s), net.at_seq(net.chip * 2 + 1 - net.core))]
        self.own = net.copy(own, spot(net.s))

    def turn(self):
        net = self.net
        for dx, copy in zip(range(1, net.chips), self.far):
            copy.wait_recv()
            spot = self.spot(lax.rem(net.chip + net.chips - dx, net.chips) * 2 + net.core)
            self.near.append(net.send(spot, spot, net.at_seq(net.chip * 2 + 1 - net.core)))

    def done(self):
        for copy in self.near:
            copy.wait_recv()
        self.own.wait()


def gather_kernel(
    shape, heads, hd,
    rate_ref, attn_ref, first_ref, second_ref, out_ref, down_ref, n1_ref, seg_ref, count_ref, x_ref,
    attn_mid, first_mid, second_mid,
    full_attn, full_first, full_second, full_out, full_down,
    n1_all, z_all, a_all, states, mixed_ref, hsum_ref, n2_own, n2_all, core_in, chip_in,
    seg_all, count_all, ss_all,
    w_attn, w_out, au_all, state, stage, term, wide_tile, hsum_tile, x_tile, n2_tile, ss_in,
    seq_buf, in_buf, out_buf, send_sem, recv_sem, local_sem,
):
    net = Net(shape, send_sem, recv_sem, local_sem)
    length, width = n1_all.shape
    cols = z_all.shape[1]
    own_rows = x_ref.shape[0]
    wide = min(512, width)
    net.barrier()
    count = Total(net, count_ref, seq_buf, in_buf, out_buf)
    attn_swap = swap(net, attn_ref, attn_mid)
    seg_own = net.copy(seg_ref, seg_all.at[net.s])
    segs = [net.send(seg_ref, seg_all.at[net.s], net.at_seq(s)) for _, _, s in net.seq_peers()]
    first_swap = swap(net, first_ref, first_mid)
    second_swap = swap(net, second_ref, second_mid)
    rows = Rows(net, n1_ref, n1_all)
    arrive(attn_swap)
    count.step()
    ring_attn = Ring(net, attn_mid, full_attn)
    ring_out = Ring(net, out_ref, full_out)
    for _ in range(net.outer):
        ring_attn.step()
        ring_out.step()
        count.step()
    arrive(first_swap)
    arrive(second_swap)
    ring_first = Ring(net, first_mid, full_first)
    ring_second = Ring(net, second_mid, full_second)
    ring_first.step()
    ring_second.step()
    ring_down = WideRing(net, down_ref, full_down)
    rows.turn()
    queue = [ring_first, ring_second, ring_down] * (net.outer - 1) + [ring_down]

    def pump(times=1):
        for _ in range(min(times, len(queue))):
            queue.pop(0).step()

    seg_own.wait()
    for copy in segs:
        copy.wait_recv()
    ring_attn.done()
    load_attn = net.copy(full_attn, w_attn)
    rows.done()
    ring_out.done()
    load_out = net.copy(full_out, w_out)
    load_attn.wait()
    load_out.wait()

    state[...] = jnp.zeros_like(state)
    per = own_rows // CHUNK

    def seg_of(n):
        at = pl.ds(pl.multiple_of(n % per * CHUNK, CHUNK), CHUNK)
        return jnp.broadcast_to(seg_all[n // per, :, at].astype(WIDE), (8, CHUNK))

    def chunks(low, steps):
        def body(n1_chunk, z_ref, a_ref, st_ref):
            n = low + pl.program_id(0)

            def project(j, _):
                at = pl.ds(pl.multiple_of(j * wide, wide), wide)
                weight = w_attn[:, :, :, :, at].reshape(width, wide)
                z_ref[:, at] = dot(n1_chunk[...], weight)
                return 0

            lax.fori_loop(0, cols // wide, project, 0)
            au_rows = au_all.at[pl.ds(pl.multiple_of(n * CHUNK, CHUNK), CHUNK)]
            attend(
                heads, hd, n, rate_ref, seg_of(jnp.maximum(n - 1, 0)), seg_of(n), z_ref, au_rows,
                a_ref, ss_all.at[n], st_ref, state,
            )

        block = lambda n: pl.BlockSpec((CHUNK, n), lambda i: (low + i, 0))
        pltpu.emit_pipeline(
            body,
            grid=(steps,),
            in_specs=[block(width)],
            out_specs=[
                block(cols),
                block(heads * hd),
                pl.BlockSpec((1, heads, hd, hd), lambda i: (low + i, 0, 0, 0)),
            ],
        )(n1_all, z_all, a_all, states)

    total = length // CHUNK
    half = total // 2
    chunks(0, half)
    pump()
    chunks(half, total - half)
    near_ss = [net.send(ss_all, ss_in.at[net.s], net.at_seq(s)) for _, _, s in net.seq_peers()]
    pump()

    used = [None, None]
    turns = [0]

    def product(row, each):
        x = au_all[pl.ds(pl.multiple_of(row, CHUNK), CHUNK)]

        def one(j, _):
            at = pl.ds(pl.multiple_of(j * wide, wide), wide)
            weight = w_out[:, :, :, :, at].reshape(heads * hd, wide)
            each(at, dot(x, weight))
            return 0

        lax.fori_loop(0, width // wide, one, 0)

    def slot():
        i = turns[0] % 2
        turns[0] += 1
        if used[i] is not None:
            net.left(used[i])
        return i

    def row_of(chip, core, t):
        return (chip * 2 + core) * own_rows + t * CHUNK

    near = {}
    far = []

    def give(dx):
        chip = lax.rem(net.chip + dx, net.chips)
        for t in range(per):
            i = slot()

            def store(at, part, i=i):
                stage[i, :, at] = part.astype(LOW)

            product(row_of(chip, 1 - net.core, t), store)
            spot = core_in.at[dx, pl.ds(t * CHUNK, CHUNK)]
            used[i] = near[dx, t] = net.send(
                stage.at[i], spot, net.at_seq(net.chip * 2 + 1 - net.core)
            )

    def keep(dx, finish=None):
        chip = lax.rem(net.chip + dx, net.chips)
        for t in range(per):
            span = pl.ds(t * CHUNK, CHUNK)
            near[dx, t].wait_recv()
            loads = [net.copy(core_in.at[dx, span], term.at[0])]
            if dx == 0:
                loads.append(net.copy(x_ref.at[span], x_tile))
                for j, copies in enumerate(far):
                    copies[t].wait_recv()
                    loads.append(net.copy(chip_in.at[j, span], term.at[j + 1]))
            else:
                i = slot()
            for load in loads:
                load.wait()

            def store(at, part):
                add = part + term[0, :, at].astype(WIDE)
                if dx == 0:
                    for j in range(len(far)):
                        add = add + term[j + 1, :, at].astype(WIDE)
                    wide_tile[:, at] = add
                else:
                    stage[i, :, at] = add.astype(LOW)

            product(row_of(chip, net.core, t), store)
            if dx == 0:
                finish(t, span)
            else:
                used[i] = net.send(
                    stage.at[i], chip_in.at[dx - 1, span], net.at_seq(chip * 2 + net.core)
                )
                far[dx - 1].append(used[i])

    def finish(t, span):
        at = net.s * per + t
        squares = ss_in[0, at]
        for j in range(1, net.seq):
            squares = squares + ss_in[j, at]
        ra = lax.rsqrt(jnp.transpose(squares)[:, :1] / width + 1e-6)

        def add(j, squares):
            at = pl.ds(pl.multiple_of(j * wide, wide), wide)
            mixed = wide_tile[:, at] * ra
            wide_tile[:, at] = mixed
            hsum = x_tile[:, at].astype(WIDE) + mixed
            hsum_tile[:, at] = hsum
            return squares + jnp.sum(hsum * hsum, axis=1, keepdims=True)

        squares = lax.fori_loop(0, width // wide, add, jnp.zeros((CHUNK, 1), WIDE))
        r2 = lax.rsqrt(squares / width + 1e-6)

        def scale(j, _):
            at = pl.ds(pl.multiple_of(j * wide, wide), wide)
            n2_tile[:, at] = (hsum_tile[:, at] * r2).astype(LOW)
            return 0

        lax.fori_loop(0, width // wide, scale, 0)
        outs = [
            net.copy(wide_tile, mixed_ref.at[span]),
            net.copy(hsum_tile, hsum_ref.at[span]),
            net.copy(n2_tile, n2_own.at[span]),
        ]
        for out in outs:
            out.wait()

    for dx in range(1, net.chips):
        far.append([])
        give(dx)
        keep(dx)
    pump()
    give(0)
    pump(2)
    for copy in near_ss:
        copy.wait_recv()
    for copy in near_ss:
        net.left(copy)
    ss_in[net.s] = ss_all[...]
    keep(0, finish)
    rows = Rows(net, n2_own, n2_all)
    pump(3)
    rows.turn()
    pump(len(queue))
    count_all[...] = count.done()
    for ring in (ring_first, ring_second, ring_down):
        ring.done()
    rows.done()
    total_ss = ss_in[0]
    for j in range(1, net.seq):
        total_ss = total_ss + ss_in[j]
    ss_all[...] = total_ss
    net.finish()


HBM = pl.BlockSpec(memory_space=pl.ANY)


def gather_all(shape, heads, hd, rates, attn, first, second, w_out, w_down, n1, seg, count, x):
    seq, fsdp, inner = shape
    outer = fsdp // inner
    chips = seq // 2
    own_rows, width = n1.shape
    length = own_rows * seq
    cols = attn.shape[2]
    chunks = length // CHUNK
    like = lambda v, lead: jax.ShapeDtypeStruct(lead + v.shape[-2:], v.dtype)
    ring = lambda v: like(v, (v.shape[0], outer, inner))
    low = lambda *dims: jax.ShapeDtypeStruct(dims, LOW)
    wide = lambda *dims: jax.ShapeDtypeStruct(dims, WIDE)
    outs = [like(v, (seq,)) for v in (attn, first, second)]
    outs += [ring(v) for v in (attn, first, second, w_out, w_down)]
    outs += [low(length, width), wide(length, cols), wide(length, heads * hd)]
    outs += [low(chunks, heads, hd, hd), wide(own_rows, width), wide(own_rows, width)]
    outs += [low(own_rows, width), low(length, width)]
    outs += [low(chips, own_rows, width), low(max(chips - 1, 1), own_rows, width)]
    in_hbm = len(outs)
    outs += [jax.ShapeDtypeStruct((seq,) + seg.shape, seg.dtype), wide(8, 128)]
    outs += [wide(chunks, 8, CHUNK)]
    copies = 7 * seq + 5 * (outer * inner + outer) + total_copies(shape) + 2 * chunks + 4 * seq
    in_vmem = pl.BlockSpec(memory_space=pltpu.VMEM)
    smem = pl.BlockSpec(memory_space=pltpu.SMEM)
    got = pl.pallas_call(
        functools.partial(gather_kernel, shape, heads, hd),
        in_specs=[smem] + [HBM] * 7 + [in_vmem, HBM],
        out_specs=[HBM] * in_hbm + [in_vmem] * 3,
        out_shape=outs,
        scratch_shapes=[
            pltpu.VMEM(ring(attn).shape, LOW),
            pltpu.VMEM(ring(w_out).shape, LOW),
            pltpu.VMEM((length, heads * hd), LOW),
            pltpu.VMEM((heads, hd, hd), WIDE),
            pltpu.VMEM((2, CHUNK, width), LOW),
            pltpu.VMEM((chips, CHUNK, width), LOW),
            pltpu.VMEM((CHUNK, width), WIDE),
            pltpu.VMEM((CHUNK, width), WIDE),
            pltpu.VMEM((CHUNK, width), LOW),
            pltpu.VMEM((CHUNK, width), LOW),
            pltpu.VMEM((seq, chunks, 8, CHUNK), WIDE),
        ]
        + total_scratch(shape)
        + [
            pltpu.SemaphoreType.DMA((copies,)),
            pltpu.SemaphoreType.DMA((copies,)),
            pltpu.SemaphoreType.DMA((24 + 6 * chunks,)),
        ],
        compiler_params=pltpu.CompilerParams(
            collective_id=0, has_side_effects=True, vmem_limit_bytes=VMEM_BYTES
        ),
        name="gather_all",
    )(rates, attn, first, second, w_out, w_down, n1, seg, count, x)
    flat = lambda v: v.reshape(-1, v.shape[-1])
    squares = got[in_hbm + 2][:, 0].reshape(length, 1)
    return [flat(v) for v in got[3:8]] + list(got[8:14]) + [got[15], got[in_hbm], got[in_hbm + 1], squares]


class Total:
    def __init__(self, net, own, seq_buf, in_buf, out_buf):
        self.net, self.bufs, self.stage = net, (seq_buf, in_buf, out_buf), 0
        self.coming = self.share(seq_buf, net.s, own[...], [net.at_seq(s) for _, _, s in net.seq_peers()])

    def share(self, buf, at, value, devices):
        buf[at] = value
        return [self.net.send(buf.at[at], buf.at[at], device) for device in devices]

    def gathered(self, buf):
        for copy in self.coming:
            copy.wait_recv()
        total = buf[0]
        for j in range(1, buf.shape[0]):
            total = total + buf[j]
        return total

    def step(self):
        net, (seq_buf, in_buf, out_buf) = self.net, self.bufs
        if self.stage == 0:
            peers = [net.at_inner(j) for j in range(1, net.inner)]
            self.coming = self.share(in_buf, net.i, self.gathered(seq_buf), peers)
        elif self.stage == 1:
            self.coming = self.share(out_buf, net.o, self.gathered(in_buf), [net.at_outer(1)])
        elif self.stage < net.outer:
            self.coming[-1].wait_recv()
            at = lax.rem(net.o + net.outer - self.stage + 1, net.outer)
            self.coming = [net.send(out_buf.at[at], out_buf.at[at], net.at_outer(1))]
        self.stage += 1

    def done(self):
        while self.stage < self.net.outer:
            self.step()
        return self.gathered(self.bufs[2])


def total_scratch(shape):
    seq, fsdp, inner = shape
    return [pltpu.VMEM((n, 8, 128), WIDE) for n in (seq, inner, fsdp // inner)]


def total_copies(shape):
    seq, fsdp, inner = shape
    return seq + inner + fsdp // inner


class Sum:
    def __init__(self, net, g, side, ring, send, load):
        self.net, self.g, self.side_ref, self.ring_ref = net, g, side, ring
        self.send_buf, self.load = send, load
        self.side = []
        self.ring = []
        for k in range(net.outer):
            o = self.spot(k)
            now = []
            for j in range(1, net.inner):
                to = lax.rem(net.i + j, net.inner)
                now.append(net.send(g.at[:, o, to], side.at[j - 1, :, o], net.at_inner(j)))
            self.side.append(now)
        self.at = 0

    def spot(self, k):
        return lax.rem(self.net.o + 2 * self.net.outer - 1 - k, self.net.outer)

    def step(self, final):
        net, k = self.net, self.at
        self.at += 1
        o = self.spot(k)
        terms = self.load
        loads = [net.copy(self.g.at[:, o, net.i], terms.at[0])]
        for j, copy in enumerate(self.side[k]):
            copy.wait_recv()
            loads.append(net.copy(self.side_ref.at[j, :, o], terms.at[j + 1]))
        count = net.inner
        if k > 0:
            self.ring[k - 1].wait_recv()
            loads.append(net.copy(self.ring_ref.at[k - 1], terms.at[count]))
            count += 1
        if k >= 2:
            net.left(self.ring[k - 2])
        for load in loads:
            load.wait()

        def one(i, _):
            total = terms[0, i].astype(WIDE)
            for j in range(1, count):
                total = total + terms[j, i].astype(WIDE)
            if k < net.outer - 1:
                self.send_buf[k % 2, i] = total.astype(LOW)
            else:
                final(i, total)
            return 0

        lax.fori_loop(0, terms.shape[1], one, 0)
        if k < net.outer - 1:
            self.ring.append(net.send(self.send_buf.at[k % 2], self.ring_ref.at[k], net.at_outer(1)))


GRADS = ("down", "first", "second", "attn", "out")
SPLIT = ("first", "second", "attn")
LOADS = ("down", "first", "attn", "out")


def back_kernel(
    shape, heads, hd,
    rate_ref, bounds_ref, segc, segr, z, a, dh, ra, mean, states, w_out, w_attn, n1, loss_ref,
    g_down, g_first, g_second,
    dn1_ref, o_down, o_out, o_loss, got_first, got_second, got_attn, g_attn,
    side_down, side_first, side_second, side_attn, side_out,
    ring_down, ring_first, ring_second, ring_attn, ring_out,
    core_in, chip_in,
    dz_all, later, dj, o_chunk, out_acc, g_out, stage, term, wide_tile,
    *rest
):
    it = iter(rest)
    take = lambda names: {name: next(it) for name in names}
    sends, loads = take(GRADS), take(LOADS)
    loads["second"] = loads["first"]
    total_bufs = [next(it) for _ in range(3)]
    send_sem, recv_sem, local_sem = (next(it) for _ in range(3))
    net = Net(shape, send_sem, recv_sem, local_sem)
    grads = dict(down=g_down, first=g_first, second=g_second, attn=g_attn, out=g_out)
    sides = dict(down=side_down, first=side_first, second=side_second, attn=side_attn, out=side_out)
    rings = dict(down=ring_down, first=ring_first, second=ring_second, attn=ring_attn, out=ring_out)
    gots = dict(first=got_first, second=got_second, attn=got_attn)
    owned = dict(down=o_down, out=o_out)
    length, cols = dz_all.shape
    width = dh.shape[1]
    count = length // CHUNK
    wide = min(512, width)

    net.barrier()
    sums, swaps, queue = {}, {}, []
    loss = Total(net, loss_ref, *total_bufs)

    def begin(name):
        sums[name] = Sum(net, grads[name], sides[name], rings[name], sends[name], loads[name])
        queue.extend([name] * net.outer)

    def pump(times=1):
        for _ in range(min(times, len(queue))):
            name = queue.pop(0)

            def final(i, rows):
                if name in owned:
                    owned[name][...] = rows
                else:
                    totals[i] = rows.astype(LOW)

            totals = sends[name].at[(net.outer - 1) % 2]
            sums[name].step(final)
            if name in SPLIT and sums[name].at == net.outer:
                swaps[name] = swap(net, totals, gots[name])

    loss.step()
    for name in ("down", "first", "second"):
        begin(name)

    later[...] = jnp.zeros_like(later)
    out_acc[...] = jnp.zeros_like(out_acc)

    def chunks(top, steps):
        def body(segc_ref, segr_ref, z_ref, a_ref, dh_ref, ra_ref, m_ref, st_ref):
            n = top - pl.program_id(0)
            dj[...] = dot(dh_ref[...], w_out[...], 1, 1)
            rows = pl.ds(pl.multiple_of(n * CHUNK, CHUNK), CHUNK)
            attend_back(
                heads, hd, n, rate_ref, bounds_ref, segc_ref, segr_ref, z_ref, a_ref, dj, ra_ref,
                m_ref, st_ref, dz_all.at[rows], o_chunk, later,
            )

            def add(j, _):
                at = pl.ds(pl.multiple_of(j * wide, wide), wide)
                out_acc[:, at] += dot(o_chunk[...], dh_ref[:, at], 0, 0)
                return 0

            lax.fori_loop(0, width // wide, add, 0)

        block = lambda n: pl.BlockSpec((CHUNK, n), lambda i: (top - i, 0))
        pltpu.emit_pipeline(
            body,
            grid=(steps,),
            in_specs=[
                block(1),
                pl.BlockSpec((1, CHUNK), lambda i: (0, top - i)),
                block(cols),
                block(heads * hd),
                block(width),
                block(1),
                block(1),
                pl.BlockSpec((1, heads, hd, hd), lambda i: (top - i, 0, 0, 0)),
            ],
        )(segc, segr, z, a, dh, ra, mean, states)

    half = count // 2
    chunks(count - 1, half)
    loss.step()
    pump()
    chunks(count - 1 - half, count - half)
    loss.step()
    pump()

    own_rows = dn1_ref.shape[0]
    tile = min(256, own_rows)
    used = [None, None]
    turns = [0]

    def product(row, each):
        x = dz_all[pl.ds(pl.multiple_of(row, tile), tile)]

        def one(j, _):
            at = pl.ds(pl.multiple_of(j * wide, wide), wide)
            each(at, dot(x, w_attn[at, :], 1, 1))
            return 0

        lax.fori_loop(0, width // wide, one, 0)

    def slot():
        i = turns[0] % 2
        turns[0] += 1
        if used[i] is not None:
            net.left(used[i])
        return i

    def row_of(chip, core, t):
        return (chip * 2 + core) * own_rows + t * tile

    near = {}
    far = []

    def give(dx):
        chip = lax.rem(net.chip + dx, net.chips)
        for t in range(own_rows // tile):
            i = slot()

            def store(at, part, i=i):
                stage[i, :, at] = part.astype(LOW)

            product(row_of(chip, 1 - net.core, t), store)
            spot = core_in.at[dx, pl.ds(t * tile, tile)]
            used[i] = near[dx, t] = net.send(
                stage.at[i], spot, net.at_seq(net.chip * 2 + 1 - net.core)
            )

    def keep(dx):
        chip = lax.rem(net.chip + dx, net.chips)
        for t in range(own_rows // tile):
            span = pl.ds(t * tile, tile)
            near[dx, t].wait_recv()
            loads = [net.copy(core_in.at[dx, span], term.at[0])]
            if dx == 0:
                for j, copies in enumerate(far):
                    copies[t].wait_recv()
                    loads.append(net.copy(chip_in.at[j, span], term.at[j + 1]))
            else:
                i = slot()
            for load in loads:
                load.wait()

            def store(at, part):
                total = part
                for j in range(len(loads)):
                    total = total + term[j, :, at].astype(WIDE)
                if dx == 0:
                    wide_tile[:, at] = total
                else:
                    stage[i, :, at] = total.astype(LOW)

            product(row_of(chip, net.core, t), store)
            if dx == 0:
                net.copy(wide_tile, dn1_ref.at[span]).wait()
            else:
                used[i] = net.send(
                    stage.at[i], chip_in.at[dx - 1, span], net.at_seq(chip * 2 + net.core)
                )
                far[dx - 1].append(used[i])

    for dx in range(1, net.chips):
        far.append([])
        give(dx)
        keep(dx)
    pump()

    parts = 2
    spread = net.outer // parts
    features = width // net.seq // parts

    def grad_body(n1_ref, g_ref):
        for j in range(cols // wide):
            at = slice(j * wide, (j + 1) * wide)
            got = dot(n1_ref[...], dz_all[:, at], 0, 0).astype(LOW)
            g_ref[:, :, :, :, at] = got.reshape(g_ref.shape[:-1] + (wide,))

    pltpu.emit_pipeline(
        grad_body,
        grid=(net.seq, parts),
        in_specs=[pl.BlockSpec((length, features), lambda i, j: (0, i * parts + j))],
        out_specs=[
            pl.BlockSpec((1, spread) + g_attn.shape[2:], lambda i, j: (i, j, 0, 0, 0)),
        ],
    )(n1, g_attn)
    begin("attn")
    for j in range(width // wide):
        at = slice(j * wide, (j + 1) * wide)
        g_out[:, :, :, :, at] = out_acc[:, at].astype(LOW).reshape(g_out.shape[:-1] + (wide,))
    begin("out")
    pump(2)
    give(0)
    pump()
    keep(0)
    o_loss[...] = loss.done()
    pump(len(queue))
    for name in SPLIT:
        arrive(swaps[name])
    net.finish()


def back_all(shape, heads, hd, rates, bounds, seg, z, a, dh, ra, mean, states, w_out, w_attn, n1, loss, grads):
    seq, fsdp, inner = shape
    outer = fsdp // inner
    length, width = dh.shape
    cols = z.shape[1]
    own_rows = length // seq
    chips = seq // 2
    tile = min(256, own_rows)
    lead = {"down": 1, "out": 1, "first": seq, "second": seq, "attn": seq}
    blocks = [
        g.reshape(lead[n], outer, inner, g.shape[0] // (lead[n] * fsdp), g.shape[1])
        for n, g in zip(GRADS, grads)
    ]
    size = {n: (g.shape[0], g.shape[3], g.shape[4]) for n, g in zip(GRADS, blocks)}
    size["attn"] = (seq, width // (seq * fsdp), cols)
    size["out"] = (1, width // (seq * fsdp), width)
    whole = lambda n: (size[n][0], outer, inner) + size[n][1:]
    low = lambda dims: jax.ShapeDtypeStruct(dims, LOW)
    row = lambda n: jax.ShapeDtypeStruct(size[n][1:], WIDE)
    outs = [jax.ShapeDtypeStruct((own_rows, width), WIDE), row("down"), row("out")]
    outs += [jax.ShapeDtypeStruct((8, 128), WIDE)]
    outs += [low(size[n]) for n in SPLIT] + [low(whole("attn"))]
    outs += [low((inner - 1, size[n][0], outer) + size[n][1:]) for n in GRADS]
    outs += [low((outer - 1,) + size[n]) for n in GRADS]
    outs += [low((chips, own_rows, width)), low((max(chips - 1, 1), own_rows, width))]
    in_vmem = pl.BlockSpec(memory_space=pltpu.VMEM)
    smem = pl.BlockSpec(memory_space=pltpu.SMEM)
    scratch = [
        pltpu.VMEM((length, cols), LOW),
        pltpu.VMEM((heads, hd, hd), WIDE),
        pltpu.VMEM((CHUNK, heads * hd), WIDE),
        pltpu.VMEM((CHUNK, heads * hd), LOW),
        pltpu.VMEM((heads * hd, width), WIDE),
        pltpu.VMEM(whole("out"), LOW),
        pltpu.VMEM((2, tile, width), LOW),
        pltpu.VMEM((chips, tile, width), LOW),
        pltpu.VMEM((tile, width), WIDE),
    ]
    scratch += [pltpu.VMEM((2,) + size[n], LOW) for n in GRADS]
    scratch += [pltpu.VMEM((inner + 1,) + size[n], LOW) for n in LOADS]
    scratch += total_scratch(shape)
    copies = 5 * (outer * inner + outer) + 3 * seq + total_copies(shape) + 2 * length // tile
    scratch += [
        pltpu.SemaphoreType.DMA((copies,)),
        pltpu.SemaphoreType.DMA((copies,)),
        pltpu.SemaphoreType.DMA((5 * outer * (inner + 1) + 3 + 4 * length // tile,)),
    ]
    return pl.pallas_call(
        functools.partial(back_kernel, shape, heads, hd),
        in_specs=[smem, smem] + [HBM] * 8 + [in_vmem] * 2 + [HBM, in_vmem] + [HBM] * 3,
        out_specs=[HBM] + [in_vmem] * 3 + [HBM] * (len(outs) - 4),
        out_shape=outs,
        scratch_shapes=scratch,
        compiler_params=pltpu.CompilerParams(
            collective_id=1, has_side_effects=True, vmem_limit_bytes=VMEM_BYTES
        ),
        name="back_all",
    )(
        rates, bounds, seg.reshape(length, 1), seg.reshape(1, length), z, a, dh, ra, mean, states,
        w_out, w_attn, n1, loss, *blocks
    )[:7]


class Moves:
    def __init__(self):
        self.seq = lax.axis_size("seq")
        self.fsdp = lax.axis_size("fsdp")
        self.inner = 2 if self.fsdp == 8 else 4
        self.outer = self.fsdp // self.inner
        self.chips = self.seq // 2
        s = lax.axis_index("seq")
        f = lax.axis_index("fsdp")
        self.s, self.f = s, f
        self.chip, self.core = s // 2, s % 2
        self.out_at, self.in_at = f // self.inner, f % self.inner
        chips, inner, outer = self.chips, self.inner, self.outer
        self.core_perm = [(i, i ^ 1) for i in range(self.seq)]
        self.chip_perm = [
            (x * 2 + c, (x + 1) % chips * 2 + c) for x in range(chips) for c in range(2)
        ]
        self.out_perm = [
            (o * inner + i, (o + 1) % outer * inner + i)
            for o in range(outer)
            for i in range(inner)
        ]
        self.in_perm = [
            (o * inner + i, o * inner + (i + 1) % inner)
            for o in range(outer)
            for i in range(inner)
        ]

    def to_core(self, v):
        return lax.ppermute(v, "seq", self.core_perm)

    def to_chip(self, v):
        return lax.ppermute(v, "seq", self.chip_perm)

    def to_out(self, v):
        return lax.ppermute(v, "fsdp", self.out_perm)

    def to_in(self, v):
        return lax.ppermute(v, "fsdp", self.in_perm)

    def gather_seq(self, v):
        whole = empty((self.seq * v.shape[0],) + v.shape[1:], v.dtype)
        t = v.shape[0]
        now = v
        for k in range(self.chips):
            later = self.to_chip(now) if k < self.chips - 1 else None
            other = self.to_core(now)
            chip = (self.chip - k) % self.chips
            place = lambda whole, part, i: lax.dynamic_update_slice_in_dim(whole, part, i * t, 0)
            whole = place(whole, now, chip * 2 + self.core)
            whole = place(whole, other, chip * 2 + 1 - self.core)
            now = later
        return whole

    def sum_axis(self, v, axis, size):
        step = 1
        while step < size:
            v = v + lax.ppermute(v, axis, [(i, i ^ step) for i in range(size)])
            step *= 2
        return v

    def sum_seq(self, v):
        return self.sum_axis(v, "seq", self.seq)

    def sum_all(self, v):
        return self.sum_axis(self.sum_seq(v), "fsdp", self.fsdp)


class ScatterSeq:
    def __init__(self, move, part, kind=LOW):
        self.move, self.part, self.kind = move, part, kind
        self.held = None
        self.term = None
        for k in range(move.chips - 1):
            total = self.own(k)
            self.held = move.to_chip(total.astype(kind))

    def own(self, k, *tokens):
        move = self.move
        self.term = self.part((move.chip - 1 - k) % move.chips, *tokens)
        term = self.term.reshape((2, -1) + self.term.shape[1:])
        give = lax.dynamic_index_in_dim(term, 1 - move.core, 0, False)
        keep = lax.dynamic_index_in_dim(term, move.core, 0, False)
        total = keep.astype(WIDE) + move.to_core(give).astype(WIDE)
        if self.held is not None:
            total = total + self.held.astype(WIDE)
        return total

    def done(self, *tokens):
        return self.own(self.move.chips - 1, *tokens)


def after(v, *tokens):
    if not tokens:
        return v
    return lax.optimization_barrier((v,) + tokens)[0]


def on_device(
    inputs,
    teacher,
    segment_ids,
    valid,
    decay_rate,
    w_query,
    w_key,
    w_value,
    w_gate,
    w_out,
    w_first,
    w_second,
    w_down,
):
    move = Moves()
    seq = move.seq
    batch, block_len, width = inputs.shape
    assert batch == 1
    heads_all = decay_rate.shape[0]
    hd = width // heads_all
    heads = heads_all // seq
    own_rows = w_query.shape[0]
    ff = w_first.shape[1]
    ffs = ff // seq
    cols = heads * 4 * hd

    shape = net_shape(seq, move.fsdp)
    keep = valid.astype(WIDE).reshape(block_len, 1)
    spread = lambda v: jnp.broadcast_to(v, (8, 128))

    attn_own, first_own, second_own = pack_columns(
        (w_query, w_key, w_value, w_gate), (w_first, w_second), seq, heads, hd
    )
    x32 = inputs.reshape(block_len, width).astype(WIDE)
    r1 = lax.rsqrt(jnp.mean(x32 * x32, axis=-1, keepdims=True) + 1e-6)
    n1 = x32 * r1
    rates = lax.dynamic_slice_in_dim(decay_rate, move.s * heads, heads, 0)
    (
        full_attn, full_first, full_second, full_out, full_down, n1_all, z, a, states, mixed_out,
        hsum, n2_all, seg, count, squares,
    ) = gather_all(
        shape,
        heads,
        hd,
        rates,
        attn_own,
        first_own,
        second_own,
        w_out[None],
        w_down[None],
        n1.astype(LOW),
        segment_ids.reshape(1, block_len),
        spread(jnp.sum(keep)),
        inputs.reshape(block_len, width),
    )
    seg = seg.reshape(seq * block_len)
    length = seg.shape[0]
    count = count[:1, :1]
    bounds = jnp.concatenate([jnp.full((1,), -1, jnp.int32), seg[CHUNK - 1 :: CHUNK]])
    ra_all = lax.rsqrt(squares / width + 1e-6)
    r2 = lax.rsqrt(jnp.mean(hsum * hsum, axis=-1, keepdims=True) + 1e-6)
    m2 = hsum * r2

    def rows_of(v, chip):
        return lax.dynamic_slice_in_dim(v, chip * 2 * block_len, 2 * block_len, 0)

    def product_scatter(pairs):
        def part(chip, *tokens):
            left = [rows_of(after(v, *tokens), chip) for v, _, _ in pairs]
            return sum(dot(l, w, 1, d) for l, (_, w, d) in zip(left, pairs)).astype(LOW)

        return ScatterSeq(move, part)

    g1 = dot(n2_all, full_first)
    g2 = dot(n2_all, full_second)
    p = (g1 * g2).astype(LOW)
    g1 = g1.astype(LOW)
    g2 = g2.astype(LOW)
    y_sum = product_scatter([(p, full_down, 0)])
    y = hsum + y_sum.done()
    layer_out = y.astype(LOW).reshape(1, block_len, width)

    error = y - teacher.reshape(block_len, width).astype(WIDE)
    tokens = block_len * seq * move.fsdp
    dy = tokens / count * keep * error
    dyb = dy.astype(LOW)
    dy_all = move.gather_seq(dyb)

    dp = dot(dy_all, full_down, 1, 1)
    dg1 = (dp * g2.astype(WIDE)).astype(LOW)
    dg2 = (dp * g1.astype(WIDE)).astype(LOW)
    dn2_sum = product_scatter([(dg1, full_first, 1), (dg2, full_second, 1)])
    grad_down = dot(after(p, dn2_sum.term), dy_all, 0, 0).astype(LOW)
    dn2 = dn2_sum.done(grad_down)
    dh = dy + r2 * (dn2 - m2 * jnp.mean(dn2 * m2, axis=-1, keepdims=True))
    dhb = dh.astype(LOW)
    mean_own = jnp.mean(after(dhb, dn2_sum.term).astype(WIDE) * mixed_out, axis=-1)
    dh_all = move.gather_seq(dhb)
    mean_all = move.gather_seq(mean_own).reshape(length, 1)
    grad_first = dot(after(n2_all, mean_own), dg1, 0, 0).astype(LOW)
    grad_second = dot(after(n2_all, grad_first), dg2, 0, 0).astype(LOW)

    dn1, share_down, share_out, loss, got_first, got_second, got_attn = back_all(
        shape, heads, hd, rates, bounds, seg, z, a, dh_all, ra_all, mean_all, states, full_out,
        full_attn, n1_all, spread(jnp.sum(keep * error * error)),
        (grad_down, grad_first, grad_second),
    )
    input_grad = dh + r1 * (dn1 - n1 * jnp.mean(dn1 * n1, axis=-1, keepdims=True))
    loss = loss[0, 0] / (width * count)
    share_first, share_second, *share_attn = unpack_columns(
        got_attn, got_first, got_second, heads, hd
    )

    return (
        layer_out,
        loss.reshape(()),
        input_grad.reshape(1, block_len, width),
        share_attn[0],
        share_attn[1],
        share_attn[2],
        share_attn[3],
        share_out,
        share_first,
        share_second,
        share_down,
    )


def solution(mesh):
    rows = P(("seq", "fsdp"), None)
    tokens = P("fsdp", "seq", None)
    return jax.shard_map(
        on_device,
        mesh=mesh,
        in_specs=(tokens, tokens, P("fsdp", "seq"), P("fsdp", "seq"), P()) + (rows,) * 8,
        out_specs=(tokens, P(), tokens) + (rows,) * 8,
        check_vma=False,
    )
```

```python
import functools

import jax
import jax.numpy as jnp
from jax import lax
from jax.experimental import pallas as pl
from jax.experimental.pallas import tpu as pltpu
from jax.sharding import PartitionSpec as P

CHUNK = 256
WIDE = jnp.float32
LOW = jnp.bfloat16
VMEM_BYTES = 60 * 1024 * 1024


def dot(left, right, left_dim=1, right_dim=0):
    return lax.dot_general(
        left, right, (((left_dim,), (right_dim,)), ((), ())), preferred_element_type=WIDE
    )


def decays(rate, place_col, place_row, chunk):
    rows = jnp.exp(-rate * place_col)
    cols = jnp.exp(rate * place_row)
    entry = jnp.exp(-rate * (place_col + 1.0))
    tail = jnp.exp(-rate * (chunk - 1.0 - place_col))
    return rows, cols, entry, tail


def masks(bounds_ref, seg_col, seg_row, n, chunk):
    before = bounds_ref[n]
    last = bounds_ref[n + 1]
    row = lax.broadcasted_iota(jnp.int32, (chunk, chunk), 0)
    col = lax.broadcasted_iota(jnp.int32, (chunk, chunk), 1)
    inner = (seg_col == seg_row) & (row >= col)
    return inner, seg_col == before, seg_col == last, jnp.where(before == last, 1.0, 0.0)


def places(chunk):
    place_col = lax.broadcasted_iota(jnp.int32, (chunk, 1), 0).astype(WIDE)
    place_row = lax.broadcasted_iota(jnp.int32, (1, chunk), 1).astype(WIDE)
    return place_col, place_row


def attend(heads, hd, n, rate_ref, seg_before, seg_row, z_ref, au_ref, a_ref, ss_ref, st_ref, state):
    chunk = z_ref.shape[0]
    seg_col = jnp.transpose(seg_row)[:, :1]
    before = jnp.where(n > 0, seg_before[:1, chunk - 1 :], -1.0)
    last = seg_row[:1, chunk - 1 :]
    row = lax.broadcasted_iota(jnp.int32, (chunk, chunk), 0)
    col = lax.broadcasted_iota(jnp.int32, (chunk, chunk), 1)
    inner = (seg_col == seg_row[:1]) & (row >= col)
    entry_on, tail_on = seg_col == before, seg_col == last
    carry = jnp.where(before == last, 1.0, 0.0)
    place_col, place_row = places(chunk)
    ones = jnp.ones((8, hd), WIDE)
    squares = jnp.zeros((8, chunk), WIDE)
    for h in range(heads):
        rate = rate_ref[h]
        base = h * 4 * hd
        zq, zk, zv, zu = (z_ref[:, base + i * hd : base + (i + 1) * hd] for i in range(4))
        q = (zq * jax.nn.sigmoid(zq)).astype(LOW)
        k = (zk * jax.nn.sigmoid(zk)).astype(LOW)
        v = (zv * jax.nn.sigmoid(zv)).astype(LOW)
        u = zu * jax.nn.sigmoid(zu)
        rows, cols, entry, tail = decays(rate, place_col, place_row, chunk)
        scores = dot(q, k, 1, 1)
        weighted = jnp.where(inner, scores * rows * cols, 0.0).astype(LOW)
        held = state[h]
        st_ref[0, h] = held.astype(LOW)
        a = dot(weighted, v) + jnp.where(entry_on, entry, 0.0) * dot(q, held.astype(LOW))
        kt = (k.astype(WIDE) * jnp.where(tail_on, tail, 0.0)).astype(LOW)
        state[h] = carry * jnp.exp(jnp.full((1, 1), -rate * chunk, WIDE)) * held + dot(kt, v, 0, 0)
        a_ref[:, h * hd : (h + 1) * hd] = a
        au_ref[:, h * hd : (h + 1) * hd] = (a * u).astype(LOW)
        squares = squares + lax.dot_general(
            ones,
            a * a,
            (((1,), (1,)), ((), ())),
            precision=lax.Precision.HIGHEST,
            preferred_element_type=WIDE,
        )
    ss_ref[...] = squares


def slope(z):
    sg = jax.nn.sigmoid(z)
    return sg * (1.0 + z * (1.0 - sg))


def attend_back(
    heads, hd, n, rate_ref, bounds_ref, segc_ref, segr_ref, z_ref, a_ref, dj_ref, ra_ref, m_ref,
    st_ref, dz_ref, o_ref, later
):
    chunk = z_ref.shape[0]
    inner, entry_on, tail_on, carry = masks(bounds_ref, segc_ref[...], segr_ref[...], n, chunk)
    place_col, place_row = places(chunk)
    ra = ra_ref[...]
    m = m_ref[...]
    for h in range(heads):
        rate = rate_ref[h]
        base = h * 4 * hd
        span = slice(h * hd, (h + 1) * hd)
        zq, zk, zv, zu = (z_ref[:, base + i * hd : base + (i + 1) * hd] for i in range(4))
        q = (zq * jax.nn.sigmoid(zq)).astype(LOW)
        k = (zk * jax.nn.sigmoid(zk)).astype(LOW)
        v = (zv * jax.nn.sigmoid(zv)).astype(LOW)
        u = zu * jax.nn.sigmoid(zu)
        an = a_ref[:, span] * ra
        dj = dj_ref[:, span]
        o_ref[:, span] = (an * u).astype(LOW)
        da = (ra * (dj * u - an * m)).astype(LOW)
        rows, cols, entry, tail = decays(rate, place_col, place_row, chunk)
        entry = jnp.where(entry_on, entry, 0.0)
        tail = jnp.where(tail_on, tail, 0.0)
        decay = jnp.where(inner, rows * cols, 0.0)
        weighted = (dot(q, k, 1, 1) * decay).astype(LOW)
        grads = (dot(da, v, 1, 1) * decay).astype(LOW)
        held = st_ref[0, h]
        after = later[h]
        after_low = after.astype(LOW)
        dq = dot(grads, k) + entry * dot(da, held, 1, 1)
        dk = dot(grads, q, 0, 0) + tail * dot(v, after_low, 1, 1)
        dv = dot(weighted, da, 0, 0) + tail * dot(k, after_low)
        qe = (q.astype(WIDE) * entry).astype(LOW)
        later[h] = carry * jnp.exp(jnp.full((1, 1), -rate * chunk, WIDE)) * after + dot(qe, da, 0, 0)
        dz_ref[:, base : base + hd] = (dq * slope(zq)).astype(LOW)
        dz_ref[:, base + hd : base + 2 * hd] = (dk * slope(zk)).astype(LOW)
        dz_ref[:, base + 2 * hd : base + 3 * hd] = (dv * slope(zv)).astype(LOW)
        dz_ref[:, base + 3 * hd : base + 4 * hd] = (dj * an * slope(zu)).astype(LOW)


def empty(shape, kind):
    return pl.pallas_call(
        lambda out: None,
        out_shape=jax.ShapeDtypeStruct(shape, kind),
        out_specs=pl.BlockSpec(memory_space=pl.ANY),
        name="empty",
    )()


def pack_kernel(seq, heads, hd, *refs):
    weights, glu, attn_out, glu_outs = refs[:4], refs[4:6], refs[6], refs[7:]
    for i in range(seq):
        for h in range(heads):
            for m, w in enumerate(weights):
                to, at = (h * 4 + m) * hd, (i * heads + h) * hd
                attn_out[i, :, to : to + hd] = w[:, at : at + hd]
        for w, out in zip(glu, glu_outs):
            n = out.shape[2]
            out[i] = w[:, i * n : (i + 1) * n]


def pack_columns(weights, glu, seq, heads, hd):
    r, kind = weights[0].shape[0], weights[0].dtype
    n = glu[0].shape[1] // seq
    return pl.pallas_call(
        functools.partial(pack_kernel, seq, heads, hd),
        out_shape=[jax.ShapeDtypeStruct((seq, r, heads * 4 * hd), kind)]
        + [jax.ShapeDtypeStruct((seq, r, n), kind)] * 2,
        compiler_params=pltpu.CompilerParams(vmem_limit_bytes=VMEM_BYTES),
        name="pack_columns",
    )(*weights, *glu)


def unpack_kernel(seq, heads, hd, attn, first, second, o_first, o_second, *o_attn):
    for i in range(seq):
        for h in range(heads):
            for m in range(4):
                at, to = (h * 4 + m) * hd, (i * heads + h) * hd
                o_attn[m][:, to : to + hd] = attn[i, :, at : at + hd].astype(WIDE)
        for ref, out in ((first, o_first), (second, o_second)):
            n = ref.shape[2]
            out[:, i * n : (i + 1) * n] = ref[i].astype(WIDE)


def unpack_columns(attn, first, second, heads, hd):
    seq, r = attn.shape[:2]
    shape = lambda n: jax.ShapeDtypeStruct((r, seq * n), WIDE)
    return pl.pallas_call(
        functools.partial(unpack_kernel, seq, heads, hd),
        out_shape=[shape(first.shape[2]), shape(second.shape[2])] + [shape(heads * hd)] * 4,
        compiler_params=pltpu.CompilerParams(vmem_limit_bytes=VMEM_BYTES),
        name="unpack_columns",
    )(attn, first, second)


class Net:
    def __init__(self, shape, send_sem, recv_sem, local_sem):
        self.seq, self.fsdp, self.inner = shape
        self.outer = self.fsdp // self.inner
        self.chips = self.seq // 2
        self.send_sem, self.recv_sem, self.local_sem = send_sem, recv_sem, local_sem
        self.used = 0
        self.locals = 0
        self.s, self.f = lax.axis_index("seq"), lax.axis_index("fsdp")
        self.chip, self.core = self.s // 2, self.s % 2
        self.o, self.i = self.f // self.inner, self.f % self.inner
        self.sent = []

    def seq_peers(self):
        for dx in range(self.chips):
            for dc in range(2):
                if dx or dc:
                    yield dx, dc, lax.rem(self.chip + dx, self.chips) * 2 + lax.rem(self.core + dc, 2)

    def at_seq(self, s):
        return (s, self.f)

    def at_inner(self, j):
        return (self.s, self.o * self.inner + lax.rem(self.i + j, self.inner))

    def at_outer(self, k):
        return (self.s, lax.rem(self.o + k, self.outer) * self.inner + self.i)

    def barrier(self):
        peers = [self.at_seq(s) for _, _, s in self.seq_peers()]
        peers += [self.at_inner(j) for j in range(1, self.inner)]
        peers += [self.at_outer(1), self.at_outer(self.outer - 1)]
        sem = pltpu.get_barrier_semaphore()
        for peer in peers:
            pl.semaphore_signal(sem, inc=1, device_id=peer, device_id_type=pl.DeviceIdType.MESH)
        pl.semaphore_wait(sem, len(peers))

    def send(self, src, dst, device):
        copy = pltpu.make_async_remote_copy(
            src_ref=src,
            dst_ref=dst,
            send_sem=self.send_sem.at[self.used],
            recv_sem=self.recv_sem.at[self.used],
            device_id=device,
            device_id_type=pl.DeviceIdType.MESH,
        )
        self.used += 1
        copy.start()
        self.sent.append(copy)
        return copy

    def copy(self, src, dst):
        copy = pltpu.make_async_copy(src, dst, self.local_sem.at[self.locals])
        self.locals += 1
        copy.start()
        return copy

    def left(self, copy):
        copy.wait_send()
        self.sent = [other for other in self.sent if other is not copy]

    def finish(self):
        for copy in self.sent:
            copy.wait_send()
        self.sent = []


def net_shape(mesh_seq, mesh_fsdp):
    return mesh_seq, mesh_fsdp, 2 if mesh_fsdp == 8 else 4


class Ring:
    def __init__(self, net, piece, full):
        self.net, self.piece, self.full = net, piece, full
        self.copies = [net.copy(piece, full.at[:, net.o, net.i])]
        self.at = 0
        self.coming = None
        self.side = []

    def step(self):
        net, full = self.net, self.full
        if self.at >= net.outer:
            return
        if self.coming is not None:
            self.coming.wait_recv()
        spot = full.at[:, lax.rem(net.o + net.outer - self.at, net.outer), net.i]
        src = self.piece if self.at == 0 else spot
        self.coming = None
        if self.at < net.outer - 1:
            self.coming = net.send(src, spot, net.at_outer(1))
        for j in range(1, net.inner):
            self.side.append(net.send(src, spot, net.at_inner(j)))
        self.at += 1

    def done(self):
        while self.at < self.net.outer:
            self.step()
        for copy in self.side:
            copy.wait_recv()
        for copy in self.copies:
            copy.wait()


class WideRing:
    def __init__(self, net, piece, full):
        self.net, self.full = net, full
        self.copies = [net.copy(piece, full.at[:, net.o, net.i])]
        self.side = [
            net.send(piece, full.at[:, net.o, net.i], net.at_inner(j)) for j in range(1, net.inner)
        ]
        self.at = 0
        self.coming = None

    def step(self):
        net, full = self.net, self.full
        if self.at >= net.outer:
            return
        if self.at == 0:
            for copy in self.side:
                copy.wait_recv()
            for copy in self.copies:
                copy.wait()
        else:
            self.coming.wait_recv()
        spot = full.at[:, lax.rem(net.o + net.outer - self.at, net.outer)]
        if self.at < net.outer - 1:
            self.coming = net.send(spot, spot, net.at_outer(1))
        self.at += 1

    def done(self):
        while self.at < self.net.outer:
            self.step()


def swap(net, blocks, got):
    own = net.copy(blocks.at[net.s], got.at[net.s])
    coming = [
        net.send(blocks.at[s], got.at[net.s], net.at_seq(s)) for _, _, s in net.seq_peers()
    ]
    return own, coming


def arrive(pair):
    own, coming = pair
    own.wait()
    for copy in coming:
        copy.wait_recv()


class Rows:
    def __init__(self, net, own, whole, start=0):
        t, each = own.shape[0], whole.shape[0] // net.seq
        self.net, self.whole = net, whole
        spot = lambda s: whole.at[pl.ds(pl.multiple_of(s * each + start, t), t)]
        self.spot = spot
        self.far = [
            net.send(own, spot(net.s), net.at_seq(lax.rem(net.chip + dx, net.chips) * 2 + net.core))
            for dx in range(1, net.chips)
        ]
        self.near = [net.send(own, spot(net.s), net.at_seq(net.chip * 2 + 1 - net.core))]
        self.own = net.copy(own, spot(net.s))

    def turn(self):
        net = self.net
        for dx, copy in zip(range(1, net.chips), self.far):
            copy.wait_recv()
            spot = self.spot(lax.rem(net.chip + net.chips - dx, net.chips) * 2 + net.core)
            self.near.append(net.send(spot, spot, net.at_seq(net.chip * 2 + 1 - net.core)))

    def done(self):
        for copy in self.near:
            copy.wait_recv()
        self.own.wait()


def gather_kernel(
    shape, heads, hd,
    rate_ref, attn_ref, first_ref, second_ref, out_ref, down_ref, n1_ref, seg_ref, count_ref, x_ref,
    attn_mid, first_mid, second_mid,
    full_attn, full_first, full_second, full_out, full_down,
    n1_all, z_all, a_all, states, mixed_ref, hsum_ref, n2_own, n2_all, core_in, chip_in,
    seg_all, count_all, ss_all,
    w_attn, w_out, au_all, state, stage, term, wide_tile, hsum_tile, x_tile, n2_tile, ss_in,
    seq_buf, in_buf, out_buf, send_sem, recv_sem, local_sem,
):
    net = Net(shape, send_sem, recv_sem, local_sem)
    length, width = n1_all.shape
    cols = z_all.shape[1]
    own_rows = x_ref.shape[0]
    wide = min(512, width)
    net.barrier()
    count = Total(net, count_ref, seq_buf, in_buf, out_buf)
    attn_swap = swap(net, attn_ref, attn_mid)
    seg_own = net.copy(seg_ref, seg_all.at[net.s])
    segs = [net.send(seg_ref, seg_all.at[net.s], net.at_seq(s)) for _, _, s in net.seq_peers()]
    first_swap = swap(net, first_ref, first_mid)
    second_swap = swap(net, second_ref, second_mid)
    rows = Rows(net, n1_ref, n1_all)
    arrive(attn_swap)
    count.step()
    ring_attn = Ring(net, attn_mid, full_attn)
    ring_out = Ring(net, out_ref, full_out)
    for _ in range(net.outer):
        ring_attn.step()
        ring_out.step()
        count.step()
    arrive(first_swap)
    arrive(second_swap)
    ring_first = Ring(net, first_mid, full_first)
    ring_second = Ring(net, second_mid, full_second)
    ring_first.step()
    ring_second.step()
    ring_down = WideRing(net, down_ref, full_down)
    rows.turn()
    queue = [ring_first, ring_second, ring_down] * (net.outer - 1) + [ring_down]

    def pump(times=1):
        for _ in range(min(times, len(queue))):
            queue.pop(0).step()

    seg_own.wait()
    for copy in segs:
        copy.wait_recv()
    ring_attn.done()
    load_attn = net.copy(full_attn, w_attn)
    rows.done()
    ring_out.done()
    load_out = net.copy(full_out, w_out)
    load_attn.wait()
    load_out.wait()

    state[...] = jnp.zeros_like(state)
    per = own_rows // CHUNK

    def seg_of(n):
        at = pl.ds(pl.multiple_of(n % per * CHUNK, CHUNK), CHUNK)
        return jnp.broadcast_to(seg_all[n // per, :, at].astype(WIDE), (8, CHUNK))

    def chunks(low, steps):
        def body(n1_chunk, z_ref, a_ref, st_ref):
            n = low + pl.program_id(0)

            def project(j, _):
                at = pl.ds(pl.multiple_of(j * wide, wide), wide)
                weight = w_attn[:, :, :, :, at].reshape(width, wide)
                z_ref[:, at] = dot(n1_chunk[...], weight)
                return 0

            lax.fori_loop(0, cols // wide, project, 0)
            au_rows = au_all.at[pl.ds(pl.multiple_of(n * CHUNK, CHUNK), CHUNK)]
            attend(
                heads, hd, n, rate_ref, seg_of(jnp.maximum(n - 1, 0)), seg_of(n), z_ref, au_rows,
                a_ref, ss_all.at[n], st_ref, state,
            )

        block = lambda n: pl.BlockSpec((CHUNK, n), lambda i: (low + i, 0))
        pltpu.emit_pipeline(
            body,
            grid=(steps,),
            in_specs=[block(width)],
            out_specs=[
                block(cols),
                block(heads * hd),
                pl.BlockSpec((1, heads, hd, hd), lambda i: (low + i, 0, 0, 0)),
            ],
        )(n1_all, z_all, a_all, states)

    total = length // CHUNK
    half = total // 2
    chunks(0, half)
    pump()
    chunks(half, total - half)
    near_ss = [net.send(ss_all, ss_in.at[net.s], net.at_seq(s)) for _, _, s in net.seq_peers()]
    pump()

    used = [None, None]
    turns = [0]

    def product(row, each):
        x = au_all[pl.ds(pl.multiple_of(row, CHUNK), CHUNK)]

        def one(j, _):
            at = pl.ds(pl.multiple_of(j * wide, wide), wide)
            weight = w_out[:, :, :, :, at].reshape(heads * hd, wide)
            each(at, dot(x, weight))
            return 0

        lax.fori_loop(0, width // wide, one, 0)

    def slot():
        i = turns[0] % 2
        turns[0] += 1
        if used[i] is not None:
            net.left(used[i])
        return i

    def row_of(chip, core, t):
        return (chip * 2 + core) * own_rows + t * CHUNK

    near = {}
    far = []

    def give(dx):
        chip = lax.rem(net.chip + dx, net.chips)
        for t in range(per):
            i = slot()

            def store(at, part, i=i):
                stage[i, :, at] = part.astype(LOW)

            product(row_of(chip, 1 - net.core, t), store)
            spot = core_in.at[dx, pl.ds(t * CHUNK, CHUNK)]
            used[i] = near[dx, t] = net.send(
                stage.at[i], spot, net.at_seq(net.chip * 2 + 1 - net.core)
            )

    def keep(dx, finish=None):
        chip = lax.rem(net.chip + dx, net.chips)
        for t in range(per):
            span = pl.ds(t * CHUNK, CHUNK)
            near[dx, t].wait_recv()
            loads = [net.copy(core_in.at[dx, span], term.at[0])]
            if dx == 0:
                loads.append(net.copy(x_ref.at[span], x_tile))
                for j, copies in enumerate(far):
                    copies[t].wait_recv()
                    loads.append(net.copy(chip_in.at[j, span], term.at[j + 1]))
            else:
                i = slot()
            for load in loads:
                load.wait()

            def store(at, part):
                add = part + term[0, :, at].astype(WIDE)
                if dx == 0:
                    for j in range(len(far)):
                        add = add + term[j + 1, :, at].astype(WIDE)
                    wide_tile[:, at] = add
                else:
                    stage[i, :, at] = add.astype(LOW)

            product(row_of(chip, net.core, t), store)
            if dx == 0:
                finish(t, span)
            else:
                used[i] = net.send(
                    stage.at[i], chip_in.at[dx - 1, span], net.at_seq(chip * 2 + net.core)
                )
                far[dx - 1].append(used[i])

    def finish(t, span):
        at = net.s * per + t
        squares = ss_in[0, at]
        for j in range(1, net.seq):
            squares = squares + ss_in[j, at]
        ra = lax.rsqrt(jnp.transpose(squares)[:, :1] / width + 1e-6)

        def add(j, squares):
            at = pl.ds(pl.multiple_of(j * wide, wide), wide)
            mixed = wide_tile[:, at] * ra
            wide_tile[:, at] = mixed
            hsum = x_tile[:, at].astype(WIDE) + mixed
            hsum_tile[:, at] = hsum
            return squares + jnp.sum(hsum * hsum, axis=1, keepdims=True)

        squares = lax.fori_loop(0, width // wide, add, jnp.zeros((CHUNK, 1), WIDE))
        r2 = lax.rsqrt(squares / width + 1e-6)

        def scale(j, _):
            at = pl.ds(pl.multiple_of(j * wide, wide), wide)
            n2_tile[:, at] = (hsum_tile[:, at] * r2).astype(LOW)
            return 0

        lax.fori_loop(0, width // wide, scale, 0)
        outs = [
            net.copy(wide_tile, mixed_ref.at[span]),
            net.copy(hsum_tile, hsum_ref.at[span]),
            net.copy(n2_tile, n2_own.at[span]),
        ]
        for out in outs:
            out.wait()

    for dx in range(1, net.chips):
        far.append([])
        give(dx)
        keep(dx)
    pump()
    give(0)
    pump(2)
    for copy in near_ss:
        copy.wait_recv()
    for copy in near_ss:
        net.left(copy)
    ss_in[net.s] = ss_all[...]
    keep(0, finish)
    rows = Rows(net, n2_own, n2_all)
    pump(3)
    rows.turn()
    pump(len(queue))
    count_all[...] = count.done()
    for ring in (ring_first, ring_second, ring_down):
        ring.done()
    rows.done()
    total_ss = ss_in[0]
    for j in range(1, net.seq):
        total_ss = total_ss + ss_in[j]
    ss_all[...] = total_ss
    net.finish()


HBM = pl.BlockSpec(memory_space=pl.ANY)


def gather_all(shape, heads, hd, rates, attn, first, second, w_out, w_down, n1, seg, count, x):
    seq, fsdp, inner = shape
    outer = fsdp // inner
    chips = seq // 2
    own_rows, width = n1.shape
    length = own_rows * seq
    cols = attn.shape[2]
    chunks = length // CHUNK
    like = lambda v, lead: jax.ShapeDtypeStruct(lead + v.shape[-2:], v.dtype)
    ring = lambda v: like(v, (v.shape[0], outer, inner))
    low = lambda *dims: jax.ShapeDtypeStruct(dims, LOW)
    wide = lambda *dims: jax.ShapeDtypeStruct(dims, WIDE)
    outs = [like(v, (seq,)) for v in (attn, first, second)]
    outs += [ring(v) for v in (attn, first, second, w_out, w_down)]
    outs += [low(length, width), wide(length, cols), wide(length, heads * hd)]
    outs += [low(chunks, heads, hd, hd), wide(own_rows, width), wide(own_rows, width)]
    outs += [low(own_rows, width), low(length, width)]
    outs += [low(chips, own_rows, width), low(max(chips - 1, 1), own_rows, width)]
    in_hbm = len(outs)
    outs += [jax.ShapeDtypeStruct((seq,) + seg.shape, seg.dtype), wide(8, 128)]
    outs += [wide(chunks, 8, CHUNK)]
    copies = 7 * seq + 5 * (outer * inner + outer) + total_copies(shape) + 2 * chunks + 4 * seq
    in_vmem = pl.BlockSpec(memory_space=pltpu.VMEM)
    smem = pl.BlockSpec(memory_space=pltpu.SMEM)
    got = pl.pallas_call(
        functools.partial(gather_kernel, shape, heads, hd),
        in_specs=[smem] + [HBM] * 7 + [in_vmem, HBM],
        out_specs=[HBM] * in_hbm + [in_vmem] * 3,
        out_shape=outs,
        scratch_shapes=[
            pltpu.VMEM(ring(attn).shape, LOW),
            pltpu.VMEM(ring(w_out).shape, LOW),
            pltpu.VMEM((length, heads * hd), LOW),
            pltpu.VMEM((heads, hd, hd), WIDE),
            pltpu.VMEM((2, CHUNK, width), LOW),
            pltpu.VMEM((chips, CHUNK, width), LOW),
            pltpu.VMEM((CHUNK, width), WIDE),
            pltpu.VMEM((CHUNK, width), WIDE),
            pltpu.VMEM((CHUNK, width), LOW),
            pltpu.VMEM((CHUNK, width), LOW),
            pltpu.VMEM((seq, chunks, 8, CHUNK), WIDE),
        ]
        + total_scratch(shape)
        + [
            pltpu.SemaphoreType.DMA((copies,)),
            pltpu.SemaphoreType.DMA((copies,)),
            pltpu.SemaphoreType.DMA((24 + 6 * chunks,)),
        ],
        compiler_params=pltpu.CompilerParams(
            collective_id=0, has_side_effects=True, vmem_limit_bytes=VMEM_BYTES
        ),
        name="gather_all",
    )(rates, attn, first, second, w_out, w_down, n1, seg, count, x)
    flat = lambda v: v.reshape(-1, v.shape[-1])
    squares = got[in_hbm + 2][:, 0].reshape(length, 1)
    return [flat(v) for v in got[3:8]] + list(got[8:14]) + [got[15], got[in_hbm], got[in_hbm + 1], squares]


class Total:
    def __init__(self, net, own, seq_buf, in_buf, out_buf):
        self.net, self.bufs, self.stage = net, (seq_buf, in_buf, out_buf), 0
        self.coming = self.share(seq_buf, net.s, own[...], [net.at_seq(s) for _, _, s in net.seq_peers()])

    def share(self, buf, at, value, devices):
        buf[at] = value
        return [self.net.send(buf.at[at], buf.at[at], device) for device in devices]

    def gathered(self, buf):
        for copy in self.coming:
            copy.wait_recv()
        total = buf[0]
        for j in range(1, buf.shape[0]):
            total = total + buf[j]
        return total

    def step(self):
        net, (seq_buf, in_buf, out_buf) = self.net, self.bufs
        if self.stage == 0:
            peers = [net.at_inner(j) for j in range(1, net.inner)]
            self.coming = self.share(in_buf, net.i, self.gathered(seq_buf), peers)
        elif self.stage == 1:
            self.coming = self.share(out_buf, net.o, self.gathered(in_buf), [net.at_outer(1)])
        elif self.stage < net.outer:
            self.coming[-1].wait_recv()
            at = lax.rem(net.o + net.outer - self.stage + 1, net.outer)
            self.coming = [net.send(out_buf.at[at], out_buf.at[at], net.at_outer(1))]
        self.stage += 1

    def done(self):
        while self.stage < self.net.outer:
            self.step()
        return self.gathered(self.bufs[2])


def total_scratch(shape):
    seq, fsdp, inner = shape
    return [pltpu.VMEM((n, 8, 128), WIDE) for n in (seq, inner, fsdp // inner)]


def total_copies(shape):
    seq, fsdp, inner = shape
    return seq + inner + fsdp // inner


class Sum:
    def __init__(self, net, g, side, ring, send, load):
        self.net, self.g, self.side_ref, self.ring_ref = net, g, side, ring
        self.send_buf, self.load = send, load
        self.side = []
        self.ring = []
        for k in range(net.outer):
            o = self.spot(k)
            now = []
            for j in range(1, net.inner):
                to = lax.rem(net.i + j, net.inner)
                now.append(net.send(g.at[:, o, to], side.at[j - 1, :, o], net.at_inner(j)))
            self.side.append(now)
        self.at = 0

    def spot(self, k):
        return lax.rem(self.net.o + 2 * self.net.outer - 1 - k, self.net.outer)

    def step(self, final):
        net, k = self.net, self.at
        self.at += 1
        o = self.spot(k)
        terms = self.load
        loads = [net.copy(self.g.at[:, o, net.i], terms.at[0])]
        for j, copy in enumerate(self.side[k]):
            copy.wait_recv()
            loads.append(net.copy(self.side_ref.at[j, :, o], terms.at[j + 1]))
        count = net.inner
        if k > 0:
            self.ring[k - 1].wait_recv()
            loads.append(net.copy(self.ring_ref.at[k - 1], terms.at[count]))
            count += 1
        if k >= 2:
            net.left(self.ring[k - 2])
        for load in loads:
            load.wait()

        def one(i, _):
            total = terms[0, i].astype(WIDE)
            for j in range(1, count):
                total = total + terms[j, i].astype(WIDE)
            if k < net.outer - 1:
                self.send_buf[k % 2, i] = total.astype(LOW)
            else:
                final(i, total)
            return 0

        lax.fori_loop(0, terms.shape[1], one, 0)
        if k < net.outer - 1:
            self.ring.append(net.send(self.send_buf.at[k % 2], self.ring_ref.at[k], net.at_outer(1)))


GRADS = ("down", "first", "second", "attn", "out")
SPLIT = ("first", "second", "attn")
LOADS = ("down", "first", "attn", "out")


def back_kernel(
    shape, heads, hd,
    rate_ref, bounds_ref, segc, segr, z, a, dh, ra, mean, states, w_out, w_attn, n1, loss_ref,
    g_down, g_first, g_second,
    dn1_ref, o_down, o_out, o_loss, got_first, got_second, got_attn, g_attn,
    side_down, side_first, side_second, side_attn, side_out,
    ring_down, ring_first, ring_second, ring_attn, ring_out,
    core_in, chip_in,
    dz_all, later, dj, o_chunk, out_acc, g_out, stage, term, wide_tile,
    *rest
):
    it = iter(rest)
    take = lambda names: {name: next(it) for name in names}
    sends, loads = take(GRADS), take(LOADS)
    loads["second"] = loads["first"]
    total_bufs = [next(it) for _ in range(3)]
    send_sem, recv_sem, local_sem = (next(it) for _ in range(3))
    net = Net(shape, send_sem, recv_sem, local_sem)
    grads = dict(down=g_down, first=g_first, second=g_second, attn=g_attn, out=g_out)
    sides = dict(down=side_down, first=side_first, second=side_second, attn=side_attn, out=side_out)
    rings = dict(down=ring_down, first=ring_first, second=ring_second, attn=ring_attn, out=ring_out)
    gots = dict(first=got_first, second=got_second, attn=got_attn)
    owned = dict(down=o_down, out=o_out)
    length, cols = dz_all.shape
    width = dh.shape[1]
    count = length // CHUNK
    wide = min(512, width)

    net.barrier()
    sums, swaps, queue = {}, {}, []
    loss = Total(net, loss_ref, *total_bufs)

    def begin(name):
        sums[name] = Sum(net, grads[name], sides[name], rings[name], sends[name], loads[name])
        queue.extend([name] * net.outer)

    def pump(times=1):
        for _ in range(min(times, len(queue))):
            name = queue.pop(0)

            def final(i, rows):
                if name in owned:
                    owned[name][...] = rows
                else:
                    totals[i] = rows.astype(LOW)

            totals = sends[name].at[(net.outer - 1) % 2]
            sums[name].step(final)
            if name in SPLIT and sums[name].at == net.outer:
                swaps[name] = swap(net, totals, gots[name])

    loss.step()
    for name in ("down", "first", "second"):
        begin(name)

    later[...] = jnp.zeros_like(later)
    out_acc[...] = jnp.zeros_like(out_acc)

    def chunks(top, steps):
        def body(segc_ref, segr_ref, z_ref, a_ref, dh_ref, ra_ref, m_ref, st_ref):
            n = top - pl.program_id(0)
            dj[...] = dot(dh_ref[...], w_out[...], 1, 1)
            rows = pl.ds(pl.multiple_of(n * CHUNK, CHUNK), CHUNK)
            attend_back(
                heads, hd, n, rate_ref, bounds_ref, segc_ref, segr_ref, z_ref, a_ref, dj, ra_ref,
                m_ref, st_ref, dz_all.at[rows], o_chunk, later,
            )

            def add(j, _):
                at = pl.ds(pl.multiple_of(j * wide, wide), wide)
                out_acc[:, at] += dot(o_chunk[...], dh_ref[:, at], 0, 0)
                return 0

            lax.fori_loop(0, width // wide, add, 0)

        block = lambda n: pl.BlockSpec((CHUNK, n), lambda i: (top - i, 0))
        pltpu.emit_pipeline(
            body,
            grid=(steps,),
            in_specs=[
                block(1),
                pl.BlockSpec((1, CHUNK), lambda i: (0, top - i)),
                block(cols),
                block(heads * hd),
                block(width),
                block(1),
                block(1),
                pl.BlockSpec((1, heads, hd, hd), lambda i: (top - i, 0, 0, 0)),
            ],
        )(segc, segr, z, a, dh, ra, mean, states)

    half = count // 2
    chunks(count - 1, half)
    loss.step()
    pump()
    chunks(count - 1 - half, count - half)
    loss.step()
    pump()

    own_rows = dn1_ref.shape[0]
    tile = min(256, own_rows)
    used = [None, None]
    turns = [0]

    def product(row, each):
        x = dz_all[pl.ds(pl.multiple_of(row, tile), tile)]

        def one(j, _):
            at = pl.ds(pl.multiple_of(j * wide, wide), wide)
            each(at, dot(x, w_attn[at, :], 1, 1))
            return 0

        lax.fori_loop(0, width // wide, one, 0)

    def slot():
        i = turns[0] % 2
        turns[0] += 1
        if used[i] is not None:
            net.left(used[i])
        return i

    def row_of(chip, core, t):
        return (chip * 2 + core) * own_rows + t * tile

    near = {}
    far = []

    def give(dx):
        chip = lax.rem(net.chip + dx, net.chips)
        for t in range(own_rows // tile):
            i = slot()

            def store(at, part, i=i):
                stage[i, :, at] = part.astype(LOW)

            product(row_of(chip, 1 - net.core, t), store)
            spot = core_in.at[dx, pl.ds(t * tile, tile)]
            used[i] = near[dx, t] = net.send(
                stage.at[i], spot, net.at_seq(net.chip * 2 + 1 - net.core)
            )

    def keep(dx):
        chip = lax.rem(net.chip + dx, net.chips)
        for t in range(own_rows // tile):
            span = pl.ds(t * tile, tile)
            near[dx, t].wait_recv()
            loads = [net.copy(core_in.at[dx, span], term.at[0])]
            if dx == 0:
                for j, copies in enumerate(far):
                    copies[t].wait_recv()
                    loads.append(net.copy(chip_in.at[j, span], term.at[j + 1]))
            else:
                i = slot()
            for load in loads:
                load.wait()

            def store(at, part):
                total = part
                for j in range(len(loads)):
                    total = total + term[j, :, at].astype(WIDE)
                if dx == 0:
                    wide_tile[:, at] = total
                else:
                    stage[i, :, at] = total.astype(LOW)

            product(row_of(chip, net.core, t), store)
            if dx == 0:
                net.copy(wide_tile, dn1_ref.at[span]).wait()
            else:
                used[i] = net.send(
                    stage.at[i], chip_in.at[dx - 1, span], net.at_seq(chip * 2 + net.core)
                )
                far[dx - 1].append(used[i])

    for dx in range(1, net.chips):
        far.append([])
        give(dx)
        keep(dx)
    pump()

    parts = 2
    spread = net.outer // parts
    features = width // net.seq // parts

    def grad_body(n1_ref, g_ref):
        for j in range(cols // wide):
            at = slice(j * wide, (j + 1) * wide)
            got = dot(n1_ref[...], dz_all[:, at], 0, 0).astype(LOW)
            g_ref[:, :, :, :, at] = got.reshape(g_ref.shape[:-1] + (wide,))

    pltpu.emit_pipeline(
        grad_body,
        grid=(net.seq, parts),
        in_specs=[pl.BlockSpec((length, features), lambda i, j: (0, i * parts + j))],
        out_specs=[
            pl.BlockSpec((1, spread) + g_attn.shape[2:], lambda i, j: (i, j, 0, 0, 0)),
        ],
    )(n1, g_attn)
    begin("attn")
    for j in range(width // wide):
        at = slice(j * wide, (j + 1) * wide)
        g_out[:, :, :, :, at] = out_acc[:, at].astype(LOW).reshape(g_out.shape[:-1] + (wide,))
    begin("out")
    pump(2)
    give(0)
    pump()
    keep(0)
    o_loss[...] = loss.done()
    pump(len(queue))
    for name in SPLIT:
        arrive(swaps[name])
    net.finish()


def back_all(shape, heads, hd, rates, bounds, seg, z, a, dh, ra, mean, states, w_out, w_attn, n1, loss, grads):
    seq, fsdp, inner = shape
    outer = fsdp // inner
    length, width = dh.shape
    cols = z.shape[1]
    own_rows = length // seq
    chips = seq // 2
    tile = min(256, own_rows)
    lead = {"down": 1, "out": 1, "first": seq, "second": seq, "attn": seq}
    blocks = [
        g.reshape(lead[n], outer, inner, g.shape[0] // (lead[n] * fsdp), g.shape[1])
        for n, g in zip(GRADS, grads)
    ]
    size = {n: (g.shape[0], g.shape[3], g.shape[4]) for n, g in zip(GRADS, blocks)}
    size["attn"] = (seq, width // (seq * fsdp), cols)
    size["out"] = (1, width // (seq * fsdp), width)
    whole = lambda n: (size[n][0], outer, inner) + size[n][1:]
    low = lambda dims: jax.ShapeDtypeStruct(dims, LOW)
    row = lambda n: jax.ShapeDtypeStruct(size[n][1:], WIDE)
    outs = [jax.ShapeDtypeStruct((own_rows, width), WIDE), row("down"), row("out")]
    outs += [jax.ShapeDtypeStruct((8, 128), WIDE)]
    outs += [low(size[n]) for n in SPLIT] + [low(whole("attn"))]
    outs += [low((inner - 1, size[n][0], outer) + size[n][1:]) for n in GRADS]
    outs += [low((outer - 1,) + size[n]) for n in GRADS]
    outs += [low((chips, own_rows, width)), low((max(chips - 1, 1), own_rows, width))]
    in_vmem = pl.BlockSpec(memory_space=pltpu.VMEM)
    smem = pl.BlockSpec(memory_space=pltpu.SMEM)
    scratch = [
        pltpu.VMEM((length, cols), LOW),
        pltpu.VMEM((heads, hd, hd), WIDE),
        pltpu.VMEM((CHUNK, heads * hd), WIDE),
        pltpu.VMEM((CHUNK, heads * hd), LOW),
        pltpu.VMEM((heads * hd, width), WIDE),
        pltpu.VMEM(whole("out"), LOW),
        pltpu.VMEM((2, tile, width), LOW),
        pltpu.VMEM((chips, tile, width), LOW),
        pltpu.VMEM((tile, width), WIDE),
    ]
    scratch += [pltpu.VMEM((2,) + size[n], LOW) for n in GRADS]
    scratch += [pltpu.VMEM((inner + 1,) + size[n], LOW) for n in LOADS]
    scratch += total_scratch(shape)
    copies = 5 * (outer * inner + outer) + 3 * seq + total_copies(shape) + 2 * length // tile
    scratch += [
        pltpu.SemaphoreType.DMA((copies,)),
        pltpu.SemaphoreType.DMA((copies,)),
        pltpu.SemaphoreType.DMA((5 * outer * (inner + 1) + 3 + 4 * length // tile,)),
    ]
    return pl.pallas_call(
        functools.partial(back_kernel, shape, heads, hd),
        in_specs=[smem, smem] + [HBM] * 8 + [in_vmem] * 2 + [HBM, in_vmem] + [HBM] * 3,
        out_specs=[HBM] + [in_vmem] * 3 + [HBM] * (len(outs) - 4),
        out_shape=outs,
        scratch_shapes=scratch,
        compiler_params=pltpu.CompilerParams(
            collective_id=1, has_side_effects=True, vmem_limit_bytes=VMEM_BYTES
        ),
        name="back_all",
    )(
        rates, bounds, seg.reshape(length, 1), seg.reshape(1, length), z, a, dh, ra, mean, states,
        w_out, w_attn, n1, loss, *blocks
    )[:7]


def spans(n, step=512):
    return [slice(at, min(at + step, n)) for at in range(0, n, step)]


def glu_kernel(
    shape,
    n2_all, w_first, w_second, w_down, hsum_ref, teacher_ref, keep_ref, scale_ref, mixed_ref,
    layer_out, g_down, g_first, g_second, dh_ref, dh_all, dy_all, dy_own, dh_own,
    core_y, chip_y, core_n, chip_n,
    loss_ref, mean_all,
    one_all, two_all, p_all, dy_wide, stage, term, wide_tile, hsum_tile, mixed_tile, low_tile, sent_tile,
    send_sem, recv_sem, local_sem,
):
    net = Net(shape, send_sem, recv_sem, local_sem)
    width = n2_all.shape[1]
    ffs = p_all.shape[1]
    own_rows = hsum_ref.shape[0]
    per = own_rows // CHUNK
    wide = min(512, width)
    blocks = width // wide
    net.barrier()

    def rows_at(n):
        return pl.ds(pl.multiple_of(n * CHUNK, CHUNK), CHUNK)

    def of_chip(dx):
        return lax.rem(net.chip + dx, net.chips)

    def tiles(dx, src, body):
        base = of_chip(dx) * 2 * per
        pltpu.emit_pipeline(
            lambda ref: body(base + pl.program_id(0), ref),
            grid=(2 * per,),
            in_specs=[pl.BlockSpec((CHUNK, width), lambda i: (base + i, 0))],
        )(src)

    def columns(each):
        def one(j, _):
            each(pl.ds(pl.multiple_of(j * wide, wide), wide))
            return 0

        lax.fori_loop(0, blocks, one, 0)

    used = [None, None]
    turns = [0]

    def slot():
        i = turns[0] % 2
        turns[0] += 1
        if used[i] is not None:
            net.left(used[i])
        return i

    class Exchange:
        def __init__(self, product, core_in, chip_in):
            self.product, self.core_in, self.chip_in = product, core_in, chip_in
            self.near, self.far = {}, {}

        def give(self, dx):
            for t in range(per):
                i = slot()
                rows = rows_at((of_chip(dx) * 2 + 1 - net.core) * per + t)

                def store(at):
                    stage[i, :, at] = self.product(rows, at).astype(LOW)

                columns(store)
                used[i] = self.near[dx, t] = net.send(
                    stage.at[i],
                    self.core_in.at[dx, pl.ds(t * CHUNK, CHUNK)],
                    net.at_seq(net.chip * 2 + 1 - net.core),
                )

        def keep(self, dx, finish=None):
            for t in range(per):
                span = pl.ds(t * CHUNK, CHUNK)
                rows = rows_at((of_chip(dx) * 2 + net.core) * per + t)
                self.near[dx, t].wait_recv()
                loads = [net.copy(self.core_in.at[dx, span], term.at[0])]
                if dx == 0:
                    for j in range(1, net.chips):
                        self.far[j, t].wait_recv()
                        loads.append(net.copy(self.chip_in.at[j - 1, span], term.at[j]))
                    loads.append(net.copy(hsum_ref.at[span], hsum_tile))
                else:
                    i = slot()
                for load in loads:
                    load.wait()

                def store(at):
                    total = self.product(rows, at) + term[0, :, at].astype(WIDE)
                    if dx == 0:
                        for j in range(1, net.chips):
                            total = total + term[j, :, at].astype(WIDE)
                        wide_tile[:, at] = total
                    else:
                        stage[i, :, at] = total.astype(LOW)

                columns(store)
                if dx == 0:
                    finish(t, span)
                else:
                    used[i] = self.far[dx, t] = net.send(
                        stage.at[i],
                        self.chip_in.at[dx - 1, span],
                        net.at_seq(of_chip(dx) * 2 + net.core),
                    )

    def hidden(n, n2):
        rows = rows_at(n)
        for b in spans(ffs):
            one = dot(n2[...], w_first[:, b])
            two = dot(n2[...], w_second[:, b])
            one_all[rows, b] = one.astype(LOW)
            two_all[rows, b] = two.astype(LOW)
            p_all[rows, b] = (one * two).astype(LOW)

    y_sum = Exchange(lambda rows, at: dot(p_all[rows, :], w_down[:, at]), core_y, chip_y)
    for dx in range(1, net.chips):
        tiles(dx, n2_all, hidden)
        y_sum.give(dx)
        y_sum.keep(dx)
    tiles(0, n2_all, hidden)
    y_sum.give(0)

    loss_ref[...] = jnp.zeros_like(loss_ref)
    dy_rows = []

    def finish_y(t, span):
        net.copy(teacher_ref.at[span], sent_tile).wait()
        keep = keep_ref[span, :]
        scale = scale_ref[:1, :1] * keep

        def one(j, squares):
            at = pl.ds(pl.multiple_of(j * wide, wide), wide)
            y = hsum_tile[:, at] + wide_tile[:, at]
            low_tile[:, at] = y.astype(LOW)
            error = y - sent_tile[:, at].astype(WIDE)
            dy = scale * error
            dy_wide[span, at] = dy
            stage[1, :, at] = dy.astype(LOW)
            return squares + jnp.sum(keep * error * error, axis=1, keepdims=True)

        squares = lax.fori_loop(0, blocks, one, jnp.zeros((CHUNK, 1), WIDE))
        loss_ref[...] += jnp.broadcast_to(jnp.sum(squares, axis=0, keepdims=True), (8, 128))
        outs = [
            net.copy(low_tile, layer_out.at[span]),
            net.copy(stage.at[1], dy_own.at[span]),
        ]
        for out in outs:
            out.wait()
        dy_rows.append(Rows(net, dy_own.at[span], dy_all, t * CHUNK))

    def free_stage():
        for i in range(2):
            if used[i] is not None:
                net.left(used[i])
            used[i] = None

    free_stage()
    y_sum.keep(0, finish_y)

    def slopes(n, dy):
        rows = rows_at(n)
        for b in spans(ffs):
            dp = dot(dy[...], w_down[b, :], 1, 1)
            one = one_all[rows, b].astype(WIDE)
            two = two_all[rows, b].astype(WIDE)
            one_all[rows, b] = (dp * two).astype(LOW)
            two_all[rows, b] = (dp * one).astype(LOW)

    n_sum = Exchange(
        lambda rows, at: dot(one_all[rows, :], w_first[at, :], 1, 1)
        + dot(two_all[rows, :], w_second[at, :], 1, 1),
        core_n,
        chip_n,
    )
    for rows in dy_rows:
        rows.near[0].wait_recv()
        rows.near = rows.near[1:]
        rows.own.wait()
    tiles(0, dy_all, slopes)
    n_sum.give(0)
    for rows in dy_rows:
        rows.turn()
    for rows in dy_rows:
        for copy in rows.near:
            copy.wait_recv()
    for dx in range(1, net.chips):
        tiles(dx, dy_all, slopes)
        n_sum.give(dx)
        n_sum.keep(dx)

    length = p_all.shape[0]
    step = 256

    def grad_down(dy, out):
        for b in spans(ffs):
            out[b, :] = dot(p_all[:, b], dy[...], 0, 0).astype(LOW)

    pltpu.emit_pipeline(
        grad_down,
        grid=(width // step,),
        in_specs=[pl.BlockSpec((length, step), lambda i: (0, i))],
        out_specs=[pl.BlockSpec((ffs, step), lambda i: (0, i))],
    )(dy_all, g_down)

    def grad_columns(held, target):
        def body(n2, out):
            for b in spans(ffs):
                out[:, b] = dot(n2[...], held[:, b], 0, 0).astype(LOW)

        pltpu.emit_pipeline(
            body,
            grid=(width // step,),
            in_specs=[pl.BlockSpec((length, step), lambda i: (0, i))],
            out_specs=[pl.BlockSpec((step, ffs), lambda i: (i, 0))],
        )(n2_all, target)

    grad_columns(one_all, g_first)
    dh_rows = []
    means = []

    def finish_n(t, span):
        net.copy(mixed_ref.at[span], mixed_tile).wait()

        def add(j, sums):
            at = pl.ds(pl.multiple_of(j * wide, wide), wide)
            hsum = hsum_tile[:, at]
            return (
                sums[0] + jnp.sum(hsum * hsum, axis=1, keepdims=True),
                sums[1] + jnp.sum(hsum * wide_tile[:, at], axis=1, keepdims=True),
            )

        zero = jnp.zeros((CHUNK, 1), WIDE)
        squares, cross = lax.fori_loop(0, blocks, add, (zero, zero))
        r2 = lax.rsqrt(squares / width + 1e-6)
        mean = r2 * cross / width

        def one(j, total):
            at = pl.ds(pl.multiple_of(j * wide, wide), wide)
            m2 = hsum_tile[:, at] * r2
            dh = dy_wide[span, at] + r2 * (wide_tile[:, at] - m2 * mean)
            wide_tile[:, at] = dh
            low = dh.astype(LOW)
            low_tile[:, at] = low
            return total + jnp.sum(low.astype(WIDE) * mixed_tile[:, at], axis=1, keepdims=True)

        total = lax.fori_loop(0, blocks, one, zero) / width
        at = net.s * per + t
        mean_all[at] = jnp.transpose(jnp.broadcast_to(total, (CHUNK, 128)))[:8]
        for _, _, s in net.seq_peers():
            means.append(net.send(mean_all.at[at], mean_all.at[at], net.at_seq(s)))
        outs = [net.copy(wide_tile, dh_ref.at[span]), net.copy(low_tile, dh_own.at[span])]
        for out in outs:
            out.wait()
        dh_rows.append(Rows(net, dh_own.at[span], dh_all, t * CHUNK))

    n_sum.keep(0, finish_n)
    grad_columns(two_all, g_second)
    for rows in dh_rows:
        rows.turn()
    for rows in dh_rows:
        rows.done()
    for copy in means:
        copy.wait_recv()
    net.finish()


def glu_all(shape, n2_all, w_first, w_second, w_down, hsum, teacher, keep, scale, mixed):
    seq, fsdp, inner = shape
    length, width = n2_all.shape
    ffs = w_first.shape[1]
    own_rows = length // seq
    chips = seq // 2
    chunks = length // CHUNK
    low = lambda *dims: jax.ShapeDtypeStruct(dims, LOW)
    wide = lambda *dims: jax.ShapeDtypeStruct(dims, WIDE)
    outs = [low(own_rows, width), low(ffs, width), low(width, ffs), low(width, ffs)]
    outs += [wide(own_rows, width), low(length, width), low(length, width)]
    outs += [low(own_rows, width)] * 2
    outs += [low(chips, own_rows, width), low(max(chips - 1, 1), own_rows, width)] * 2
    in_hbm = len(outs)
    outs += [wide(8, 128), wide(chunks, 8, CHUNK)]
    in_vmem = pl.BlockSpec(memory_space=pltpu.VMEM)
    copies = 16 * chunks + 16 * seq
    return pl.pallas_call(
        functools.partial(glu_kernel, shape),
        in_specs=[HBM] + [in_vmem] * 3 + [HBM] * 2 + [in_vmem] * 2 + [HBM],
        out_specs=[HBM] * in_hbm + [in_vmem] * 2,
        out_shape=outs,
        scratch_shapes=[pltpu.VMEM((length, ffs), LOW)] * 3
        + [
            pltpu.VMEM((own_rows, width), WIDE),
            pltpu.VMEM((2, CHUNK, width), LOW),
            pltpu.VMEM((chips, CHUNK, width), LOW),
            pltpu.VMEM((CHUNK, width), WIDE),
            pltpu.VMEM((CHUNK, width), WIDE),
            pltpu.VMEM((CHUNK, width), WIDE),
            pltpu.VMEM((CHUNK, width), LOW),
            pltpu.VMEM((CHUNK, width), LOW),
            pltpu.SemaphoreType.DMA((copies,)),
            pltpu.SemaphoreType.DMA((copies,)),
            pltpu.SemaphoreType.DMA((16 * chunks,)),
        ],
        compiler_params=pltpu.CompilerParams(
            collective_id=2, has_side_effects=True, vmem_limit_bytes=VMEM_BYTES
        ),
        name="glu_all",
    )(n2_all, w_first, w_second, w_down, hsum, teacher, keep, scale, mixed)


def on_device(
    inputs,
    teacher,
    segment_ids,
    valid,
    decay_rate,
    w_query,
    w_key,
    w_value,
    w_gate,
    w_out,
    w_first,
    w_second,
    w_down,
):
    seq, fsdp = lax.axis_size("seq"), lax.axis_size("fsdp")
    batch, block_len, width = inputs.shape
    assert batch == 1
    heads_all = decay_rate.shape[0]
    hd = width // heads_all
    heads = heads_all // seq
    own_rows = w_query.shape[0]
    ff = w_first.shape[1]
    ffs = ff // seq
    cols = heads * 4 * hd

    shape = net_shape(seq, fsdp)
    keep = valid.astype(WIDE).reshape(block_len, 1)
    spread = lambda v: jnp.broadcast_to(v, (8, 128))

    attn_own, first_own, second_own = pack_columns(
        (w_query, w_key, w_value, w_gate), (w_first, w_second), seq, heads, hd
    )
    x32 = inputs.reshape(block_len, width).astype(WIDE)
    r1 = lax.rsqrt(jnp.mean(x32 * x32, axis=-1, keepdims=True) + 1e-6)
    n1 = x32 * r1
    rates = lax.dynamic_slice_in_dim(decay_rate, lax.axis_index("seq") * heads, heads, 0)
    (
        full_attn, full_first, full_second, full_out, full_down, n1_all, z, a, states, mixed_out,
        hsum, n2_all, seg, count, squares,
    ) = gather_all(
        shape,
        heads,
        hd,
        rates,
        attn_own,
        first_own,
        second_own,
        w_out[None],
        w_down[None],
        n1.astype(LOW),
        segment_ids.reshape(1, block_len),
        spread(jnp.sum(keep)),
        inputs.reshape(block_len, width),
    )
    seg = seg.reshape(seq * block_len)
    length = seg.shape[0]
    count = count[:1, :1]
    bounds = jnp.concatenate([jnp.full((1,), -1, jnp.int32), seg[CHUNK - 1 :: CHUNK]])
    ra_all = lax.rsqrt(squares / width + 1e-6)

    tokens = block_len * seq * fsdp
    layer_out, grad_down, grad_first, grad_second, dh, dh_all, *_, loss_own, means = glu_all(
        shape,
        n2_all,
        full_first,
        full_second,
        full_down,
        hsum,
        teacher.reshape(block_len, width),
        keep,
        spread(tokens / count),
        mixed_out,
    )
    layer_out = layer_out.reshape(1, block_len, width)
    mean_all = means[:, 0].reshape(length, 1)

    dn1, share_down, share_out, loss, got_first, got_second, got_attn = back_all(
        shape, heads, hd, rates, bounds, seg, z, a, dh_all, ra_all, mean_all, states, full_out,
        full_attn, n1_all, loss_own,
        (grad_down, grad_first, grad_second),
    )
    input_grad = dh + r1 * (dn1 - n1 * jnp.mean(dn1 * n1, axis=-1, keepdims=True))
    loss = loss[0, 0] / (width * count)
    share_first, share_second, *share_attn = unpack_columns(
        got_attn, got_first, got_second, heads, hd
    )

    return (
        layer_out,
        loss.reshape(()),
        input_grad.reshape(1, block_len, width),
        share_attn[0],
        share_attn[1],
        share_attn[2],
        share_attn[3],
        share_out,
        share_first,
        share_second,
        share_down,
    )


def solution(mesh):
    rows = P(("seq", "fsdp"), None)
    tokens = P("fsdp", "seq", None)
    return jax.shard_map(
        on_device,
        mesh=mesh,
        in_specs=(tokens, tokens, P("fsdp", "seq"), P("fsdp", "seq"), P()) + (rows,) * 8,
        out_specs=(tokens, P(), tokens) + (rows,) * 8,
        check_vma=False,
    )
```

```python
import functools

import jax
import jax.numpy as jnp
from jax import lax
from jax.experimental import pallas as pl
from jax.experimental.pallas import tpu as pltpu
from jax.sharding import PartitionSpec as P

CHUNK = 256
WIDE = jnp.float32
LOW = jnp.bfloat16
VMEM_BYTES = 60 * 1024 * 1024


def dot(left, right, left_dim=1, right_dim=0):
    return lax.dot_general(
        left, right, (((left_dim,), (right_dim,)), ((), ())), preferred_element_type=WIDE
    )


def decays(rate, place_col, place_row, chunk):
    rows = jnp.exp(-rate * place_col)
    cols = jnp.exp(rate * place_row)
    entry = jnp.exp(-rate * (place_col + 1.0))
    tail = jnp.exp(-rate * (chunk - 1.0 - place_col))
    return rows, cols, entry, tail


def masks(bounds_ref, seg_col, seg_row, n, chunk):
    before = bounds_ref[n]
    last = bounds_ref[n + 1]
    row = lax.broadcasted_iota(jnp.int32, (chunk, chunk), 0)
    col = lax.broadcasted_iota(jnp.int32, (chunk, chunk), 1)
    inner = (seg_col == seg_row) & (row >= col)
    return inner, seg_col == before, seg_col == last, jnp.where(before == last, 1.0, 0.0)


def places(chunk):
    place_col = lax.broadcasted_iota(jnp.int32, (chunk, 1), 0).astype(WIDE)
    place_row = lax.broadcasted_iota(jnp.int32, (1, chunk), 1).astype(WIDE)
    return place_col, place_row


def attend(heads, hd, n, rate_ref, seg_before, seg_row, z_ref, au_ref, a_ref, ss_ref, st_ref, state):
    chunk = z_ref.shape[0]
    seg_col = jnp.transpose(seg_row)[:, :1]
    before = jnp.where(n > 0, seg_before[:1, chunk - 1 :], -1.0)
    last = seg_row[:1, chunk - 1 :]
    row = lax.broadcasted_iota(jnp.int32, (chunk, chunk), 0)
    col = lax.broadcasted_iota(jnp.int32, (chunk, chunk), 1)
    inner = (seg_col == seg_row[:1]) & (row >= col)
    entry_on, tail_on = seg_col == before, seg_col == last
    carry = jnp.where(before == last, 1.0, 0.0)
    place_col, place_row = places(chunk)
    ones = jnp.ones((8, hd), WIDE)
    squares = jnp.zeros((8, chunk), WIDE)
    for h in range(heads):
        rate = rate_ref[h]
        base = h * 4 * hd
        zq, zk, zv, zu = (z_ref[:, base + i * hd : base + (i + 1) * hd] for i in range(4))
        q = (zq * jax.nn.sigmoid(zq)).astype(LOW)
        k = (zk * jax.nn.sigmoid(zk)).astype(LOW)
        v = (zv * jax.nn.sigmoid(zv)).astype(LOW)
        u = zu * jax.nn.sigmoid(zu)
        rows, cols, entry, tail = decays(rate, place_col, place_row, chunk)
        scores = dot(q, k, 1, 1)
        weighted = jnp.where(inner, scores * rows * cols, 0.0).astype(LOW)
        held = state[h]
        st_ref[0, h] = held.astype(LOW)
        a = dot(weighted, v) + jnp.where(entry_on, entry, 0.0) * dot(q, held.astype(LOW))
        kt = (k.astype(WIDE) * jnp.where(tail_on, tail, 0.0)).astype(LOW)
        state[h] = carry * jnp.exp(jnp.full((1, 1), -rate * chunk, WIDE)) * held + dot(kt, v, 0, 0)
        a_ref[:, h * hd : (h + 1) * hd] = a
        au_ref[:, h * hd : (h + 1) * hd] = (a * u).astype(LOW)
        squares = squares + lax.dot_general(
            ones,
            a * a,
            (((1,), (1,)), ((), ())),
            precision=lax.Precision.HIGHEST,
            preferred_element_type=WIDE,
        )
    ss_ref[...] = squares


def slope(z):
    sg = jax.nn.sigmoid(z)
    return sg * (1.0 + z * (1.0 - sg))


def attend_back(
    heads, hd, n, rate_ref, bounds_ref, segc_ref, segr_ref, z_ref, a_ref, dj_ref, ra_ref, m_ref,
    st_ref, dz_ref, o_ref, later
):
    chunk = z_ref.shape[0]
    inner, entry_on, tail_on, carry = masks(bounds_ref, segc_ref[...], segr_ref[...], n, chunk)
    place_col, place_row = places(chunk)
    ra = ra_ref[...]
    m = m_ref[...]
    for h in range(heads):
        rate = rate_ref[h]
        base = h * 4 * hd
        span = slice(h * hd, (h + 1) * hd)
        zq, zk, zv, zu = (z_ref[:, base + i * hd : base + (i + 1) * hd] for i in range(4))
        q = (zq * jax.nn.sigmoid(zq)).astype(LOW)
        k = (zk * jax.nn.sigmoid(zk)).astype(LOW)
        v = (zv * jax.nn.sigmoid(zv)).astype(LOW)
        u = zu * jax.nn.sigmoid(zu)
        an = a_ref[:, span] * ra
        dj = dj_ref[:, span]
        o_ref[:, span] = (an * u).astype(LOW)
        da = (ra * (dj * u - an * m)).astype(LOW)
        rows, cols, entry, tail = decays(rate, place_col, place_row, chunk)
        entry = jnp.where(entry_on, entry, 0.0)
        tail = jnp.where(tail_on, tail, 0.0)
        decay = jnp.where(inner, rows * cols, 0.0)
        weighted = (dot(q, k, 1, 1) * decay).astype(LOW)
        grads = (dot(da, v, 1, 1) * decay).astype(LOW)
        held = st_ref[0, h]
        after = later[h]
        after_low = after.astype(LOW)
        dq = dot(grads, k) + entry * dot(da, held, 1, 1)
        dk = dot(grads, q, 0, 0) + tail * dot(v, after_low, 1, 1)
        dv = dot(weighted, da, 0, 0) + tail * dot(k, after_low)
        qe = (q.astype(WIDE) * entry).astype(LOW)
        later[h] = carry * jnp.exp(jnp.full((1, 1), -rate * chunk, WIDE)) * after + dot(qe, da, 0, 0)
        dz_ref[:, base : base + hd] = (dq * slope(zq)).astype(LOW)
        dz_ref[:, base + hd : base + 2 * hd] = (dk * slope(zk)).astype(LOW)
        dz_ref[:, base + 2 * hd : base + 3 * hd] = (dv * slope(zv)).astype(LOW)
        dz_ref[:, base + 3 * hd : base + 4 * hd] = (dj * an * slope(zu)).astype(LOW)


def empty(shape, kind):
    return pl.pallas_call(
        lambda out: None,
        out_shape=jax.ShapeDtypeStruct(shape, kind),
        out_specs=pl.BlockSpec(memory_space=pl.ANY),
        name="empty",
    )()


def pack_kernel(seq, heads, hd, *refs):
    weights, glu, attn_out, glu_outs = refs[:4], refs[4:6], refs[6], refs[7:]
    for i in range(seq):
        for h in range(heads):
            for m, w in enumerate(weights):
                to, at = (h * 4 + m) * hd, (i * heads + h) * hd
                attn_out[i, :, to : to + hd] = w[:, at : at + hd]
        for w, out in zip(glu, glu_outs):
            n = out.shape[2]
            out[i] = w[:, i * n : (i + 1) * n]


def pack_columns(weights, glu, seq, heads, hd):
    r, kind = weights[0].shape[0], weights[0].dtype
    n = glu[0].shape[1] // seq
    return pl.pallas_call(
        functools.partial(pack_kernel, seq, heads, hd),
        out_shape=[jax.ShapeDtypeStruct((seq, r, heads * 4 * hd), kind)]
        + [jax.ShapeDtypeStruct((seq, r, n), kind)] * 2,
        compiler_params=pltpu.CompilerParams(vmem_limit_bytes=VMEM_BYTES),
        name="pack_columns",
    )(*weights, *glu)


def unpack_kernel(seq, heads, hd, attn, first, second, o_first, o_second, *o_attn):
    for i in range(seq):
        for h in range(heads):
            for m in range(4):
                at, to = (h * 4 + m) * hd, (i * heads + h) * hd
                o_attn[m][:, to : to + hd] = attn[i, :, at : at + hd].astype(WIDE)
        for ref, out in ((first, o_first), (second, o_second)):
            n = ref.shape[2]
            out[:, i * n : (i + 1) * n] = ref[i].astype(WIDE)


def unpack_columns(attn, first, second, heads, hd):
    seq, r = attn.shape[:2]
    shape = lambda n: jax.ShapeDtypeStruct((r, seq * n), WIDE)
    return pl.pallas_call(
        functools.partial(unpack_kernel, seq, heads, hd),
        out_shape=[shape(first.shape[2]), shape(second.shape[2])] + [shape(heads * hd)] * 4,
        compiler_params=pltpu.CompilerParams(vmem_limit_bytes=VMEM_BYTES),
        name="unpack_columns",
    )(attn, first, second)


class Net:
    def __init__(self, shape, send_sem, recv_sem, local_sem):
        self.seq, self.fsdp, self.inner = shape
        self.outer = self.fsdp // self.inner
        self.chips = self.seq // 2
        self.send_sem, self.recv_sem, self.local_sem = send_sem, recv_sem, local_sem
        self.used = 0
        self.locals = 0
        self.s, self.f = lax.axis_index("seq"), lax.axis_index("fsdp")
        self.chip, self.core = self.s // 2, self.s % 2
        self.o, self.i = self.f // self.inner, self.f % self.inner
        self.sent = []

    def seq_peers(self):
        for dx in range(self.chips):
            for dc in range(2):
                if dx or dc:
                    yield dx, dc, lax.rem(self.chip + dx, self.chips) * 2 + lax.rem(self.core + dc, 2)

    def at_seq(self, s):
        return (s, self.f)

    def at_inner(self, j):
        return (self.s, self.o * self.inner + lax.rem(self.i + j, self.inner))

    def at_outer(self, k):
        return (self.s, lax.rem(self.o + k, self.outer) * self.inner + self.i)

    def barrier(self):
        peers = [self.at_seq(s) for _, _, s in self.seq_peers()]
        peers += [self.at_inner(j) for j in range(1, self.inner)]
        peers += [self.at_outer(1), self.at_outer(self.outer - 1)]
        sem = pltpu.get_barrier_semaphore()
        for peer in peers:
            pl.semaphore_signal(sem, inc=1, device_id=peer, device_id_type=pl.DeviceIdType.MESH)
        pl.semaphore_wait(sem, len(peers))

    def send(self, src, dst, device):
        copy = pltpu.make_async_remote_copy(
            src_ref=src,
            dst_ref=dst,
            send_sem=self.send_sem.at[self.used],
            recv_sem=self.recv_sem.at[self.used],
            device_id=device,
            device_id_type=pl.DeviceIdType.MESH,
        )
        self.used += 1
        copy.start()
        self.sent.append(copy)
        return copy

    def copy(self, src, dst):
        copy = pltpu.make_async_copy(src, dst, self.local_sem.at[self.locals])
        self.locals += 1
        copy.start()
        return copy

    def left(self, copy):
        copy.wait_send()
        self.sent = [other for other in self.sent if other is not copy]

    def finish(self):
        for copy in self.sent:
            copy.wait_send()
        self.sent = []


def net_shape(mesh_seq, mesh_fsdp):
    return mesh_seq, mesh_fsdp, 2 if mesh_fsdp == 8 else 4


class Ring:
    def __init__(self, net, piece, full):
        self.net, self.piece, self.full = net, piece, full
        self.copies = [net.copy(piece, full.at[:, net.o, net.i])]
        self.at = 0
        self.coming = None
        self.side = []

    def step(self):
        net, full = self.net, self.full
        if self.at >= net.outer:
            return
        if self.coming is not None:
            self.coming.wait_recv()
        spot = full.at[:, lax.rem(net.o + net.outer - self.at, net.outer), net.i]
        src = self.piece if self.at == 0 else spot
        self.coming = None
        if self.at < net.outer - 1:
            self.coming = net.send(src, spot, net.at_outer(1))
        for j in range(1, net.inner):
            self.side.append(net.send(src, spot, net.at_inner(j)))
        self.at += 1

    def done(self):
        while self.at < self.net.outer:
            self.step()
        for copy in self.side:
            copy.wait_recv()
        for copy in self.copies:
            copy.wait()


class WideRing:
    def __init__(self, net, piece, full):
        self.net, self.full = net, full
        self.copies = [net.copy(piece, full.at[:, net.o, net.i])]
        self.side = [
            net.send(piece, full.at[:, net.o, net.i], net.at_inner(j)) for j in range(1, net.inner)
        ]
        self.at = 0
        self.coming = None

    def step(self):
        net, full = self.net, self.full
        if self.at >= net.outer:
            return
        if self.at == 0:
            for copy in self.side:
                copy.wait_recv()
            for copy in self.copies:
                copy.wait()
        else:
            self.coming.wait_recv()
        spot = full.at[:, lax.rem(net.o + net.outer - self.at, net.outer)]
        if self.at < net.outer - 1:
            self.coming = net.send(spot, spot, net.at_outer(1))
        self.at += 1

    def done(self):
        while self.at < self.net.outer:
            self.step()


def swap(net, blocks, got):
    own = net.copy(blocks.at[net.s], got.at[net.s])
    coming = [
        net.send(blocks.at[s], got.at[net.s], net.at_seq(s)) for _, _, s in net.seq_peers()
    ]
    return own, coming


def arrive(pair):
    own, coming = pair
    own.wait()
    for copy in coming:
        copy.wait_recv()


class Rows:
    def __init__(self, net, own, whole, start=0):
        t, each = own.shape[0], whole.shape[0] // net.seq
        self.net, self.whole = net, whole
        spot = lambda s: whole.at[pl.ds(pl.multiple_of(s * each + start, t), t)]
        self.spot = spot
        self.far = [
            net.send(own, spot(net.s), net.at_seq(lax.rem(net.chip + dx, net.chips) * 2 + net.core))
            for dx in range(1, net.chips)
        ]
        self.near = [net.send(own, spot(net.s), net.at_seq(net.chip * 2 + 1 - net.core))]
        self.own = net.copy(own, spot(net.s))

    def turn(self):
        net = self.net
        for dx, copy in zip(range(1, net.chips), self.far):
            copy.wait_recv()
            spot = self.spot(lax.rem(net.chip + net.chips - dx, net.chips) * 2 + net.core)
            self.near.append(net.send(spot, spot, net.at_seq(net.chip * 2 + 1 - net.core)))

    def done(self):
        for copy in self.near:
            copy.wait_recv()
        self.own.wait()


def gather_kernel(
    shape, heads, hd,
    rate_ref, attn_ref, first_ref, second_ref, out_ref, down_ref, n1_ref, seg_ref, count_ref, x_ref,
    attn_mid, first_mid, second_mid,
    full_attn, full_first, full_second, full_out, full_down,
    n1_all, z_all, a_all, states, mixed_ref, hsum_ref, n2_own, n2_all, core_in, chip_in,
    seg_all, count_all, ss_all,
    w_attn, w_out, au_all, state, stage, term, wide_tile, hsum_tile, x_tile, n2_tile, ss_in,
    seq_buf, in_buf, out_buf, send_sem, recv_sem, local_sem,
):
    net = Net(shape, send_sem, recv_sem, local_sem)
    length, width = n1_all.shape
    cols = z_all.shape[1]
    own_rows = x_ref.shape[0]
    wide = min(512, width)
    net.barrier()
    count = Total(net, count_ref, seq_buf, in_buf, out_buf)
    attn_swap = swap(net, attn_ref, attn_mid)
    seg_own = net.copy(seg_ref, seg_all.at[net.s])
    segs = [net.send(seg_ref, seg_all.at[net.s], net.at_seq(s)) for _, _, s in net.seq_peers()]
    first_swap = swap(net, first_ref, first_mid)
    second_swap = swap(net, second_ref, second_mid)
    rows = Rows(net, n1_ref, n1_all)
    arrive(attn_swap)
    count.step()
    ring_attn = Ring(net, attn_mid, full_attn)
    ring_out = Ring(net, out_ref, full_out)
    for _ in range(net.outer):
        ring_attn.step()
        ring_out.step()
        count.step()
    arrive(first_swap)
    arrive(second_swap)
    ring_first = Ring(net, first_mid, full_first)
    ring_second = Ring(net, second_mid, full_second)
    ring_first.step()
    ring_second.step()
    ring_down = WideRing(net, down_ref, full_down)
    rows.turn()
    queue = [ring_first, ring_second, ring_down] * (net.outer - 1) + [ring_down]

    def pump(times=1):
        for _ in range(min(times, len(queue))):
            queue.pop(0).step()

    seg_own.wait()
    for copy in segs:
        copy.wait_recv()
    ring_attn.done()
    load_attn = net.copy(full_attn, w_attn)
    rows.done()
    ring_out.done()
    load_out = net.copy(full_out, w_out)
    load_attn.wait()
    load_out.wait()

    state[...] = jnp.zeros_like(state)
    per = own_rows // CHUNK

    def seg_of(n):
        at = pl.ds(pl.multiple_of(n % per * CHUNK, CHUNK), CHUNK)
        return jnp.broadcast_to(seg_all[n // per, :, at].astype(WIDE), (8, CHUNK))

    def chunks(low, steps):
        def body(n1_chunk, z_ref, a_ref, st_ref):
            n = low + pl.program_id(0)

            def project(j, _):
                at = pl.ds(pl.multiple_of(j * wide, wide), wide)
                weight = w_attn[:, :, :, :, at].reshape(width, wide)
                z_ref[:, at] = dot(n1_chunk[...], weight)
                return 0

            lax.fori_loop(0, cols // wide, project, 0)
            au_rows = au_all.at[pl.ds(pl.multiple_of(n * CHUNK, CHUNK), CHUNK)]
            attend(
                heads, hd, n, rate_ref, seg_of(jnp.maximum(n - 1, 0)), seg_of(n), z_ref, au_rows,
                a_ref, ss_all.at[n], st_ref, state,
            )

        block = lambda n: pl.BlockSpec((CHUNK, n), lambda i: (low + i, 0))
        pltpu.emit_pipeline(
            body,
            grid=(steps,),
            in_specs=[block(width)],
            out_specs=[
                block(cols),
                block(heads * hd),
                pl.BlockSpec((1, heads, hd, hd), lambda i: (low + i, 0, 0, 0)),
            ],
        )(n1_all, z_all, a_all, states)

    total = length // CHUNK
    half = total // 2
    chunks(0, half)
    pump()
    chunks(half, total - half)
    near_ss = [net.send(ss_all, ss_in.at[net.s], net.at_seq(s)) for _, _, s in net.seq_peers()]
    pump()

    used = [None, None]
    turns = [0]

    def product(row, each):
        x = au_all[pl.ds(pl.multiple_of(row, CHUNK), CHUNK)]

        def one(j, _):
            at = pl.ds(pl.multiple_of(j * wide, wide), wide)
            weight = w_out[:, :, :, :, at].reshape(heads * hd, wide)
            each(at, dot(x, weight))
            return 0

        lax.fori_loop(0, width // wide, one, 0)

    def slot():
        i = turns[0] % 2
        turns[0] += 1
        if used[i] is not None:
            net.left(used[i])
        return i

    def row_of(chip, core, t):
        return (chip * 2 + core) * own_rows + t * CHUNK

    near = {}
    far = []

    def give(dx):
        chip = lax.rem(net.chip + dx, net.chips)
        for t in range(per):
            i = slot()

            def store(at, part, i=i):
                stage[i, :, at] = part.astype(LOW)

            product(row_of(chip, 1 - net.core, t), store)
            spot = core_in.at[dx, pl.ds(t * CHUNK, CHUNK)]
            used[i] = near[dx, t] = net.send(
                stage.at[i], spot, net.at_seq(net.chip * 2 + 1 - net.core)
            )

    def keep(dx, finish=None):
        chip = lax.rem(net.chip + dx, net.chips)
        for t in range(per):
            span = pl.ds(t * CHUNK, CHUNK)
            near[dx, t].wait_recv()
            loads = [net.copy(core_in.at[dx, span], term.at[0])]
            if dx == 0:
                loads.append(net.copy(x_ref.at[span], x_tile))
                for j, copies in enumerate(far):
                    copies[t].wait_recv()
                    loads.append(net.copy(chip_in.at[j, span], term.at[j + 1]))
            else:
                i = slot()
            for load in loads:
                load.wait()

            def store(at, part):
                add = part + term[0, :, at].astype(WIDE)
                if dx == 0:
                    for j in range(len(far)):
                        add = add + term[j + 1, :, at].astype(WIDE)
                    wide_tile[:, at] = add
                else:
                    stage[i, :, at] = add.astype(LOW)

            product(row_of(chip, net.core, t), store)
            if dx == 0:
                finish(t, span)
            else:
                used[i] = net.send(
                    stage.at[i], chip_in.at[dx - 1, span], net.at_seq(chip * 2 + net.core)
                )
                far[dx - 1].append(used[i])

    def finish(t, span):
        at = net.s * per + t
        squares = ss_in[0, at]
        for j in range(1, net.seq):
            squares = squares + ss_in[j, at]
        ra = lax.rsqrt(jnp.transpose(squares)[:, :1] / width + 1e-6)

        def add(j, squares):
            at = pl.ds(pl.multiple_of(j * wide, wide), wide)
            mixed = wide_tile[:, at] * ra
            wide_tile[:, at] = mixed
            hsum = x_tile[:, at].astype(WIDE) + mixed
            hsum_tile[:, at] = hsum
            return squares + jnp.sum(hsum * hsum, axis=1, keepdims=True)

        squares = lax.fori_loop(0, width // wide, add, jnp.zeros((CHUNK, 1), WIDE))
        r2 = lax.rsqrt(squares / width + 1e-6)

        def scale(j, _):
            at = pl.ds(pl.multiple_of(j * wide, wide), wide)
            n2_tile[:, at] = (hsum_tile[:, at] * r2).astype(LOW)
            return 0

        lax.fori_loop(0, width // wide, scale, 0)
        outs = [
            net.copy(wide_tile, mixed_ref.at[span]),
            net.copy(hsum_tile, hsum_ref.at[span]),
            net.copy(n2_tile, n2_own.at[span]),
        ]
        for out in outs:
            out.wait()

    for dx in range(1, net.chips):
        far.append([])
        give(dx)
        keep(dx)
    pump()
    give(0)
    pump(2)
    for copy in near_ss:
        copy.wait_recv()
    for copy in near_ss:
        net.left(copy)
    ss_in[net.s] = ss_all[...]
    keep(0, finish)
    rows = Rows(net, n2_own, n2_all)
    pump(3)
    rows.turn()
    pump(len(queue))
    count_all[...] = count.done()
    for ring in (ring_first, ring_second, ring_down):
        ring.done()
    rows.done()
    total_ss = ss_in[0]
    for j in range(1, net.seq):
        total_ss = total_ss + ss_in[j]
    ss_all[...] = total_ss
    net.finish()


HBM = pl.BlockSpec(memory_space=pl.ANY)


def gather_all(shape, heads, hd, rates, attn, first, second, w_out, w_down, n1, seg, count, x):
    seq, fsdp, inner = shape
    outer = fsdp // inner
    chips = seq // 2
    own_rows, width = n1.shape
    length = own_rows * seq
    cols = attn.shape[2]
    chunks = length // CHUNK
    like = lambda v, lead: jax.ShapeDtypeStruct(lead + v.shape[-2:], v.dtype)
    ring = lambda v: like(v, (v.shape[0], outer, inner))
    low = lambda *dims: jax.ShapeDtypeStruct(dims, LOW)
    wide = lambda *dims: jax.ShapeDtypeStruct(dims, WIDE)
    outs = [like(v, (seq,)) for v in (attn, first, second)]
    outs += [ring(v) for v in (attn, first, second, w_out, w_down)]
    outs += [low(length, width), wide(length, cols), wide(length, heads * hd)]
    outs += [low(chunks, heads, hd, hd), wide(own_rows, width), wide(own_rows, width)]
    outs += [low(own_rows, width), low(length, width)]
    outs += [low(chips, own_rows, width), low(max(chips - 1, 1), own_rows, width)]
    in_hbm = len(outs)
    outs += [jax.ShapeDtypeStruct((seq,) + seg.shape, seg.dtype), wide(8, 128)]
    outs += [wide(chunks, 8, CHUNK)]
    copies = 7 * seq + 5 * (outer * inner + outer) + total_copies(shape) + 2 * chunks + 4 * seq
    in_vmem = pl.BlockSpec(memory_space=pltpu.VMEM)
    smem = pl.BlockSpec(memory_space=pltpu.SMEM)
    got = pl.pallas_call(
        functools.partial(gather_kernel, shape, heads, hd),
        in_specs=[smem] + [HBM] * 7 + [in_vmem, HBM],
        out_specs=[HBM] * in_hbm + [in_vmem] * 3,
        out_shape=outs,
        scratch_shapes=[
            pltpu.VMEM(ring(attn).shape, LOW),
            pltpu.VMEM(ring(w_out).shape, LOW),
            pltpu.VMEM((length, heads * hd), LOW),
            pltpu.VMEM((heads, hd, hd), WIDE),
            pltpu.VMEM((2, CHUNK, width), LOW),
            pltpu.VMEM((chips, CHUNK, width), LOW),
            pltpu.VMEM((CHUNK, width), WIDE),
            pltpu.VMEM((CHUNK, width), WIDE),
            pltpu.VMEM((CHUNK, width), LOW),
            pltpu.VMEM((CHUNK, width), LOW),
            pltpu.VMEM((seq, chunks, 8, CHUNK), WIDE),
        ]
        + total_scratch(shape)
        + [
            pltpu.SemaphoreType.DMA((copies,)),
            pltpu.SemaphoreType.DMA((copies,)),
            pltpu.SemaphoreType.DMA((24 + 6 * chunks,)),
        ],
        compiler_params=pltpu.CompilerParams(
            collective_id=0, has_side_effects=True, vmem_limit_bytes=VMEM_BYTES
        ),
        name="gather_all",
    )(rates, attn, first, second, w_out, w_down, n1, seg, count, x)
    flat = lambda v: v.reshape(-1, v.shape[-1])
    squares = got[in_hbm + 2][:, 0].reshape(length, 1)
    return [flat(v) for v in got[3:8]] + list(got[8:14]) + [got[15], got[in_hbm], got[in_hbm + 1], squares]


class Total:
    def __init__(self, net, own, seq_buf, in_buf, out_buf):
        self.net, self.bufs, self.stage = net, (seq_buf, in_buf, out_buf), 0
        self.coming = self.share(seq_buf, net.s, own[...], [net.at_seq(s) for _, _, s in net.seq_peers()])

    def share(self, buf, at, value, devices):
        buf[at] = value
        return [self.net.send(buf.at[at], buf.at[at], device) for device in devices]

    def gathered(self, buf):
        for copy in self.coming:
            copy.wait_recv()
        total = buf[0]
        for j in range(1, buf.shape[0]):
            total = total + buf[j]
        return total

    def step(self):
        net, (seq_buf, in_buf, out_buf) = self.net, self.bufs
        if self.stage == 0:
            peers = [net.at_inner(j) for j in range(1, net.inner)]
            self.coming = self.share(in_buf, net.i, self.gathered(seq_buf), peers)
        elif self.stage == 1:
            self.coming = self.share(out_buf, net.o, self.gathered(in_buf), [net.at_outer(1)])
        elif self.stage < net.outer:
            self.coming[-1].wait_recv()
            at = lax.rem(net.o + net.outer - self.stage + 1, net.outer)
            self.coming = [net.send(out_buf.at[at], out_buf.at[at], net.at_outer(1))]
        self.stage += 1

    def done(self):
        while self.stage < self.net.outer:
            self.step()
        return self.gathered(self.bufs[2])


def total_scratch(shape):
    seq, fsdp, inner = shape
    return [pltpu.VMEM((n, 8, 128), WIDE) for n in (seq, inner, fsdp // inner)]


def total_copies(shape):
    seq, fsdp, inner = shape
    return seq + inner + fsdp // inner


class Sum:
    def __init__(self, net, g, side, ring, send, load, there=False):
        self.net, self.g, self.side_ref, self.ring_ref = net, g, side, ring
        self.send_buf, self.load = send, load
        self.side = []
        self.ring = []
        self.at = 0
        self.there = there
        for k in range(0 if there else net.outer):
            o = self.spot(k)
            now = []
            for j in range(1, net.inner):
                to = lax.rem(net.i + j, net.inner)
                now.append(net.send(g.at[:, o, to], side.at[j - 1, :, o], net.at_inner(j)))
            self.side.append(now)

    def spot(self, k):
        return lax.rem(self.net.o + 2 * self.net.outer - 1 - k, self.net.outer)

    def step(self, final):
        net, k = self.net, self.at
        self.at += 1
        o = self.spot(k)
        terms = self.load
        loads = [net.copy(self.g.at[:, o, net.i], terms.at[0])]
        for j in range(net.inner - 1):
            if not self.there:
                self.side[k][j].wait_recv()
            loads.append(net.copy(self.side_ref.at[j, :, o], terms.at[j + 1]))
        count = net.inner
        if k > 0:
            self.ring[k - 1].wait_recv()
            loads.append(net.copy(self.ring_ref.at[k - 1], terms.at[count]))
            count += 1
        if k >= 2:
            net.left(self.ring[k - 2])
        for load in loads:
            load.wait()

        def one(i, _):
            total = terms[0, i].astype(WIDE)
            for j in range(1, count):
                total = total + terms[j, i].astype(WIDE)
            if k < net.outer - 1:
                self.send_buf[k % 2, i] = total.astype(LOW)
            else:
                final(i, total)
            return 0

        lax.fori_loop(0, terms.shape[1], one, 0)
        if k < net.outer - 1:
            self.ring.append(net.send(self.send_buf.at[k % 2], self.ring_ref.at[k], net.at_outer(1)))


GRADS = ("down", "second", "attn", "out")
SPLIT = ("second", "attn")


def back_kernel(
    shape, heads, hd,
    rate_ref, bounds_ref, segc, segr, z, a, dh, ra, mean, states, w_out, w_attn, n1, loss_ref,
    g_down, g_second, side_second,
    dn1_ref, o_down, o_out, o_loss, got_second, got_attn, g_attn,
    side_down, side_attn, side_out,
    ring_down, ring_second, ring_attn, ring_out,
    core_in, chip_in,
    dz_all, later, dj, o_chunk, out_acc, g_out, stage, term, wide_tile,
    *rest
):
    it = iter(rest)
    take = lambda names: {name: next(it) for name in names}
    sends, loads = take(GRADS), take(GRADS)
    total_bufs = [next(it) for _ in range(3)]
    send_sem, recv_sem, local_sem = (next(it) for _ in range(3))
    net = Net(shape, send_sem, recv_sem, local_sem)
    grads = dict(down=g_down, second=g_second, attn=g_attn, out=g_out)
    sides = dict(down=side_down, second=side_second, attn=side_attn, out=side_out)
    rings = dict(down=ring_down, second=ring_second, attn=ring_attn, out=ring_out)
    gots = dict(second=got_second, attn=got_attn)
    owned = dict(down=o_down, out=o_out)
    length, cols = dz_all.shape
    width = dh.shape[1]
    count = length // CHUNK
    wide = min(512, width)

    net.barrier()
    sums, swaps, queue = {}, {}, []
    loss = Total(net, loss_ref, *total_bufs)

    def begin(name):
        there = name == "second"
        sums[name] = Sum(net, grads[name], sides[name], rings[name], sends[name], loads[name], there)
        queue.extend([name] * net.outer)

    def pump(times=1):
        for _ in range(min(times, len(queue))):
            name = queue.pop(0)

            def final(i, rows):
                if name in owned:
                    owned[name][...] = rows
                else:
                    totals[i] = rows.astype(LOW)

            totals = sends[name].at[(net.outer - 1) % 2]
            sums[name].step(final)
            if name in SPLIT and sums[name].at == net.outer:
                swaps[name] = swap(net, totals, gots[name])

    loss.step()
    for name in ("second", "down"):
        begin(name)
    pump()

    later[...] = jnp.zeros_like(later)
    out_acc[...] = jnp.zeros_like(out_acc)

    def chunks(top, steps):
        def body(segc_ref, segr_ref, z_ref, a_ref, dh_ref, ra_ref, m_ref, st_ref):
            n = top - pl.program_id(0)
            dj[...] = dot(dh_ref[...], w_out[...], 1, 1)
            rows = pl.ds(pl.multiple_of(n * CHUNK, CHUNK), CHUNK)
            attend_back(
                heads, hd, n, rate_ref, bounds_ref, segc_ref, segr_ref, z_ref, a_ref, dj, ra_ref,
                m_ref, st_ref, dz_all.at[rows], o_chunk, later,
            )

            def add(j, _):
                at = pl.ds(pl.multiple_of(j * wide, wide), wide)
                out_acc[:, at] += dot(o_chunk[...], dh_ref[:, at], 0, 0)
                return 0

            lax.fori_loop(0, width // wide, add, 0)

        block = lambda n: pl.BlockSpec((CHUNK, n), lambda i: (top - i, 0))
        pltpu.emit_pipeline(
            body,
            grid=(steps,),
            in_specs=[
                block(1),
                pl.BlockSpec((1, CHUNK), lambda i: (0, top - i)),
                block(cols),
                block(heads * hd),
                block(width),
                block(1),
                block(1),
                pl.BlockSpec((1, heads, hd, hd), lambda i: (top - i, 0, 0, 0)),
            ],
        )(segc, segr, z, a, dh, ra, mean, states)

    half = count // 2
    chunks(count - 1, half)
    loss.step()
    pump()
    chunks(count - 1 - half, count - half)
    loss.step()
    pump()

    own_rows = dn1_ref.shape[0]
    tile = min(256, own_rows)
    used = [None, None]
    turns = [0]

    def product(row, each):
        x = dz_all[pl.ds(pl.multiple_of(row, tile), tile)]

        def one(j, _):
            at = pl.ds(pl.multiple_of(j * wide, wide), wide)
            each(at, dot(x, w_attn[at, :], 1, 1))
            return 0

        lax.fori_loop(0, width // wide, one, 0)

    def slot():
        i = turns[0] % 2
        turns[0] += 1
        if used[i] is not None:
            net.left(used[i])
        return i

    def row_of(chip, core, t):
        return (chip * 2 + core) * own_rows + t * tile

    near = {}
    far = []

    def give(dx):
        chip = lax.rem(net.chip + dx, net.chips)
        for t in range(own_rows // tile):
            i = slot()

            def store(at, part, i=i):
                stage[i, :, at] = part.astype(LOW)

            product(row_of(chip, 1 - net.core, t), store)
            spot = core_in.at[dx, pl.ds(t * tile, tile)]
            used[i] = near[dx, t] = net.send(
                stage.at[i], spot, net.at_seq(net.chip * 2 + 1 - net.core)
            )

    def keep(dx):
        chip = lax.rem(net.chip + dx, net.chips)
        for t in range(own_rows // tile):
            span = pl.ds(t * tile, tile)
            near[dx, t].wait_recv()
            loads = [net.copy(core_in.at[dx, span], term.at[0])]
            if dx == 0:
                for j, copies in enumerate(far):
                    copies[t].wait_recv()
                    loads.append(net.copy(chip_in.at[j, span], term.at[j + 1]))
            else:
                i = slot()
            for load in loads:
                load.wait()

            def store(at, part):
                total = part
                for j in range(len(loads)):
                    total = total + term[j, :, at].astype(WIDE)
                if dx == 0:
                    wide_tile[:, at] = total
                else:
                    stage[i, :, at] = total.astype(LOW)

            product(row_of(chip, net.core, t), store)
            if dx == 0:
                net.copy(wide_tile, dn1_ref.at[span]).wait()
            else:
                used[i] = net.send(
                    stage.at[i], chip_in.at[dx - 1, span], net.at_seq(chip * 2 + net.core)
                )
                far[dx - 1].append(used[i])

    for dx in range(1, net.chips):
        far.append([])
        give(dx)
        keep(dx)
    pump()

    parts = 2
    spread = net.outer // parts
    features = width // net.seq // parts

    def grad_body(n1_ref, g_ref):
        for j in range(cols // wide):
            at = slice(j * wide, (j + 1) * wide)
            got = dot(n1_ref[...], dz_all[:, at], 0, 0).astype(LOW)
            g_ref[:, :, :, :, at] = got.reshape(g_ref.shape[:-1] + (wide,))

    pltpu.emit_pipeline(
        grad_body,
        grid=(net.seq, parts),
        in_specs=[pl.BlockSpec((length, features), lambda i, j: (0, i * parts + j))],
        out_specs=[
            pl.BlockSpec((1, spread) + g_attn.shape[2:], lambda i, j: (i, j, 0, 0, 0)),
        ],
    )(n1, g_attn)
    begin("attn")
    for j in range(width // wide):
        at = slice(j * wide, (j + 1) * wide)
        g_out[:, :, :, :, at] = out_acc[:, at].astype(LOW).reshape(g_out.shape[:-1] + (wide,))
    begin("out")
    pump(2)
    give(0)
    pump()
    keep(0)
    o_loss[...] = loss.done()
    pump(len(queue))
    for name in SPLIT:
        arrive(swaps[name])
    net.finish()


def back_all(shape, heads, hd, rates, bounds, seg, z, a, dh, ra, mean, states, w_out, w_attn, n1, loss, g_down, g_second, side_second):
    seq, fsdp, inner = shape
    outer = fsdp // inner
    length, width = dh.shape
    cols = z.shape[1]
    own_rows = length // seq
    chips = seq // 2
    tile = min(256, own_rows)
    g_down = g_down.reshape(1, outer, inner, g_down.shape[0] // fsdp, width)
    size = {
        n: (g.shape[0], g.shape[3], g.shape[4]) for n, g in (("down", g_down), ("second", g_second))
    }
    size["attn"] = (seq, width // (seq * fsdp), cols)
    size["out"] = (1, width // (seq * fsdp), width)
    whole = lambda n: (size[n][0], outer, inner) + size[n][1:]
    low = lambda dims: jax.ShapeDtypeStruct(dims, LOW)
    row = lambda n: jax.ShapeDtypeStruct(size[n][1:], WIDE)
    outs = [jax.ShapeDtypeStruct((own_rows, width), WIDE), row("down"), row("out")]
    outs += [jax.ShapeDtypeStruct((8, 128), WIDE)]
    outs += [low(size[n]) for n in SPLIT] + [low(whole("attn"))]
    outs += [
        low((inner - 1, size[n][0], outer) + size[n][1:]) for n in GRADS if n != "second"
    ]
    outs += [low((outer - 1,) + size[n]) for n in GRADS]
    outs += [low((chips, own_rows, width)), low((max(chips - 1, 1), own_rows, width))]
    in_vmem = pl.BlockSpec(memory_space=pltpu.VMEM)
    smem = pl.BlockSpec(memory_space=pltpu.SMEM)
    scratch = [
        pltpu.VMEM((length, cols), LOW),
        pltpu.VMEM((heads, hd, hd), WIDE),
        pltpu.VMEM((CHUNK, heads * hd), WIDE),
        pltpu.VMEM((CHUNK, heads * hd), LOW),
        pltpu.VMEM((heads * hd, width), WIDE),
        pltpu.VMEM(whole("out"), LOW),
        pltpu.VMEM((2, tile, width), LOW),
        pltpu.VMEM((chips, tile, width), LOW),
        pltpu.VMEM((tile, width), WIDE),
    ]
    scratch += [pltpu.VMEM((2,) + size[n], LOW) for n in GRADS]
    scratch += [pltpu.VMEM((inner + 1,) + size[n], LOW) for n in GRADS]
    scratch += total_scratch(shape)
    copies = 5 * (outer * inner + outer) + 3 * seq + total_copies(shape) + 2 * length // tile
    scratch += [
        pltpu.SemaphoreType.DMA((copies,)),
        pltpu.SemaphoreType.DMA((copies,)),
        pltpu.SemaphoreType.DMA((5 * outer * (inner + 1) + 3 + 4 * length // tile,)),
    ]
    return pl.pallas_call(
        functools.partial(back_kernel, shape, heads, hd),
        in_specs=[smem, smem] + [HBM] * 8 + [in_vmem] * 2 + [HBM, in_vmem] + [HBM] * 3,
        out_specs=[HBM] + [in_vmem] * 3 + [HBM] * (len(outs) - 4),
        out_shape=outs,
        scratch_shapes=scratch,
        compiler_params=pltpu.CompilerParams(
            collective_id=1, has_side_effects=True, vmem_limit_bytes=VMEM_BYTES
        ),
        name="back_all",
    )(
        rates, bounds, seg.reshape(length, 1), seg.reshape(1, length), z, a, dh, ra, mean, states,
        w_out, w_attn, n1, loss, g_down, g_second, side_second
    )[:6]


def spans(n, step=512):
    return [slice(at, min(at + step, n)) for at in range(0, n, step)]


def glu_kernel(
    shape,
    n2_all, w_first, w_second, w_down, hsum_ref, teacher_ref, keep_ref, scale_ref, mixed_ref,
    layer_out, g_down, g_first, g_second, dh_ref, dh_all, dy_all, dy_own, dh_own,
    core_y, chip_y, core_n, chip_n, side_first, side_second, ring_first, got_first,
    loss_ref, mean_all,
    one_all, two_all, p_all, dy_wide, stage, term, wide_tile, hsum_tile, mixed_tile, low_tile, sent_tile, sum_send, sum_load,
    send_sem, recv_sem, local_sem,
):
    net = Net(shape, send_sem, recv_sem, local_sem)
    width = n2_all.shape[1]
    ffs = p_all.shape[1]
    own_rows = hsum_ref.shape[0]
    per = own_rows // CHUNK
    wide = min(512, width)
    blocks = width // wide
    net.barrier()

    def rows_at(n):
        return pl.ds(pl.multiple_of(n * CHUNK, CHUNK), CHUNK)

    def of_chip(dx):
        return lax.rem(net.chip + dx, net.chips)

    def tiles(dx, src, body):
        base = of_chip(dx) * 2 * per
        pltpu.emit_pipeline(
            lambda ref: body(base + pl.program_id(0), ref),
            grid=(2 * per,),
            in_specs=[pl.BlockSpec((CHUNK, width), lambda i: (base + i, 0))],
        )(src)

    def columns(each):
        def one(j, _):
            each(pl.ds(pl.multiple_of(j * wide, wide), wide))
            return 0

        lax.fori_loop(0, blocks, one, 0)

    used = [None, None]
    turns = [0]

    def slot():
        i = turns[0] % 2
        turns[0] += 1
        if used[i] is not None:
            net.left(used[i])
        return i

    class Exchange:
        def __init__(self, product, core_in, chip_in):
            self.product, self.core_in, self.chip_in = product, core_in, chip_in
            self.near, self.far = {}, {}

        def give(self, dx):
            for t in range(per):
                i = slot()
                rows = rows_at((of_chip(dx) * 2 + 1 - net.core) * per + t)

                def store(at):
                    stage[i, :, at] = self.product(rows, at).astype(LOW)

                columns(store)
                used[i] = self.near[dx, t] = net.send(
                    stage.at[i],
                    self.core_in.at[dx, pl.ds(t * CHUNK, CHUNK)],
                    net.at_seq(net.chip * 2 + 1 - net.core),
                )

        def keep(self, dx, finish=None):
            for t in range(per):
                span = pl.ds(t * CHUNK, CHUNK)
                rows = rows_at((of_chip(dx) * 2 + net.core) * per + t)
                self.near[dx, t].wait_recv()
                loads = [net.copy(self.core_in.at[dx, span], term.at[0])]
                if dx == 0:
                    for j in range(1, net.chips):
                        self.far[j, t].wait_recv()
                        loads.append(net.copy(self.chip_in.at[j - 1, span], term.at[j]))
                    loads.append(net.copy(hsum_ref.at[span], hsum_tile))
                else:
                    i = slot()
                for load in loads:
                    load.wait()

                def store(at):
                    total = self.product(rows, at) + term[0, :, at].astype(WIDE)
                    if dx == 0:
                        for j in range(1, net.chips):
                            total = total + term[j, :, at].astype(WIDE)
                        wide_tile[:, at] = total
                    else:
                        stage[i, :, at] = total.astype(LOW)

                columns(store)
                if dx == 0:
                    finish(t, span)
                else:
                    used[i] = self.far[dx, t] = net.send(
                        stage.at[i],
                        self.chip_in.at[dx - 1, span],
                        net.at_seq(of_chip(dx) * 2 + net.core),
                    )

    def hidden(n, n2):
        rows = rows_at(n)
        for b in spans(ffs):
            one = dot(n2[...], w_first[:, b])
            two = dot(n2[...], w_second[:, b])
            one_all[rows, b] = one.astype(LOW)
            two_all[rows, b] = two.astype(LOW)
            p_all[rows, b] = (one * two).astype(LOW)

    y_sum = Exchange(lambda rows, at: dot(p_all[rows, :], w_down[:, at]), core_y, chip_y)
    for dx in range(1, net.chips):
        tiles(dx, n2_all, hidden)
        y_sum.give(dx)
        y_sum.keep(dx)
    tiles(0, n2_all, hidden)
    y_sum.give(0)

    loss_ref[...] = jnp.zeros_like(loss_ref)
    dy_rows = []

    def finish_y(t, span):
        net.copy(teacher_ref.at[span], sent_tile).wait()
        keep = keep_ref[span, :]
        scale = scale_ref[:1, :1] * keep

        def one(j, squares):
            at = pl.ds(pl.multiple_of(j * wide, wide), wide)
            y = hsum_tile[:, at] + wide_tile[:, at]
            low_tile[:, at] = y.astype(LOW)
            error = y - sent_tile[:, at].astype(WIDE)
            dy = scale * error
            dy_wide[span, at] = dy
            stage[1, :, at] = dy.astype(LOW)
            return squares + jnp.sum(keep * error * error, axis=1, keepdims=True)

        squares = lax.fori_loop(0, blocks, one, jnp.zeros((CHUNK, 1), WIDE))
        loss_ref[...] += jnp.broadcast_to(jnp.sum(squares, axis=0, keepdims=True), (8, 128))
        outs = [
            net.copy(low_tile, layer_out.at[span]),
            net.copy(stage.at[1], dy_own.at[span]),
        ]
        for out in outs:
            out.wait()
        dy_rows.append(Rows(net, dy_own.at[span], dy_all, t * CHUNK))

    def free_stage():
        for i in range(2):
            if used[i] is not None:
                net.left(used[i])
            used[i] = None

    free_stage()
    y_sum.keep(0, finish_y)

    def slopes(n, dy):
        rows = rows_at(n)
        for b in spans(ffs):
            dp = dot(dy[...], w_down[b, :], 1, 1)
            one = one_all[rows, b].astype(WIDE)
            two = two_all[rows, b].astype(WIDE)
            one_all[rows, b] = (dp * two).astype(LOW)
            two_all[rows, b] = (dp * one).astype(LOW)

    n_sum = Exchange(
        lambda rows, at: dot(one_all[rows, :], w_first[at, :], 1, 1)
        + dot(two_all[rows, :], w_second[at, :], 1, 1),
        core_n,
        chip_n,
    )
    for rows in dy_rows:
        rows.near[0].wait_recv()
        rows.near = rows.near[1:]
        rows.own.wait()
    tiles(0, dy_all, slopes)
    n_sum.give(0)
    for rows in dy_rows:
        rows.turn()
    for rows in dy_rows:
        for copy in rows.near:
            copy.wait_recv()
    for dx in range(1, net.chips):
        tiles(dx, dy_all, slopes)
        n_sum.give(dx)
        n_sum.keep(dx)

    length = p_all.shape[0]
    step = 256

    def grad_down(dy, out):
        for b in spans(ffs):
            out[b, :] = dot(p_all[:, b], dy[...], 0, 0).astype(LOW)

    parts = 2
    spread = net.outer // parts
    features = width // net.seq // parts

    def grad_columns(held, target):
        def body(n2, out):
            for b in spans(ffs):
                got = dot(n2[...], held[:, b], 0, 0).astype(LOW)
                out[:, :, :, :, b] = got.reshape(out.shape[:-1] + (got.shape[1],))

        pltpu.emit_pipeline(
            body,
            grid=(net.seq, parts),
            in_specs=[pl.BlockSpec((length, features), lambda i, j: (0, i * parts + j))],
            out_specs=[
                pl.BlockSpec((1, spread) + target.shape[2:], lambda i, j: (i, j, 0, 0, 0)),
            ],
        )(n2_all, target)

    def no_final(i, rows):
        sum_send[(net.outer - 1) % 2, i] = rows.astype(LOW)

    grad_columns(one_all, g_first)
    sum_first = Sum(net, g_first, side_first, ring_first, sum_send, sum_load)
    grad_columns(two_all, g_second)
    sides = []
    for k in range(net.outer):
        o = sum_first.spot(k)
        for j in range(1, net.inner):
            to = lax.rem(net.i + j, net.inner)
            sides.append(
                net.send(g_second.at[:, o, to], side_second.at[j - 1, :, o], net.at_inner(j))
            )
    sum_first.step(no_final)
    dh_rows = []
    means = []

    def finish_n(t, span):
        net.copy(mixed_ref.at[span], mixed_tile).wait()

        def add(j, sums):
            at = pl.ds(pl.multiple_of(j * wide, wide), wide)
            hsum = hsum_tile[:, at]
            return (
                sums[0] + jnp.sum(hsum * hsum, axis=1, keepdims=True),
                sums[1] + jnp.sum(hsum * wide_tile[:, at], axis=1, keepdims=True),
            )

        zero = jnp.zeros((CHUNK, 1), WIDE)
        squares, cross = lax.fori_loop(0, blocks, add, (zero, zero))
        r2 = lax.rsqrt(squares / width + 1e-6)
        mean = r2 * cross / width

        def one(j, total):
            at = pl.ds(pl.multiple_of(j * wide, wide), wide)
            m2 = hsum_tile[:, at] * r2
            dh = dy_wide[span, at] + r2 * (wide_tile[:, at] - m2 * mean)
            wide_tile[:, at] = dh
            low = dh.astype(LOW)
            low_tile[:, at] = low
            return total + jnp.sum(low.astype(WIDE) * mixed_tile[:, at], axis=1, keepdims=True)

        total = lax.fori_loop(0, blocks, one, zero) / width
        at = net.s * per + t
        mean_all[at] = jnp.transpose(jnp.broadcast_to(total, (CHUNK, 128)))[:8]
        for _, _, s in net.seq_peers():
            means.append(net.send(mean_all.at[at], mean_all.at[at], net.at_seq(s)))
        outs = [net.copy(wide_tile, dh_ref.at[span]), net.copy(low_tile, dh_own.at[span])]
        for out in outs:
            out.wait()
        dh_rows.append(Rows(net, dh_own.at[span], dh_all, t * CHUNK))

    n_sum.keep(0, finish_n)
    sum_first.step(no_final)
    pltpu.emit_pipeline(
        grad_down,
        grid=(width // step,),
        in_specs=[pl.BlockSpec((length, step), lambda i: (0, i))],
        out_specs=[pl.BlockSpec((ffs, step), lambda i: (0, i))],
    )(dy_all, g_down)
    while sum_first.at < net.outer:
        sum_first.step(no_final)
    swap_first = swap(net, sum_send.at[(net.outer - 1) % 2], got_first)
    for rows in dh_rows:
        rows.turn()
    for rows in dh_rows:
        rows.done()
    for copy in means:
        copy.wait_recv()
    for copy in sides:
        copy.wait_recv()
    arrive(swap_first)
    net.finish()


def glu_all(shape, n2_all, w_first, w_second, w_down, hsum, teacher, keep, scale, mixed):
    seq, fsdp, inner = shape
    length, width = n2_all.shape
    ffs = w_first.shape[1]
    own_rows = length // seq
    chips = seq // 2
    chunks = length // CHUNK
    low = lambda *dims: jax.ShapeDtypeStruct(dims, LOW)
    wide = lambda *dims: jax.ShapeDtypeStruct(dims, WIDE)
    outer = fsdp // inner
    r = width // (seq * fsdp)
    whole = low(seq, outer, inner, r, ffs)
    outs = [low(own_rows, width), low(ffs, width), whole, whole]
    outs += [wide(own_rows, width), low(length, width), low(length, width)]
    outs += [low(own_rows, width)] * 2
    outs += [low(chips, own_rows, width), low(max(chips - 1, 1), own_rows, width)] * 2
    outs += [low(inner - 1, seq, outer, r, ffs)] * 2 + [low(outer - 1, seq, r, ffs)]
    outs += [low(seq, r, ffs)]
    in_hbm = len(outs)
    outs += [wide(8, 128), wide(chunks, 8, CHUNK)]
    in_vmem = pl.BlockSpec(memory_space=pltpu.VMEM)
    copies = 16 * chunks + 16 * seq + 3 * outer * inner
    return pl.pallas_call(
        functools.partial(glu_kernel, shape),
        in_specs=[HBM] + [in_vmem] * 3 + [HBM] * 2 + [in_vmem] * 2 + [HBM],
        out_specs=[HBM] * in_hbm + [in_vmem] * 2,
        out_shape=outs,
        scratch_shapes=[pltpu.VMEM((length, ffs), LOW)] * 3
        + [
            pltpu.VMEM((own_rows, width), WIDE),
            pltpu.VMEM((2, CHUNK, width), LOW),
            pltpu.VMEM((chips, CHUNK, width), LOW),
            pltpu.VMEM((CHUNK, width), WIDE),
            pltpu.VMEM((CHUNK, width), WIDE),
            pltpu.VMEM((CHUNK, width), WIDE),
            pltpu.VMEM((CHUNK, width), LOW),
            pltpu.VMEM((CHUNK, width), LOW),
            pltpu.VMEM((2, seq, r, ffs), LOW),
            pltpu.VMEM((inner + 1, seq, r, ffs), LOW),
            pltpu.SemaphoreType.DMA((copies,)),
            pltpu.SemaphoreType.DMA((copies,)),
            pltpu.SemaphoreType.DMA((16 * chunks + outer * (inner + 1) + seq,)),
        ],
        compiler_params=pltpu.CompilerParams(
            collective_id=2, has_side_effects=True, vmem_limit_bytes=VMEM_BYTES
        ),
        name="glu_all",
    )(n2_all, w_first, w_second, w_down, hsum, teacher, keep, scale, mixed)


def on_device(
    inputs,
    teacher,
    segment_ids,
    valid,
    decay_rate,
    w_query,
    w_key,
    w_value,
    w_gate,
    w_out,
    w_first,
    w_second,
    w_down,
):
    seq, fsdp = lax.axis_size("seq"), lax.axis_size("fsdp")
    batch, block_len, width = inputs.shape
    assert batch == 1
    heads_all = decay_rate.shape[0]
    hd = width // heads_all
    heads = heads_all // seq
    own_rows = w_query.shape[0]
    ff = w_first.shape[1]
    ffs = ff // seq
    cols = heads * 4 * hd

    shape = net_shape(seq, fsdp)
    keep = valid.astype(WIDE).reshape(block_len, 1)
    spread = lambda v: jnp.broadcast_to(v, (8, 128))

    attn_own, first_own, second_own = pack_columns(
        (w_query, w_key, w_value, w_gate), (w_first, w_second), seq, heads, hd
    )
    x32 = inputs.reshape(block_len, width).astype(WIDE)
    r1 = lax.rsqrt(jnp.mean(x32 * x32, axis=-1, keepdims=True) + 1e-6)
    n1 = x32 * r1
    rates = lax.dynamic_slice_in_dim(decay_rate, lax.axis_index("seq") * heads, heads, 0)
    (
        full_attn, full_first, full_second, full_out, full_down, n1_all, z, a, states, mixed_out,
        hsum, n2_all, seg, count, squares,
    ) = gather_all(
        shape,
        heads,
        hd,
        rates,
        attn_own,
        first_own,
        second_own,
        w_out[None],
        w_down[None],
        n1.astype(LOW),
        segment_ids.reshape(1, block_len),
        spread(jnp.sum(keep)),
        inputs.reshape(block_len, width),
    )
    seg = seg.reshape(seq * block_len)
    length = seg.shape[0]
    count = count[:1, :1]
    bounds = jnp.concatenate([jnp.full((1,), -1, jnp.int32), seg[CHUNK - 1 :: CHUNK]])
    ra_all = lax.rsqrt(squares / width + 1e-6)

    tokens = block_len * seq * fsdp
    layer_out, grad_down, _, grad_second, dh, dh_all, *others, loss_own, means = glu_all(
        shape,
        n2_all,
        full_first,
        full_second,
        full_down,
        hsum,
        teacher.reshape(block_len, width),
        keep,
        spread(tokens / count),
        mixed_out,
    )
    layer_out = layer_out.reshape(1, block_len, width)
    mean_all = means[:, 0].reshape(length, 1)
    side_second, got_first = others[-3], others[-1]

    dn1, share_down, share_out, loss, got_second, got_attn = back_all(
        shape, heads, hd, rates, bounds, seg, z, a, dh_all, ra_all, mean_all, states, full_out,
        full_attn, n1_all, loss_own,
        grad_down, grad_second, side_second,
    )
    input_grad = dh + r1 * (dn1 - n1 * jnp.mean(dn1 * n1, axis=-1, keepdims=True))
    loss = loss[0, 0] / (width * count)
    share_first, share_second, *share_attn = unpack_columns(
        got_attn, got_first, got_second, heads, hd
    )

    return (
        layer_out,
        loss.reshape(()),
        input_grad.reshape(1, block_len, width),
        share_attn[0],
        share_attn[1],
        share_attn[2],
        share_attn[3],
        share_out,
        share_first,
        share_second,
        share_down,
    )


def solution(mesh):
    rows = P(("seq", "fsdp"), None)
    tokens = P("fsdp", "seq", None)
    return jax.shard_map(
        on_device,
        mesh=mesh,
        in_specs=(tokens, tokens, P("fsdp", "seq"), P("fsdp", "seq"), P()) + (rows,) * 8,
        out_specs=(tokens, P(), tokens) + (rows,) * 8,
        check_vma=False,
    )
```

```python
import functools

import jax
import jax.numpy as jnp
from jax import lax
from jax.experimental import pallas as pl
from jax.experimental.pallas import tpu as pltpu
from jax.sharding import PartitionSpec as P

CHUNK = 256
WIDE = jnp.float32
LOW = jnp.bfloat16
VMEM_BYTES = 60 * 1024 * 1024


def dot(left, right, left_dim=1, right_dim=0):
    return lax.dot_general(
        left, right, (((left_dim,), (right_dim,)), ((), ())), preferred_element_type=WIDE
    )


def decays(rate, place_col, place_row, chunk):
    rows = jnp.exp(-rate * place_col)
    cols = jnp.exp(rate * place_row)
    entry = jnp.exp(-rate * (place_col + 1.0))
    tail = jnp.exp(-rate * (chunk - 1.0 - place_col))
    return rows, cols, entry, tail


def masks(bounds_ref, seg_col, seg_row, n, chunk):
    before = bounds_ref[n]
    last = bounds_ref[n + 1]
    row = lax.broadcasted_iota(jnp.int32, (chunk, chunk), 0)
    col = lax.broadcasted_iota(jnp.int32, (chunk, chunk), 1)
    inner = (seg_col == seg_row) & (row >= col)
    return inner, seg_col == before, seg_col == last, jnp.where(before == last, 1.0, 0.0)


def places(chunk):
    place_col = lax.broadcasted_iota(jnp.int32, (chunk, 1), 0).astype(WIDE)
    place_row = lax.broadcasted_iota(jnp.int32, (1, chunk), 1).astype(WIDE)
    return place_col, place_row


def attend(heads, hd, n, rate_ref, seg_before, seg_row, z_ref, au_ref, a_ref, ss_ref, st_ref, state):
    chunk = z_ref.shape[0]
    seg_col = jnp.transpose(seg_row)[:, :1]
    before = jnp.where(n > 0, seg_before[:1, chunk - 1 :], -1.0)
    last = seg_row[:1, chunk - 1 :]
    row = lax.broadcasted_iota(jnp.int32, (chunk, chunk), 0)
    col = lax.broadcasted_iota(jnp.int32, (chunk, chunk), 1)
    inner = (seg_col == seg_row[:1]) & (row >= col)
    entry_on, tail_on = seg_col == before, seg_col == last
    carry = jnp.where(before == last, 1.0, 0.0)
    place_col, place_row = places(chunk)
    ones = jnp.ones((8, hd), WIDE)
    squares = jnp.zeros((8, chunk), WIDE)
    for h in range(heads):
        rate = rate_ref[h]
        base = h * 4 * hd
        zq, zk, zv, zu = (z_ref[:, base + i * hd : base + (i + 1) * hd] for i in range(4))
        q = (zq * jax.nn.sigmoid(zq)).astype(LOW)
        k = (zk * jax.nn.sigmoid(zk)).astype(LOW)
        v = (zv * jax.nn.sigmoid(zv)).astype(LOW)
        u = zu * jax.nn.sigmoid(zu)
        rows, cols, entry, tail = decays(rate, place_col, place_row, chunk)
        scores = dot(q, k, 1, 1)
        weighted = jnp.where(inner, scores * rows * cols, 0.0).astype(LOW)
        held = state[h]
        st_ref[0, h] = held.astype(LOW)
        a = dot(weighted, v) + jnp.where(entry_on, entry, 0.0) * dot(q, held.astype(LOW))
        kt = (k.astype(WIDE) * jnp.where(tail_on, tail, 0.0)).astype(LOW)
        state[h] = carry * jnp.exp(jnp.full((1, 1), -rate * chunk, WIDE)) * held + dot(kt, v, 0, 0)
        a_ref[:, h * hd : (h + 1) * hd] = a
        au_ref[:, h * hd : (h + 1) * hd] = (a * u).astype(LOW)
        squares = squares + lax.dot_general(
            ones,
            a * a,
            (((1,), (1,)), ((), ())),
            precision=lax.Precision.HIGHEST,
            preferred_element_type=WIDE,
        )
    ss_ref[...] = squares


def slope(z):
    sg = jax.nn.sigmoid(z)
    return sg * (1.0 + z * (1.0 - sg))


def attend_back(
    heads, hd, n, rate_ref, bounds_ref, segc_ref, segr_ref, z_ref, a_ref, dj_ref, ra_ref, m_ref,
    st_ref, dz_ref, o_ref, later
):
    chunk = z_ref.shape[0]
    inner, entry_on, tail_on, carry = masks(bounds_ref, segc_ref[...], segr_ref[...], n, chunk)
    place_col, place_row = places(chunk)
    ra = ra_ref[...]
    m = m_ref[...]
    for h in range(heads):
        rate = rate_ref[h]
        base = h * 4 * hd
        span = slice(h * hd, (h + 1) * hd)
        zq, zk, zv, zu = (z_ref[:, base + i * hd : base + (i + 1) * hd] for i in range(4))
        q = (zq * jax.nn.sigmoid(zq)).astype(LOW)
        k = (zk * jax.nn.sigmoid(zk)).astype(LOW)
        v = (zv * jax.nn.sigmoid(zv)).astype(LOW)
        u = zu * jax.nn.sigmoid(zu)
        an = a_ref[:, span] * ra
        dj = dj_ref[:, span]
        o_ref[:, span] = (an * u).astype(LOW)
        da = (ra * (dj * u - an * m)).astype(LOW)
        rows, cols, entry, tail = decays(rate, place_col, place_row, chunk)
        entry = jnp.where(entry_on, entry, 0.0)
        tail = jnp.where(tail_on, tail, 0.0)
        decay = jnp.where(inner, rows * cols, 0.0)
        weighted = (dot(q, k, 1, 1) * decay).astype(LOW)
        grads = (dot(da, v, 1, 1) * decay).astype(LOW)
        held = st_ref[0, h]
        after = later[h]
        after_low = after.astype(LOW)
        dq = dot(grads, k) + entry * dot(da, held, 1, 1)
        dk = dot(grads, q, 0, 0) + tail * dot(v, after_low, 1, 1)
        dv = dot(weighted, da, 0, 0) + tail * dot(k, after_low)
        qe = (q.astype(WIDE) * entry).astype(LOW)
        later[h] = carry * jnp.exp(jnp.full((1, 1), -rate * chunk, WIDE)) * after + dot(qe, da, 0, 0)
        dz_ref[:, base : base + hd] = (dq * slope(zq)).astype(LOW)
        dz_ref[:, base + hd : base + 2 * hd] = (dk * slope(zk)).astype(LOW)
        dz_ref[:, base + 2 * hd : base + 3 * hd] = (dv * slope(zv)).astype(LOW)
        dz_ref[:, base + 3 * hd : base + 4 * hd] = (dj * an * slope(zu)).astype(LOW)


def empty(shape, kind):
    return pl.pallas_call(
        lambda out: None,
        out_shape=jax.ShapeDtypeStruct(shape, kind),
        out_specs=pl.BlockSpec(memory_space=pl.ANY),
        name="empty",
    )()


def pack_kernel(seq, heads, hd, *refs):
    weights, glu, attn_out, glu_outs = refs[:4], refs[4:6], refs[6], refs[7:]
    for i in range(seq):
        for h in range(heads):
            for m, w in enumerate(weights):
                to, at = (h * 4 + m) * hd, (i * heads + h) * hd
                attn_out[i, :, to : to + hd] = w[:, at : at + hd]
        for w, out in zip(glu, glu_outs):
            n = out.shape[2]
            out[i] = w[:, i * n : (i + 1) * n]


def pack_columns(weights, glu, seq, heads, hd):
    r, kind = weights[0].shape[0], weights[0].dtype
    n = glu[0].shape[1] // seq
    return pl.pallas_call(
        functools.partial(pack_kernel, seq, heads, hd),
        out_shape=[jax.ShapeDtypeStruct((seq, r, heads * 4 * hd), kind)]
        + [jax.ShapeDtypeStruct((seq, r, n), kind)] * 2,
        compiler_params=pltpu.CompilerParams(vmem_limit_bytes=VMEM_BYTES),
        name="pack_columns",
    )(*weights, *glu)


def unpack_kernel(seq, heads, hd, attn, first, second, o_first, o_second, *o_attn):
    for i in range(seq):
        for h in range(heads):
            for m in range(4):
                at, to = (h * 4 + m) * hd, (i * heads + h) * hd
                o_attn[m][:, to : to + hd] = attn[i, :, at : at + hd].astype(WIDE)
        for ref, out in ((first, o_first), (second, o_second)):
            n = ref.shape[2]
            out[:, i * n : (i + 1) * n] = ref[i].astype(WIDE)


def unpack_columns(attn, first, second, heads, hd):
    seq, r = attn.shape[:2]
    shape = lambda n: jax.ShapeDtypeStruct((r, seq * n), WIDE)
    return pl.pallas_call(
        functools.partial(unpack_kernel, seq, heads, hd),
        out_shape=[shape(first.shape[2]), shape(second.shape[2])] + [shape(heads * hd)] * 4,
        compiler_params=pltpu.CompilerParams(vmem_limit_bytes=VMEM_BYTES),
        name="unpack_columns",
    )(attn, first, second)


class Net:
    def __init__(self, shape, send_sem, recv_sem, local_sem):
        self.seq, self.fsdp, self.inner = shape
        self.outer = self.fsdp // self.inner
        self.chips = self.seq // 2
        self.send_sem, self.recv_sem, self.local_sem = send_sem, recv_sem, local_sem
        self.used = 0
        self.locals = 0
        self.s, self.f = lax.axis_index("seq"), lax.axis_index("fsdp")
        self.chip, self.core = self.s // 2, self.s % 2
        self.o, self.i = self.f // self.inner, self.f % self.inner
        self.sent = []

    def seq_peers(self):
        for dx in range(self.chips):
            for dc in range(2):
                if dx or dc:
                    yield dx, dc, lax.rem(self.chip + dx, self.chips) * 2 + lax.rem(self.core + dc, 2)

    def at_seq(self, s):
        return (s, self.f)

    def at_inner(self, j):
        return (self.s, self.o * self.inner + lax.rem(self.i + j, self.inner))

    def at_outer(self, k):
        return (self.s, lax.rem(self.o + k, self.outer) * self.inner + self.i)

    def barrier(self):
        peers = [self.at_seq(s) for _, _, s in self.seq_peers()]
        peers += [self.at_inner(j) for j in range(1, self.inner)]
        peers += [self.at_outer(1), self.at_outer(self.outer - 1)]
        sem = pltpu.get_barrier_semaphore()
        for peer in peers:
            pl.semaphore_signal(sem, inc=1, device_id=peer, device_id_type=pl.DeviceIdType.MESH)
        pl.semaphore_wait(sem, len(peers))

    def send(self, src, dst, device):
        copy = pltpu.make_async_remote_copy(
            src_ref=src,
            dst_ref=dst,
            send_sem=self.send_sem.at[self.used],
            recv_sem=self.recv_sem.at[self.used],
            device_id=device,
            device_id_type=pl.DeviceIdType.MESH,
        )
        self.used += 1
        copy.start()
        self.sent.append(copy)
        return copy

    def copy(self, src, dst):
        copy = pltpu.make_async_copy(src, dst, self.local_sem.at[self.locals])
        self.locals += 1
        copy.start()
        return copy

    def left(self, copy):
        copy.wait_send()
        self.sent = [other for other in self.sent if other is not copy]

    def finish(self):
        for copy in self.sent:
            copy.wait_send()
        self.sent = []


def net_shape(mesh_seq, mesh_fsdp):
    return mesh_seq, mesh_fsdp, 2 if mesh_fsdp == 8 else 4


class Ring:
    def __init__(self, net, piece, full):
        self.net, self.piece, self.full = net, piece, full
        self.copies = [net.copy(piece, full.at[:, net.o, net.i])]
        self.at = 0
        self.coming = None
        self.side = []

    def step(self):
        net, full = self.net, self.full
        if self.at >= net.outer:
            return
        if self.coming is not None:
            self.coming.wait_recv()
        spot = full.at[:, lax.rem(net.o + net.outer - self.at, net.outer), net.i]
        src = self.piece if self.at == 0 else spot
        self.coming = None
        if self.at < net.outer - 1:
            self.coming = net.send(src, spot, net.at_outer(1))
        for j in range(1, net.inner):
            self.side.append(net.send(src, spot, net.at_inner(j)))
        self.at += 1

    def done(self):
        while self.at < self.net.outer:
            self.step()
        for copy in self.side:
            copy.wait_recv()
        for copy in self.copies:
            copy.wait()


class WideRing:
    def __init__(self, net, piece, full):
        self.net, self.full = net, full
        self.copies = [net.copy(piece, full.at[:, net.o, net.i])]
        self.side = [
            net.send(piece, full.at[:, net.o, net.i], net.at_inner(j)) for j in range(1, net.inner)
        ]
        self.at = 0
        self.coming = None

    def step(self):
        net, full = self.net, self.full
        if self.at >= net.outer:
            return
        if self.at == 0:
            for copy in self.side:
                copy.wait_recv()
            for copy in self.copies:
                copy.wait()
        else:
            self.coming.wait_recv()
        spot = full.at[:, lax.rem(net.o + net.outer - self.at, net.outer)]
        if self.at < net.outer - 1:
            self.coming = net.send(spot, spot, net.at_outer(1))
        self.at += 1

    def done(self):
        while self.at < self.net.outer:
            self.step()


def swap(net, blocks, got):
    own = net.copy(blocks.at[net.s], got.at[net.s])
    coming = [
        net.send(blocks.at[s], got.at[net.s], net.at_seq(s)) for _, _, s in net.seq_peers()
    ]
    return own, coming


def arrive(pair):
    own, coming = pair
    own.wait()
    for copy in coming:
        copy.wait_recv()


class Rows:
    def __init__(self, net, own, whole, start=0):
        t, each = own.shape[0], whole.shape[0] // net.seq
        self.net, self.whole = net, whole
        spot = lambda s: whole.at[pl.ds(pl.multiple_of(s * each + start, t), t)]
        self.spot = spot
        self.far = [
            net.send(own, spot(net.s), net.at_seq(lax.rem(net.chip + dx, net.chips) * 2 + net.core))
            for dx in range(1, net.chips)
        ]
        self.near = [net.send(own, spot(net.s), net.at_seq(net.chip * 2 + 1 - net.core))]
        self.own = net.copy(own, spot(net.s))

    def turn(self):
        net = self.net
        for dx, copy in zip(range(1, net.chips), self.far):
            copy.wait_recv()
            spot = self.spot(lax.rem(net.chip + net.chips - dx, net.chips) * 2 + net.core)
            self.near.append(net.send(spot, spot, net.at_seq(net.chip * 2 + 1 - net.core)))

    def done(self):
        for copy in self.near:
            copy.wait_recv()
        self.own.wait()


def gather_kernel(
    shape, heads, hd,
    rate_ref, attn_ref, first_ref, second_ref, out_ref, down_ref, n1_ref, seg_ref, count_ref, x_ref,
    attn_mid, first_mid, second_mid,
    full_attn, full_first, full_second, full_out, full_down,
    n1_all, z_all, a_all, states, mixed_ref, hsum_ref, n2_own, n2_all, core_in, chip_in,
    seg_all, count_all, ss_all,
    w_attn, w_out, au_all, state, stage, term, wide_tile, hsum_tile, x_tile, n2_tile, ss_in,
    seq_buf, in_buf, out_buf, send_sem, recv_sem, local_sem,
):
    net = Net(shape, send_sem, recv_sem, local_sem)
    length, width = n1_all.shape
    cols = z_all.shape[1]
    own_rows = x_ref.shape[0]
    wide = min(512, width)
    net.barrier()
    count = Total(net, count_ref, seq_buf, in_buf, out_buf)
    attn_swap = swap(net, attn_ref, attn_mid)
    seg_own = net.copy(seg_ref, seg_all.at[net.s])
    segs = [net.send(seg_ref, seg_all.at[net.s], net.at_seq(s)) for _, _, s in net.seq_peers()]
    first_swap = swap(net, first_ref, first_mid)
    second_swap = swap(net, second_ref, second_mid)
    rows = Rows(net, n1_ref, n1_all)
    arrive(attn_swap)
    count.step()
    ring_attn = Ring(net, attn_mid, full_attn)
    ring_out = Ring(net, out_ref, full_out)
    for _ in range(net.outer):
        ring_attn.step()
        ring_out.step()
        count.step()
    arrive(first_swap)
    arrive(second_swap)
    ring_first = Ring(net, first_mid, full_first)
    ring_second = Ring(net, second_mid, full_second)
    ring_first.step()
    ring_second.step()
    ring_down = WideRing(net, down_ref, full_down)
    rows.turn()
    queue = [ring_first, ring_second, ring_down] * (net.outer - 1) + [ring_down]

    def pump(times=1):
        for _ in range(min(times, len(queue))):
            queue.pop(0).step()

    seg_own.wait()
    for copy in segs:
        copy.wait_recv()
    ring_attn.done()
    load_attn = net.copy(full_attn, w_attn)
    rows.done()
    ring_out.done()
    load_out = net.copy(full_out, w_out)
    load_attn.wait()
    load_out.wait()

    state[...] = jnp.zeros_like(state)
    per = own_rows // CHUNK

    def seg_of(n):
        at = pl.ds(pl.multiple_of(n % per * CHUNK, CHUNK), CHUNK)
        return jnp.broadcast_to(seg_all[n // per, :, at].astype(WIDE), (8, CHUNK))

    def chunks(low, steps):
        def body(n1_chunk, z_ref, a_ref, st_ref):
            n = low + pl.program_id(0)

            def project(j, _):
                at = pl.ds(pl.multiple_of(j * wide, wide), wide)
                weight = w_attn[:, :, :, :, at].reshape(width, wide)
                z_ref[:, at] = dot(n1_chunk[...], weight)
                return 0

            lax.fori_loop(0, cols // wide, project, 0)
            au_rows = au_all.at[pl.ds(pl.multiple_of(n * CHUNK, CHUNK), CHUNK)]
            attend(
                heads, hd, n, rate_ref, seg_of(jnp.maximum(n - 1, 0)), seg_of(n), z_ref, au_rows,
                a_ref, ss_all.at[n], st_ref, state,
            )

        block = lambda n: pl.BlockSpec((CHUNK, n), lambda i: (low + i, 0))
        pltpu.emit_pipeline(
            body,
            grid=(steps,),
            in_specs=[block(width)],
            out_specs=[
                block(cols),
                block(heads * hd),
                pl.BlockSpec((1, heads, hd, hd), lambda i: (low + i, 0, 0, 0)),
            ],
        )(n1_all, z_all, a_all, states)

    total = length // CHUNK
    half = total // 2
    chunks(0, half)
    pump()
    chunks(half, total - half)
    near_ss = [net.send(ss_all, ss_in.at[net.s], net.at_seq(s)) for _, _, s in net.seq_peers()]
    pump()

    used = [None, None]
    turns = [0]

    def product(row, each):
        x = au_all[pl.ds(pl.multiple_of(row, CHUNK), CHUNK)]

        def one(j, _):
            at = pl.ds(pl.multiple_of(j * wide, wide), wide)
            weight = w_out[:, :, :, :, at].reshape(heads * hd, wide)
            each(at, dot(x, weight))
            return 0

        lax.fori_loop(0, width // wide, one, 0)

    def slot():
        i = turns[0] % 2
        turns[0] += 1
        if used[i] is not None:
            net.left(used[i])
        return i

    def row_of(chip, core, t):
        return (chip * 2 + core) * own_rows + t * CHUNK

    near = {}
    far = []

    def give(dx):
        chip = lax.rem(net.chip + dx, net.chips)
        for t in range(per):
            i = slot()

            def store(at, part, i=i):
                stage[i, :, at] = part.astype(LOW)

            product(row_of(chip, 1 - net.core, t), store)
            spot = core_in.at[dx, pl.ds(t * CHUNK, CHUNK)]
            used[i] = near[dx, t] = net.send(
                stage.at[i], spot, net.at_seq(net.chip * 2 + 1 - net.core)
            )

    def keep(dx, finish=None):
        chip = lax.rem(net.chip + dx, net.chips)
        for t in range(per):
            span = pl.ds(t * CHUNK, CHUNK)
            near[dx, t].wait_recv()
            loads = [net.copy(core_in.at[dx, span], term.at[0])]
            if dx == 0:
                loads.append(net.copy(x_ref.at[span], x_tile))
                for j, copies in enumerate(far):
                    copies[t].wait_recv()
                    loads.append(net.copy(chip_in.at[j, span], term.at[j + 1]))
            else:
                i = slot()
            for load in loads:
                load.wait()

            def store(at, part):
                add = part + term[0, :, at].astype(WIDE)
                if dx == 0:
                    for j in range(len(far)):
                        add = add + term[j + 1, :, at].astype(WIDE)
                    wide_tile[:, at] = add
                else:
                    stage[i, :, at] = add.astype(LOW)

            product(row_of(chip, net.core, t), store)
            if dx == 0:
                finish(t, span)
            else:
                used[i] = net.send(
                    stage.at[i], chip_in.at[dx - 1, span], net.at_seq(chip * 2 + net.core)
                )
                far[dx - 1].append(used[i])

    def finish(t, span):
        at = net.s * per + t
        squares = ss_in[0, at]
        for j in range(1, net.seq):
            squares = squares + ss_in[j, at]
        ra = lax.rsqrt(jnp.transpose(squares)[:, :1] / width + 1e-6)

        def add(j, squares):
            at = pl.ds(pl.multiple_of(j * wide, wide), wide)
            mixed = wide_tile[:, at] * ra
            wide_tile[:, at] = mixed
            hsum = x_tile[:, at].astype(WIDE) + mixed
            hsum_tile[:, at] = hsum
            return squares + jnp.sum(hsum * hsum, axis=1, keepdims=True)

        squares = lax.fori_loop(0, width // wide, add, jnp.zeros((CHUNK, 1), WIDE))
        r2 = lax.rsqrt(squares / width + 1e-6)

        def scale(j, _):
            at = pl.ds(pl.multiple_of(j * wide, wide), wide)
            n2_tile[:, at] = (hsum_tile[:, at] * r2).astype(LOW)
            return 0

        lax.fori_loop(0, width // wide, scale, 0)
        outs = [
            net.copy(wide_tile, mixed_ref.at[span]),
            net.copy(hsum_tile, hsum_ref.at[span]),
            net.copy(n2_tile, n2_own.at[span]),
        ]
        for out in outs:
            out.wait()

    for dx in range(1, net.chips):
        far.append([])
        give(dx)
        keep(dx)
    pump()
    give(0)
    pump(2)
    for copy in near_ss:
        copy.wait_recv()
    for copy in near_ss:
        net.left(copy)
    ss_in[net.s] = ss_all[...]
    keep(0, finish)
    rows = Rows(net, n2_own, n2_all)
    pump(3)
    rows.turn()
    pump(len(queue))
    count_all[...] = count.done()
    for ring in (ring_first, ring_second, ring_down):
        ring.done()
    rows.done()
    total_ss = ss_in[0]
    for j in range(1, net.seq):
        total_ss = total_ss + ss_in[j]
    ss_all[...] = total_ss
    net.finish()


HBM = pl.BlockSpec(memory_space=pl.ANY)


def gather_all(shape, heads, hd, rates, attn, first, second, w_out, w_down, n1, seg, count, x):
    seq, fsdp, inner = shape
    outer = fsdp // inner
    chips = seq // 2
    own_rows, width = n1.shape
    length = own_rows * seq
    cols = attn.shape[2]
    chunks = length // CHUNK
    like = lambda v, lead: jax.ShapeDtypeStruct(lead + v.shape[-2:], v.dtype)
    ring = lambda v: like(v, (v.shape[0], outer, inner))
    low = lambda *dims: jax.ShapeDtypeStruct(dims, LOW)
    wide = lambda *dims: jax.ShapeDtypeStruct(dims, WIDE)
    outs = [like(v, (seq,)) for v in (attn, first, second)]
    outs += [ring(v) for v in (attn, first, second, w_out, w_down)]
    outs += [low(length, width), wide(length, cols), wide(length, heads * hd)]
    outs += [low(chunks, heads, hd, hd), wide(own_rows, width), wide(own_rows, width)]
    outs += [low(own_rows, width), low(length, width)]
    outs += [low(chips, own_rows, width), low(max(chips - 1, 1), own_rows, width)]
    in_hbm = len(outs)
    outs += [jax.ShapeDtypeStruct((seq,) + seg.shape, seg.dtype), wide(8, 128)]
    outs += [wide(chunks, 8, CHUNK)]
    copies = 7 * seq + 5 * (outer * inner + outer) + total_copies(shape) + 2 * chunks + 4 * seq
    in_vmem = pl.BlockSpec(memory_space=pltpu.VMEM)
    smem = pl.BlockSpec(memory_space=pltpu.SMEM)
    got = pl.pallas_call(
        functools.partial(gather_kernel, shape, heads, hd),
        in_specs=[smem] + [HBM] * 7 + [in_vmem, HBM],
        out_specs=[HBM] * in_hbm + [in_vmem] * 3,
        out_shape=outs,
        scratch_shapes=[
            pltpu.VMEM(ring(attn).shape, LOW),
            pltpu.VMEM(ring(w_out).shape, LOW),
            pltpu.VMEM((length, heads * hd), LOW),
            pltpu.VMEM((heads, hd, hd), WIDE),
            pltpu.VMEM((2, CHUNK, width), LOW),
            pltpu.VMEM((chips, CHUNK, width), LOW),
            pltpu.VMEM((CHUNK, width), WIDE),
            pltpu.VMEM((CHUNK, width), WIDE),
            pltpu.VMEM((CHUNK, width), LOW),
            pltpu.VMEM((CHUNK, width), LOW),
            pltpu.VMEM((seq, chunks, 8, CHUNK), WIDE),
        ]
        + total_scratch(shape)
        + [
            pltpu.SemaphoreType.DMA((copies,)),
            pltpu.SemaphoreType.DMA((copies,)),
            pltpu.SemaphoreType.DMA((24 + 6 * chunks,)),
        ],
        compiler_params=pltpu.CompilerParams(
            collective_id=0, has_side_effects=True, vmem_limit_bytes=VMEM_BYTES
        ),
        name="gather_all",
    )(rates, attn, first, second, w_out, w_down, n1, seg, count, x)
    flat = lambda v: v.reshape(-1, v.shape[-1])
    squares = got[in_hbm + 2][:, 0].reshape(length, 1)
    return [flat(v) for v in got[3:8]] + list(got[8:14]) + [got[15], got[in_hbm], got[in_hbm + 1], squares]


class Total:
    def __init__(self, net, own, seq_buf, in_buf, out_buf):
        self.net, self.bufs, self.stage = net, (seq_buf, in_buf, out_buf), 0
        self.coming = self.share(seq_buf, net.s, own[...], [net.at_seq(s) for _, _, s in net.seq_peers()])

    def share(self, buf, at, value, devices):
        buf[at] = value
        return [self.net.send(buf.at[at], buf.at[at], device) for device in devices]

    def gathered(self, buf):
        for copy in self.coming:
            copy.wait_recv()
        total = buf[0]
        for j in range(1, buf.shape[0]):
            total = total + buf[j]
        return total

    def step(self):
        net, (seq_buf, in_buf, out_buf) = self.net, self.bufs
        if self.stage == 0:
            peers = [net.at_inner(j) for j in range(1, net.inner)]
            self.coming = self.share(in_buf, net.i, self.gathered(seq_buf), peers)
        elif self.stage == 1:
            self.coming = self.share(out_buf, net.o, self.gathered(in_buf), [net.at_outer(1)])
        elif self.stage < net.outer:
            self.coming[-1].wait_recv()
            at = lax.rem(net.o + net.outer - self.stage + 1, net.outer)
            self.coming = [net.send(out_buf.at[at], out_buf.at[at], net.at_outer(1))]
        self.stage += 1

    def done(self):
        while self.stage < self.net.outer:
            self.step()
        return self.gathered(self.bufs[2])


def total_scratch(shape):
    seq, fsdp, inner = shape
    return [pltpu.VMEM((n, 8, 128), WIDE) for n in (seq, inner, fsdp // inner)]


def total_copies(shape):
    seq, fsdp, inner = shape
    return seq + inner + fsdp // inner


class Sum:
    def __init__(self, net, g, side, ring, send, load, early=None, there=0):
        self.net, self.g, self.side_ref, self.ring_ref = net, g, side, ring
        self.send_buf, self.load = send, load
        self.side = []
        self.ring = []
        self.at = 0
        self.early, self.there = early, there
        for k in range(there, net.outer):
            o = self.spot(k)
            now = []
            for j in range(1, net.inner):
                to = lax.rem(net.i + j, net.inner)
                now.append(net.send(g.at[:, o, to], side.at[j - 1, :, o], net.at_inner(j)))
            self.side.append(now)

    def spot(self, k):
        return lax.rem(self.net.o + 2 * self.net.outer - 1 - k, self.net.outer)

    def step(self, final):
        net, k = self.net, self.at
        self.at += 1
        o = self.spot(k)
        terms = self.load
        loads = [net.copy(self.g.at[:, o, net.i], terms.at[0])]
        for j in range(net.inner - 1):
            side = self.early if k < self.there else self.side_ref
            if k >= self.there:
                self.side[k - self.there][j].wait_recv()
            loads.append(net.copy(side.at[j, :, o], terms.at[j + 1]))
        count = net.inner
        if k > 0:
            self.ring[k - 1].wait_recv()
            loads.append(net.copy(self.ring_ref.at[k - 1], terms.at[count]))
            count += 1
        if k >= 2:
            net.left(self.ring[k - 2])
        for load in loads:
            load.wait()

        def one(i, _):
            total = terms[0, i].astype(WIDE)
            for j in range(1, count):
                total = total + terms[j, i].astype(WIDE)
            if k < net.outer - 1:
                self.send_buf[k % 2, i] = total.astype(LOW)
            else:
                final(i, total)
            return 0

        lax.fori_loop(0, terms.shape[1], one, 0)
        if k < net.outer - 1:
            self.ring.append(net.send(self.send_buf.at[k % 2], self.ring_ref.at[k], net.at_outer(1)))


GRADS = ("down", "second", "attn", "out")


def early_steps(outer):
    return outer // 2


SPLIT = ("second", "attn")


def back_kernel(
    shape, heads, hd,
    rate_ref, bounds_ref, segc, segr, z, a, dh, ra, mean, states, w_out, w_attn, n1, loss_ref,
    g_down, g_second, early_second,
    dn1_ref, o_down, o_out, o_loss, got_second, got_attn, g_attn,
    side_down, side_second, side_attn, side_out,
    ring_down, ring_second, ring_attn, ring_out,
    core_in, chip_in,
    dz_all, later, dj, o_chunk, out_acc, g_out, stage, term, wide_tile,
    *rest
):
    it = iter(rest)
    take = lambda names: {name: next(it) for name in names}
    sends, loads = take(GRADS), take(GRADS)
    total_bufs = [next(it) for _ in range(3)]
    send_sem, recv_sem, local_sem = (next(it) for _ in range(3))
    net = Net(shape, send_sem, recv_sem, local_sem)
    grads = dict(down=g_down, second=g_second, attn=g_attn, out=g_out)
    sides = dict(down=side_down, second=side_second, attn=side_attn, out=side_out)
    rings = dict(down=ring_down, second=ring_second, attn=ring_attn, out=ring_out)
    gots = dict(second=got_second, attn=got_attn)
    owned = dict(down=o_down, out=o_out)
    length, cols = dz_all.shape
    width = dh.shape[1]
    count = length // CHUNK
    wide = min(512, width)

    net.barrier()
    sums, swaps, queue = {}, {}, []
    loss = Total(net, loss_ref, *total_bufs)

    def begin(name):
        early = (early_second, early_steps(net.outer)) if name == "second" else ()
        sums[name] = Sum(net, grads[name], sides[name], rings[name], sends[name], loads[name], *early)
        queue.extend([name] * net.outer)

    def pump(times=1):
        for _ in range(min(times, len(queue))):
            name = queue.pop(0)

            def final(i, rows):
                if name in owned:
                    owned[name][...] = rows
                else:
                    totals[i] = rows.astype(LOW)

            totals = sends[name].at[(net.outer - 1) % 2]
            sums[name].step(final)
            if name in SPLIT and sums[name].at == net.outer:
                swaps[name] = swap(net, totals, gots[name])

    loss.step()
    for name in ("second", "down"):
        begin(name)
    pump()

    later[...] = jnp.zeros_like(later)
    out_acc[...] = jnp.zeros_like(out_acc)

    def chunks(top, steps):
        def body(segc_ref, segr_ref, z_ref, a_ref, dh_ref, ra_ref, m_ref, st_ref):
            n = top - pl.program_id(0)
            dj[...] = dot(dh_ref[...], w_out[...], 1, 1)
            rows = pl.ds(pl.multiple_of(n * CHUNK, CHUNK), CHUNK)
            attend_back(
                heads, hd, n, rate_ref, bounds_ref, segc_ref, segr_ref, z_ref, a_ref, dj, ra_ref,
                m_ref, st_ref, dz_all.at[rows], o_chunk, later,
            )

            def add(j, _):
                at = pl.ds(pl.multiple_of(j * wide, wide), wide)
                out_acc[:, at] += dot(o_chunk[...], dh_ref[:, at], 0, 0)
                return 0

            lax.fori_loop(0, width // wide, add, 0)

        block = lambda n: pl.BlockSpec((CHUNK, n), lambda i: (top - i, 0))
        pltpu.emit_pipeline(
            body,
            grid=(steps,),
            in_specs=[
                block(1),
                pl.BlockSpec((1, CHUNK), lambda i: (0, top - i)),
                block(cols),
                block(heads * hd),
                block(width),
                block(1),
                block(1),
                pl.BlockSpec((1, heads, hd, hd), lambda i: (top - i, 0, 0, 0)),
            ],
        )(segc, segr, z, a, dh, ra, mean, states)

    half = count // 2
    chunks(count - 1, half)
    loss.step()
    pump()
    chunks(count - 1 - half, count - half)
    loss.step()
    pump()

    own_rows = dn1_ref.shape[0]
    tile = min(256, own_rows)
    used = [None, None]
    turns = [0]

    def product(row, each):
        x = dz_all[pl.ds(pl.multiple_of(row, tile), tile)]

        def one(j, _):
            at = pl.ds(pl.multiple_of(j * wide, wide), wide)
            each(at, dot(x, w_attn[at, :], 1, 1))
            return 0

        lax.fori_loop(0, width // wide, one, 0)

    def slot():
        i = turns[0] % 2
        turns[0] += 1
        if used[i] is not None:
            net.left(used[i])
        return i

    def row_of(chip, core, t):
        return (chip * 2 + core) * own_rows + t * tile

    near = {}
    far = []

    def give(dx):
        chip = lax.rem(net.chip + dx, net.chips)
        for t in range(own_rows // tile):
            i = slot()

            def store(at, part, i=i):
                stage[i, :, at] = part.astype(LOW)

            product(row_of(chip, 1 - net.core, t), store)
            spot = core_in.at[dx, pl.ds(t * tile, tile)]
            used[i] = near[dx, t] = net.send(
                stage.at[i], spot, net.at_seq(net.chip * 2 + 1 - net.core)
            )

    def keep(dx):
        chip = lax.rem(net.chip + dx, net.chips)
        for t in range(own_rows // tile):
            span = pl.ds(t * tile, tile)
            near[dx, t].wait_recv()
            loads = [net.copy(core_in.at[dx, span], term.at[0])]
            if dx == 0:
                for j, copies in enumerate(far):
                    copies[t].wait_recv()
                    loads.append(net.copy(chip_in.at[j, span], term.at[j + 1]))
            else:
                i = slot()
            for load in loads:
                load.wait()

            def store(at, part):
                total = part
                for j in range(len(loads)):
                    total = total + term[j, :, at].astype(WIDE)
                if dx == 0:
                    wide_tile[:, at] = total
                else:
                    stage[i, :, at] = total.astype(LOW)

            product(row_of(chip, net.core, t), store)
            if dx == 0:
                net.copy(wide_tile, dn1_ref.at[span]).wait()
            else:
                used[i] = net.send(
                    stage.at[i], chip_in.at[dx - 1, span], net.at_seq(chip * 2 + net.core)
                )
                far[dx - 1].append(used[i])

    for dx in range(1, net.chips):
        far.append([])
        give(dx)
        keep(dx)
    pump()

    parts = 2
    spread = net.outer // parts
    features = width // net.seq // parts

    def grad_body(n1_ref, g_ref):
        for j in range(cols // wide):
            at = slice(j * wide, (j + 1) * wide)
            got = dot(n1_ref[...], dz_all[:, at], 0, 0).astype(LOW)
            g_ref[:, :, :, :, at] = got.reshape(g_ref.shape[:-1] + (wide,))

    pltpu.emit_pipeline(
        grad_body,
        grid=(net.seq, parts),
        in_specs=[pl.BlockSpec((length, features), lambda i, j: (0, i * parts + j))],
        out_specs=[
            pl.BlockSpec((1, spread) + g_attn.shape[2:], lambda i, j: (i, j, 0, 0, 0)),
        ],
    )(n1, g_attn)
    begin("attn")
    for j in range(width // wide):
        at = slice(j * wide, (j + 1) * wide)
        g_out[:, :, :, :, at] = out_acc[:, at].astype(LOW).reshape(g_out.shape[:-1] + (wide,))
    begin("out")
    pump(2)
    give(0)
    pump()
    keep(0)
    o_loss[...] = loss.done()
    pump(len(queue))
    for name in SPLIT:
        arrive(swaps[name])
    net.finish()


def back_all(shape, heads, hd, rates, bounds, seg, z, a, dh, ra, mean, states, w_out, w_attn, n1, loss, g_down, g_second, side_second):
    seq, fsdp, inner = shape
    outer = fsdp // inner
    length, width = dh.shape
    cols = z.shape[1]
    own_rows = length // seq
    chips = seq // 2
    tile = min(256, own_rows)
    g_down = g_down.reshape(1, outer, inner, g_down.shape[0] // fsdp, width)
    size = {
        n: (g.shape[0], g.shape[3], g.shape[4]) for n, g in (("down", g_down), ("second", g_second))
    }
    size["attn"] = (seq, width // (seq * fsdp), cols)
    size["out"] = (1, width // (seq * fsdp), width)
    whole = lambda n: (size[n][0], outer, inner) + size[n][1:]
    low = lambda dims: jax.ShapeDtypeStruct(dims, LOW)
    row = lambda n: jax.ShapeDtypeStruct(size[n][1:], WIDE)
    outs = [jax.ShapeDtypeStruct((own_rows, width), WIDE), row("down"), row("out")]
    outs += [jax.ShapeDtypeStruct((8, 128), WIDE)]
    outs += [low(size[n]) for n in SPLIT] + [low(whole("attn"))]
    outs += [low((inner - 1, size[n][0], outer) + size[n][1:]) for n in GRADS]
    outs += [low((outer - 1,) + size[n]) for n in GRADS]
    outs += [low((chips, own_rows, width)), low((max(chips - 1, 1), own_rows, width))]
    in_vmem = pl.BlockSpec(memory_space=pltpu.VMEM)
    smem = pl.BlockSpec(memory_space=pltpu.SMEM)
    scratch = [
        pltpu.VMEM((length, cols), LOW),
        pltpu.VMEM((heads, hd, hd), WIDE),
        pltpu.VMEM((CHUNK, heads * hd), WIDE),
        pltpu.VMEM((CHUNK, heads * hd), LOW),
        pltpu.VMEM((heads * hd, width), WIDE),
        pltpu.VMEM(whole("out"), LOW),
        pltpu.VMEM((2, tile, width), LOW),
        pltpu.VMEM((chips, tile, width), LOW),
        pltpu.VMEM((tile, width), WIDE),
    ]
    scratch += [pltpu.VMEM((2,) + size[n], LOW) for n in GRADS]
    scratch += [pltpu.VMEM((inner + 1,) + size[n], LOW) for n in GRADS]
    scratch += total_scratch(shape)
    copies = 5 * (outer * inner + outer) + 3 * seq + total_copies(shape) + 2 * length // tile
    scratch += [
        pltpu.SemaphoreType.DMA((copies,)),
        pltpu.SemaphoreType.DMA((copies,)),
        pltpu.SemaphoreType.DMA((5 * outer * (inner + 1) + 3 + 4 * length // tile,)),
    ]
    return pl.pallas_call(
        functools.partial(back_kernel, shape, heads, hd),
        in_specs=[smem, smem] + [HBM] * 8 + [in_vmem] * 2 + [HBM, in_vmem] + [HBM] * 3,
        out_specs=[HBM] + [in_vmem] * 3 + [HBM] * (len(outs) - 4),
        out_shape=outs,
        scratch_shapes=scratch,
        compiler_params=pltpu.CompilerParams(
            collective_id=1, has_side_effects=True, vmem_limit_bytes=VMEM_BYTES
        ),
        name="back_all",
    )(
        rates, bounds, seg.reshape(length, 1), seg.reshape(1, length), z, a, dh, ra, mean, states,
        w_out, w_attn, n1, loss, g_down, g_second, side_second
    )[:6]


def spans(n, step=512):
    return [slice(at, min(at + step, n)) for at in range(0, n, step)]


def glu_kernel(
    shape,
    n2_all, w_first, w_second, w_down, hsum_ref, teacher_ref, keep_ref, scale_ref, mixed_ref,
    layer_out, g_down, g_first, g_second, dh_ref, dh_all, dy_all, dy_own, dh_own,
    core_y, chip_y, core_n, chip_n, side_first, side_second, ring_first, got_first,
    loss_ref, mean_all,
    one_all, two_all, p_all, dy_wide, stage, term, wide_tile, hsum_tile, mixed_tile, low_tile, sent_tile, sum_send, sum_load,
    send_sem, recv_sem, local_sem,
):
    net = Net(shape, send_sem, recv_sem, local_sem)
    width = n2_all.shape[1]
    ffs = p_all.shape[1]
    own_rows = hsum_ref.shape[0]
    per = own_rows // CHUNK
    wide = min(512, width)
    blocks = width // wide
    net.barrier()

    def rows_at(n):
        return pl.ds(pl.multiple_of(n * CHUNK, CHUNK), CHUNK)

    def of_chip(dx):
        return lax.rem(net.chip + dx, net.chips)

    def tiles(dx, src, body):
        base = of_chip(dx) * 2 * per
        pltpu.emit_pipeline(
            lambda ref: body(base + pl.program_id(0), ref),
            grid=(2 * per,),
            in_specs=[pl.BlockSpec((CHUNK, width), lambda i: (base + i, 0))],
        )(src)

    def columns(each):
        def one(j, _):
            each(pl.ds(pl.multiple_of(j * wide, wide), wide))
            return 0

        lax.fori_loop(0, blocks, one, 0)

    used = [None, None]
    turns = [0]

    def slot():
        i = turns[0] % 2
        turns[0] += 1
        if used[i] is not None:
            net.left(used[i])
        return i

    class Exchange:
        def __init__(self, product, core_in, chip_in):
            self.product, self.core_in, self.chip_in = product, core_in, chip_in
            self.near, self.far = {}, {}

        def give(self, dx):
            for t in range(per):
                i = slot()
                rows = rows_at((of_chip(dx) * 2 + 1 - net.core) * per + t)

                def store(at):
                    stage[i, :, at] = self.product(rows, at).astype(LOW)

                columns(store)
                used[i] = self.near[dx, t] = net.send(
                    stage.at[i],
                    self.core_in.at[dx, pl.ds(t * CHUNK, CHUNK)],
                    net.at_seq(net.chip * 2 + 1 - net.core),
                )

        def keep(self, dx, finish=None):
            for t in range(per):
                span = pl.ds(t * CHUNK, CHUNK)
                rows = rows_at((of_chip(dx) * 2 + net.core) * per + t)
                self.near[dx, t].wait_recv()
                loads = [net.copy(self.core_in.at[dx, span], term.at[0])]
                if dx == 0:
                    for j in range(1, net.chips):
                        self.far[j, t].wait_recv()
                        loads.append(net.copy(self.chip_in.at[j - 1, span], term.at[j]))
                    loads.append(net.copy(hsum_ref.at[span], hsum_tile))
                else:
                    i = slot()
                for load in loads:
                    load.wait()

                def store(at):
                    total = self.product(rows, at) + term[0, :, at].astype(WIDE)
                    if dx == 0:
                        for j in range(1, net.chips):
                            total = total + term[j, :, at].astype(WIDE)
                        wide_tile[:, at] = total
                    else:
                        stage[i, :, at] = total.astype(LOW)

                columns(store)
                if dx == 0:
                    finish(t, span)
                else:
                    used[i] = self.far[dx, t] = net.send(
                        stage.at[i],
                        self.chip_in.at[dx - 1, span],
                        net.at_seq(of_chip(dx) * 2 + net.core),
                    )

    def hidden(n, n2):
        rows = rows_at(n)
        for b in spans(ffs):
            one = dot(n2[...], w_first[:, b])
            two = dot(n2[...], w_second[:, b])
            one_all[rows, b] = one.astype(LOW)
            two_all[rows, b] = two.astype(LOW)
            p_all[rows, b] = (one * two).astype(LOW)

    y_sum = Exchange(lambda rows, at: dot(p_all[rows, :], w_down[:, at]), core_y, chip_y)
    for dx in range(1, net.chips):
        tiles(dx, n2_all, hidden)
        y_sum.give(dx)
        y_sum.keep(dx)
    tiles(0, n2_all, hidden)
    y_sum.give(0)

    loss_ref[...] = jnp.zeros_like(loss_ref)
    dy_rows = []

    def finish_y(t, span):
        net.copy(teacher_ref.at[span], sent_tile).wait()
        keep = keep_ref[span, :]
        scale = scale_ref[:1, :1] * keep

        def one(j, squares):
            at = pl.ds(pl.multiple_of(j * wide, wide), wide)
            y = hsum_tile[:, at] + wide_tile[:, at]
            low_tile[:, at] = y.astype(LOW)
            error = y - sent_tile[:, at].astype(WIDE)
            dy = scale * error
            dy_wide[span, at] = dy
            stage[1, :, at] = dy.astype(LOW)
            return squares + jnp.sum(keep * error * error, axis=1, keepdims=True)

        squares = lax.fori_loop(0, blocks, one, jnp.zeros((CHUNK, 1), WIDE))
        loss_ref[...] += jnp.broadcast_to(jnp.sum(squares, axis=0, keepdims=True), (8, 128))
        outs = [
            net.copy(low_tile, layer_out.at[span]),
            net.copy(stage.at[1], dy_own.at[span]),
        ]
        for out in outs:
            out.wait()
        dy_rows.append(Rows(net, dy_own.at[span], dy_all, t * CHUNK))

    def free_stage():
        for i in range(2):
            if used[i] is not None:
                net.left(used[i])
            used[i] = None

    free_stage()
    y_sum.keep(0, finish_y)

    def slopes(n, dy):
        rows = rows_at(n)
        for b in spans(ffs):
            dp = dot(dy[...], w_down[b, :], 1, 1)
            one = one_all[rows, b].astype(WIDE)
            two = two_all[rows, b].astype(WIDE)
            one_all[rows, b] = (dp * two).astype(LOW)
            two_all[rows, b] = (dp * one).astype(LOW)

    n_sum = Exchange(
        lambda rows, at: dot(one_all[rows, :], w_first[at, :], 1, 1)
        + dot(two_all[rows, :], w_second[at, :], 1, 1),
        core_n,
        chip_n,
    )
    for rows in dy_rows:
        rows.near[0].wait_recv()
        rows.near = rows.near[1:]
        rows.own.wait()
    tiles(0, dy_all, slopes)
    n_sum.give(0)
    for rows in dy_rows:
        rows.turn()
    for rows in dy_rows:
        for copy in rows.near:
            copy.wait_recv()
    for dx in range(1, net.chips):
        tiles(dx, dy_all, slopes)
        n_sum.give(dx)
        n_sum.keep(dx)

    length = p_all.shape[0]
    step = 256

    def grad_down(dy, out):
        for b in spans(ffs):
            out[b, :] = dot(p_all[:, b], dy[...], 0, 0).astype(LOW)

    parts = 2
    spread = net.outer // parts
    features = width // net.seq // parts

    def grad_columns(held, target):
        def body(n2, out):
            for b in spans(ffs):
                got = dot(n2[...], held[:, b], 0, 0).astype(LOW)
                out[:, :, :, :, b] = got.reshape(out.shape[:-1] + (got.shape[1],))

        pltpu.emit_pipeline(
            body,
            grid=(net.seq, parts),
            in_specs=[pl.BlockSpec((length, features), lambda i, j: (0, i * parts + j))],
            out_specs=[
                pl.BlockSpec((1, spread) + target.shape[2:], lambda i, j: (i, j, 0, 0, 0)),
            ],
        )(n2_all, target)

    def no_final(i, rows):
        sum_send[(net.outer - 1) % 2, i] = rows.astype(LOW)

    grad_columns(one_all, g_first)
    sum_first = Sum(net, g_first, side_first, ring_first, sum_send, sum_load)
    grad_columns(two_all, g_second)
    sides = []
    for k in range(early_steps(net.outer)):
        o = sum_first.spot(k)
        for j in range(1, net.inner):
            to = lax.rem(net.i + j, net.inner)
            sides.append(
                net.send(g_second.at[:, o, to], side_second.at[j - 1, :, o], net.at_inner(j))
            )
    sum_first.step(no_final)
    dh_rows = []
    means = []

    def finish_n(t, span):
        net.copy(mixed_ref.at[span], mixed_tile).wait()

        def add(j, sums):
            at = pl.ds(pl.multiple_of(j * wide, wide), wide)
            hsum = hsum_tile[:, at]
            return (
                sums[0] + jnp.sum(hsum * hsum, axis=1, keepdims=True),
                sums[1] + jnp.sum(hsum * wide_tile[:, at], axis=1, keepdims=True),
            )

        zero = jnp.zeros((CHUNK, 1), WIDE)
        squares, cross = lax.fori_loop(0, blocks, add, (zero, zero))
        r2 = lax.rsqrt(squares / width + 1e-6)
        mean = r2 * cross / width

        def one(j, total):
            at = pl.ds(pl.multiple_of(j * wide, wide), wide)
            m2 = hsum_tile[:, at] * r2
            dh = dy_wide[span, at] + r2 * (wide_tile[:, at] - m2 * mean)
            wide_tile[:, at] = dh
            low = dh.astype(LOW)
            low_tile[:, at] = low
            return total + jnp.sum(low.astype(WIDE) * mixed_tile[:, at], axis=1, keepdims=True)

        total = lax.fori_loop(0, blocks, one, zero) / width
        at = net.s * per + t
        mean_all[at] = jnp.transpose(jnp.broadcast_to(total, (CHUNK, 128)))[:8]
        for _, _, s in net.seq_peers():
            means.append(net.send(mean_all.at[at], mean_all.at[at], net.at_seq(s)))
        outs = [net.copy(wide_tile, dh_ref.at[span]), net.copy(low_tile, dh_own.at[span])]
        for out in outs:
            out.wait()
        dh_rows.append(Rows(net, dh_own.at[span], dh_all, t * CHUNK))

    n_sum.keep(0, finish_n)
    sum_first.step(no_final)
    pltpu.emit_pipeline(
        grad_down,
        grid=(width // step,),
        in_specs=[pl.BlockSpec((length, step), lambda i: (0, i))],
        out_specs=[pl.BlockSpec((ffs, step), lambda i: (0, i))],
    )(dy_all, g_down)
    while sum_first.at < net.outer:
        sum_first.step(no_final)
    swap_first = swap(net, sum_send.at[(net.outer - 1) % 2], got_first)
    for rows in dh_rows:
        rows.turn()
    for rows in dh_rows:
        rows.done()
    for copy in means:
        copy.wait_recv()
    for copy in sides:
        copy.wait_recv()
    arrive(swap_first)
    net.finish()


def glu_all(shape, n2_all, w_first, w_second, w_down, hsum, teacher, keep, scale, mixed):
    seq, fsdp, inner = shape
    length, width = n2_all.shape
    ffs = w_first.shape[1]
    own_rows = length // seq
    chips = seq // 2
    chunks = length // CHUNK
    low = lambda *dims: jax.ShapeDtypeStruct(dims, LOW)
    wide = lambda *dims: jax.ShapeDtypeStruct(dims, WIDE)
    outer = fsdp // inner
    r = width // (seq * fsdp)
    whole = low(seq, outer, inner, r, ffs)
    outs = [low(own_rows, width), low(ffs, width), whole, whole]
    outs += [wide(own_rows, width), low(length, width), low(length, width)]
    outs += [low(own_rows, width)] * 2
    outs += [low(chips, own_rows, width), low(max(chips - 1, 1), own_rows, width)] * 2
    outs += [low(inner - 1, seq, outer, r, ffs)] * 2 + [low(outer - 1, seq, r, ffs)]
    outs += [low(seq, r, ffs)]
    in_hbm = len(outs)
    outs += [wide(8, 128), wide(chunks, 8, CHUNK)]
    in_vmem = pl.BlockSpec(memory_space=pltpu.VMEM)
    copies = 16 * chunks + 16 * seq + 3 * outer * inner
    return pl.pallas_call(
        functools.partial(glu_kernel, shape),
        in_specs=[HBM] + [in_vmem] * 3 + [HBM] * 2 + [in_vmem] * 2 + [HBM],
        out_specs=[HBM] * in_hbm + [in_vmem] * 2,
        out_shape=outs,
        scratch_shapes=[pltpu.VMEM((length, ffs), LOW)] * 3
        + [
            pltpu.VMEM((own_rows, width), WIDE),
            pltpu.VMEM((2, CHUNK, width), LOW),
            pltpu.VMEM((chips, CHUNK, width), LOW),
            pltpu.VMEM((CHUNK, width), WIDE),
            pltpu.VMEM((CHUNK, width), WIDE),
            pltpu.VMEM((CHUNK, width), WIDE),
            pltpu.VMEM((CHUNK, width), LOW),
            pltpu.VMEM((CHUNK, width), LOW),
            pltpu.VMEM((2, seq, r, ffs), LOW),
            pltpu.VMEM((inner + 1, seq, r, ffs), LOW),
            pltpu.SemaphoreType.DMA((copies,)),
            pltpu.SemaphoreType.DMA((copies,)),
            pltpu.SemaphoreType.DMA((16 * chunks + outer * (inner + 1) + seq,)),
        ],
        compiler_params=pltpu.CompilerParams(
            collective_id=2, has_side_effects=True, vmem_limit_bytes=VMEM_BYTES
        ),
        name="glu_all",
    )(n2_all, w_first, w_second, w_down, hsum, teacher, keep, scale, mixed)


def on_device(
    inputs,
    teacher,
    segment_ids,
    valid,
    decay_rate,
    w_query,
    w_key,
    w_value,
    w_gate,
    w_out,
    w_first,
    w_second,
    w_down,
):
    seq, fsdp = lax.axis_size("seq"), lax.axis_size("fsdp")
    batch, block_len, width = inputs.shape
    assert batch == 1
    heads_all = decay_rate.shape[0]
    hd = width // heads_all
    heads = heads_all // seq
    own_rows = w_query.shape[0]
    ff = w_first.shape[1]
    ffs = ff // seq
    cols = heads * 4 * hd

    shape = net_shape(seq, fsdp)
    keep = valid.astype(WIDE).reshape(block_len, 1)
    spread = lambda v: jnp.broadcast_to(v, (8, 128))

    attn_own, first_own, second_own = pack_columns(
        (w_query, w_key, w_value, w_gate), (w_first, w_second), seq, heads, hd
    )
    x32 = inputs.reshape(block_len, width).astype(WIDE)
    r1 = lax.rsqrt(jnp.mean(x32 * x32, axis=-1, keepdims=True) + 1e-6)
    n1 = x32 * r1
    rates = lax.dynamic_slice_in_dim(decay_rate, lax.axis_index("seq") * heads, heads, 0)
    (
        full_attn, full_first, full_second, full_out, full_down, n1_all, z, a, states, mixed_out,
        hsum, n2_all, seg, count, squares,
    ) = gather_all(
        shape,
        heads,
        hd,
        rates,
        attn_own,
        first_own,
        second_own,
        w_out[None],
        w_down[None],
        n1.astype(LOW),
        segment_ids.reshape(1, block_len),
        spread(jnp.sum(keep)),
        inputs.reshape(block_len, width),
    )
    seg = seg.reshape(seq * block_len)
    length = seg.shape[0]
    count = count[:1, :1]
    bounds = jnp.concatenate([jnp.full((1,), -1, jnp.int32), seg[CHUNK - 1 :: CHUNK]])
    ra_all = lax.rsqrt(squares / width + 1e-6)

    tokens = block_len * seq * fsdp
    layer_out, grad_down, _, grad_second, dh, dh_all, *others, loss_own, means = glu_all(
        shape,
        n2_all,
        full_first,
        full_second,
        full_down,
        hsum,
        teacher.reshape(block_len, width),
        keep,
        spread(tokens / count),
        mixed_out,
    )
    layer_out = layer_out.reshape(1, block_len, width)
    mean_all = means[:, 0].reshape(length, 1)
    side_second, got_first = others[-3], others[-1]

    dn1, share_down, share_out, loss, got_second, got_attn = back_all(
        shape, heads, hd, rates, bounds, seg, z, a, dh_all, ra_all, mean_all, states, full_out,
        full_attn, n1_all, loss_own,
        grad_down, grad_second, side_second,
    )
    input_grad = dh + r1 * (dn1 - n1 * jnp.mean(dn1 * n1, axis=-1, keepdims=True))
    loss = loss[0, 0] / (width * count)
    share_first, share_second, *share_attn = unpack_columns(
        got_attn, got_first, got_second, heads, hd
    )

    return (
        layer_out,
        loss.reshape(()),
        input_grad.reshape(1, block_len, width),
        share_attn[0],
        share_attn[1],
        share_attn[2],
        share_attn[3],
        share_out,
        share_first,
        share_second,
        share_down,
    )


def solution(mesh):
    rows = P(("seq", "fsdp"), None)
    tokens = P("fsdp", "seq", None)
    return jax.shard_map(
        on_device,
        mesh=mesh,
        in_specs=(tokens, tokens, P("fsdp", "seq"), P("fsdp", "seq"), P()) + (rows,) * 8,
        out_specs=(tokens, P(), tokens) + (rows,) * 8,
        check_vma=False,
    )
```
